256 devices in a mesh: cam: 8 (over z), frame: 16 (over x, y_hi, core), head: 2 (over y_lo).
Axes of the slice: x: 4, y: 4 (y_hi: 2, y_lo: 2; y = y_hi * 2 + y_lo), z: 8, core: 2. Of those that a mesh axis runs over, the one named last changes fastest.
Arguments:
- queries: bfloat16 [8, 32, 4, 64, 1024], P('cam', 'frame', None, None, 'head'), may hold values from -8 to 8
- keys: bfloat16 [8, 32, 4, 64, 1024], P('cam', 'frame', None, None, 'head'), may hold values from -8 to 8
- values: bfloat16 [8, 32, 4, 64, 1024], P('cam', 'frame', None, None, 'head'), may hold values from -3 to 3
- offsets: int32 [8, 2], replicated, may hold values from 0 to 16
- w_out: bfloat16 [1024, 2048], P('head'), may hold values from -0.1875 to 0.1875
- grad_out: bfloat16 [8, 32, 2, 4, 16, 2048], P('cam', 'frame', None, None, None, 'head'), may hold values from -6 to 6
Outputs:
- layer_out: bfloat16 [8, 32, 2, 4, 16, 2048], P('cam', 'frame', None, None, None, 'head')
- grad_queries: float32 [8, 32, 4, 64, 1024], P('cam', 'frame', None, None, 'head')
- grad_keys: float32 [8, 32, 4, 64, 1024], P('cam', 'frame', None, None, 'head')
- grad_values: float32 [8, 32, 4, 64, 1024], P('cam', 'frame', None, None, 'head')
- grad_w_out: float32 [1024, 2048], P('head')
The draws below stay inside these ranges and needn't reach their ends.
Inputs may be any that keep to these rules, and one draw needn't show every extreme that they name: offsets[c,0] places camera c's strip toward camera c+1 at 32 + offsets[c,0]; offsets[c,1] places camera c+1's strip toward camera c at offsets[c,1].
All inputs are finite; a program needn't handle non-finite values.
Results may differ from the reference program's by a relative error of at most 0.04.
Values may be sent and summed in bfloat16 or wider, within the bound.
A program may use at most 128 MiB of HBM per device.

```python
import jax
import jax.numpy as jnp
from jax import lax

HEADS = 8
HD = 128
D = 2048
WIDTH = 64
ROWS = 4
STRIP = 16
CAMS = 8
FRAMES = 32


def draw_queries(key, part):
    grid_shape = (CAMS, FRAMES, ROWS, WIDTH, HEADS * HD)
    key = jax.random.fold_in(key, 3)
    normal_vals = 1.4 * jax.random.normal(key, grid_shape, jnp.float32)
    return jnp.clip(normal_vals, -8.0, 8.0).astype(jnp.bfloat16)


def draw_keys(key, part):
    grid_shape = (CAMS, FRAMES, ROWS, WIDTH, HEADS * HD)
    key = jax.random.fold_in(key, 5)
    normal_vals = 1.4 * jax.random.normal(key, grid_shape, jnp.float32)
    return jnp.clip(normal_vals, -8.0, 8.0).astype(jnp.bfloat16)


def with_ends(entries, rng, smallest, largest):
    place = [jax.random.randint(jax.random.fold_in(rng, axis), (), 0, length) for axis, length in enumerate(entries.shape)]
    longest = entries.shape.index(max(entries.shape))
    next_to = place[:longest] + [(place[longest] + 1) % entries.shape[longest]] + place[longest + 1:]
    return entries.at[tuple(place)].set(smallest).at[tuple(next_to)].set(largest)


def level_of(rng, extent, shards, low, largest):
    def one(dim, shards_of):
        heights = jax.random.uniform(jax.random.fold_in(jax.random.fold_in(rng, 6), dim), (shards_of,), jnp.float32, low / len(shards), largest / len(shards))
        return jnp.repeat(jnp.exp(heights), extent[dim] // shards_of).reshape((-1,) + (1,) * (len(extent) - dim - 1))

    factor_of = one(*shards[0])
    for cut in shards[1:]:
        factor_of = factor_of * one(*cut)
    return factor_of


def centred(rng, dims, scale, reach, split=(), kind=jnp.bfloat16):
    gain = level_of(rng, dims, split, -0.22, 0.18) if split else 1.0
    result = jax.random.normal(rng, dims, jnp.float32) * scale * gain
    return jnp.minimum(jnp.maximum(result, -reach), reach).astype(kind)


def setup_inputs(seed: int = 0) -> dict:
    streams_of = jax.random.split(jax.random.key(seed), 7)
    return {
        "queries": draw_queries(jax.random.fold_in(streams_of[6], 71), 0),
        "keys": draw_keys(jax.random.fold_in(streams_of[6], 71), 0),
        "values": centred(streams_of[2], (CAMS, FRAMES, ROWS, WIDTH, HEADS * HD), 0.5, 3.0, ((0, 8), (1, 16), (4, 2))),
        "offsets": with_ends(jax.random.randint(streams_of[3], (CAMS, 2), 0, STRIP + 1), jax.random.fold_in(streams_of[3], 1), 0, STRIP).astype(jnp.int32),
        "w_out": centred(streams_of[4], (HEADS * HD, D), (HEADS * HD) ** -0.5, 0.1875, ((0, 2),)),
        "grad_out": centred(streams_of[5], (CAMS, FRAMES, 2, ROWS, STRIP, D), 1.0, 6.0, ((0, 8), (1, 16), (5, 2))),
    }


def cut_strips(grid_field, first_cols):
    def cut_one(block_cam, first_col):
        return lax.dynamic_slice_in_dim(block_cam, first_col, WIDTH // 4, 2)
    return jax.vmap(cut_one)(grid_field, first_cols)


def place_strips(strip_vals, left_first, right_first):
    def place_one(left_part, right_part, left_col, right_col):
        full_grid = jnp.zeros((FRAMES, ROWS, WIDTH, HEADS * HD), jnp.float32)
        full_grid = lax.dynamic_update_slice_in_dim(full_grid, left_part, left_col, 2)
        return lax.dynamic_update_slice_in_dim(full_grid, right_part, right_col, 2)
    return jax.vmap(place_one)(strip_vals[:, :, 0], strip_vals[:, :, 1], left_first, right_first)


def partner_of(strip_vals):
    return jnp.stack([jnp.roll(strip_vals[:, :, 1], 1, axis=0), jnp.roll(strip_vals[:, :, 0], -1, axis=0)], axis=2)


def attend(tensors):
    score_scale = HD ** -0.5
    query_heads, key_heads, value_heads, grad_heads = [member.astype(jnp.float32) for member in tensors]
    scores = jnp.einsum('qhd,khd->hqk', query_heads, key_heads) * score_scale
    row_max = jnp.max(scores, axis=-1, keepdims=True)
    exp_scores = jnp.exp(scores - row_max)
    row_total = jnp.sum(exp_scores, axis=-1, keepdims=True)
    prob_full = exp_scores / row_total
    weights = lax.optimization_barrier(prob_full.astype(jnp.bfloat16)).astype(jnp.float32)
    attended = jnp.einsum('hqk,khd->qhd', weights, value_heads).astype(jnp.bfloat16)
    row_delta = jnp.sum(grad_heads * attended.astype(jnp.float32), axis=-1)
    grad_prob = jnp.einsum('qhd,khd->hqk', grad_heads, value_heads)
    grad_score = (prob_full * (grad_prob - row_delta.T[:, :, None]) * score_scale).astype(jnp.bfloat16)
    grad_score = lax.optimization_barrier(grad_score).astype(jnp.float32)
    grad_query = jnp.einsum('hqk,khd->qhd', grad_score, key_heads)
    grad_key = jnp.einsum('hqk,qhd->khd', grad_score, query_heads)
    grad_value = jnp.einsum('hqk,qhd->khd', weights, grad_heads)
    return attended, grad_query, grad_key, grad_value


def reference(queries, keys, values, offsets, w_out, grad_out):
    strip_width = WIDTH // 4
    right_first = (WIDTH // 2 + offsets[:, 0]).astype(jnp.int32)
    left_first = jnp.roll(offsets[:, 1], 1).astype(jnp.int32)

    def sides_of(grid_field):
        return jnp.stack([cut_strips(grid_field, left_first), cut_strips(grid_field, right_first)], axis=2)

    query_sides = sides_of(queries)
    key_partner = partner_of(sides_of(keys))
    value_partner = partner_of(sides_of(values))
    token_count = FRAMES * ROWS * strip_width
    grad_rows = grad_out.reshape(-1, D)
    grad_attn = jnp.dot(grad_rows, w_out.T, preferred_element_type=jnp.float32).astype(jnp.bfloat16)
    grad_attn = grad_attn.reshape(CAMS, FRAMES, 2, ROWS, strip_width, HEADS * HD)

    def flatten(strip_vals):
        moved = jnp.transpose(strip_vals, (0, 2, 1, 3, 4, 5))
        return moved.reshape(CAMS * 2, token_count, HEADS, HD)

    def unflatten(flat_vals):
        shaped = flat_vals.reshape(CAMS, 2, FRAMES, ROWS, strip_width, HEADS * HD)
        return jnp.transpose(shaped, (0, 2, 1, 3, 4, 5))

    attended, grad_query, grad_key, grad_value = lax.map(
        attend, (flatten(query_sides), flatten(key_partner), flatten(value_partner), flatten(grad_attn)))
    attended = unflatten(attended)
    attn_rows = attended.reshape(-1, HEADS * HD)
    layer_out = jnp.dot(attn_rows, w_out, preferred_element_type=jnp.float32).astype(jnp.bfloat16)
    layer_out = layer_out.reshape(grad_out.shape)
    grad_w_out = jnp.dot(attn_rows.T, grad_rows, preferred_element_type=jnp.float32)
    grad_queries = place_strips(unflatten(grad_query).astype(jnp.float32), left_first, right_first)
    grad_keys = place_strips(partner_of(unflatten(grad_key)).astype(jnp.float32), left_first, right_first)
    grad_values = place_strips(partner_of(unflatten(grad_value)).astype(jnp.float32), left_first, right_first)
    return layer_out, grad_queries, grad_keys, grad_values, grad_w_out
```

```python
import functools

import jax
import jax.numpy as jnp
from jax import lax
from jax.experimental import pallas as pl
from jax.experimental.pallas import tpu as pltpu
from jax.sharding import PartitionSpec as P

HD = 128
BF = jnp.bfloat16
F32 = jnp.float32
MESH = pl.DeviceIdType.MESH
LOG2E = 1.4426950408889634
NT = (((1,), (1,)), ((), ()))


def dot(a, b):
    return jnp.dot(a, b, preferred_element_type=F32)


def dot_nt(a, b):
    return lax.dot_general(a, b, NT, preferred_element_type=F32)


def each(count, fn):
    def step(i, carry):
        fn(i)
        return carry

    lax.fori_loop(0, count, step, 0)


def transposed(block):
    return block.astype(F32).T


def selector(off):
    rows = lax.broadcasted_iota(jnp.int32, (128, 256), 0)
    cols = lax.broadcasted_iota(jnp.int32, (128, 256), 1)
    hit = cols == rows + (lax.shift_right_logical(rows, 4) * 16 + off)
    return jnp.where(hit, 1.0, 0.0).astype(BF)


def selector_t(off):
    rows = lax.broadcasted_iota(jnp.int32, (256, 128), 1)
    cols = lax.broadcasted_iota(jnp.int32, (256, 128), 0)
    hit = cols == rows + (lax.shift_right_logical(rows, 4) * 16 + off)
    return jnp.where(hit, 1.0, 0.0).astype(BF)


def main_kernel(
    offs, q_hbm, k_hbm, v_hbm, w_hbm, g_hbm,
    lo_out, dq_out, dkv_out, gw_out,
    q_in, k_in, v_in, w, gfull,
    q_send, kv_send, do_send, q_recv, kv_recv, do_recv,
    kt, vt, probs, o_t, rl,
    att_send, att_recv, dq_send, dk_acc, dv_acc, dkv_send,
    a_rows, a_t, core_send, core_recv, own, lo_send, lo_recv,
    x_send, x_recv, vx, z_send, z_recv, y_send, y_recv,
    in_sem, g_ss, g_rs, q_ss, q_rs, kv_ss, kv_rs, do_ss, do_rs,
    att_ss, att_rs, dq_ss, dq_rs, dkv_ss, dkv_rs, core_ss, core_rs, lo_ss, lo_rs,
    x_ss, x_rs, z_ss, z_rs, y_ss, y_rs, zg_ss, zg_rs, xg_ss, xg_rs, xf_ss, xf_rs,
    cg_ss, cg_rs,
):
    c = lax.axis_index("cam")
    f = lax.axis_index("frame")
    hh = lax.axis_index("head")
    x, yh, k = f // 4, (f // 2) % 2, f % 2
    u = x * 2 + k
    scale = HD ** (-0.5)

    def frame_of(unit):
        return (unit // 2) * 4 + yh * 2 + unit % 2

    def frame_x(to_x):
        return to_x * 4 + yh * 2 + k

    def remote(src, dst, ss, rs, **where):
        return pltpu.make_async_remote_copy(
            src_ref=src, dst_ref=dst, send_sem=ss, recv_sem=rs,
            device_id=where, device_id_type=MESH)

    other_core = x * 4 + yh * 2 + 1 - k
    other_half = x * 4 + (1 - yh) * 2 + k
    xp, xm, xo = (x + 1) % 4, (x + 3) % 4, (x + 2) % 4

    barrier = pltpu.get_barrier_semaphore()

    def greet(**where):
        pl.semaphore_signal(barrier, inc=1, device_id=where, device_id_type=MESH)

    def greet_cams(i):
        greet(cam=(c + 1) % 8, frame=i)
        greet(cam=(c + 7) % 8, frame=i)

    loads = [
        pltpu.make_async_copy(src, dst, in_sem.at[i])
        for i, (src, dst) in enumerate(
            ((k_hbm, k_in), (v_hbm, v_in), (q_hbm, q_in), (g_hbm, gfull.at[hh]), (w_hbm, w)))
    ]
    for load in loads:
        load.start()
    each(16, greet_cams)
    each(7, lambda i: greet(frame=frame_of((u + 1 + i) % 8)))
    each(5, lambda i: greet(cam=(c + 2 + i) % 8))
    greet(frame=other_half)
    greet(head=1 - hh)

    off = (offs[(c + 7) % 8, 1], offs[c, 0])
    sel = [selector(o) for o in off]

    def strip(ref, side):
        window = ref[:, :, side * 32:(side + 1) * 32, :].reshape(256, 512)
        return dot(sel[side], window).astype(BF)

    for i, ref in enumerate((k_in, v_in)):
        loads[i].wait()
        for side in range(2):
            cut = strip(ref, side)
            for h in range(4):
                kv_send[(1 - side) * 4 + h, i] = cut[:, h * 128:(h + 1) * 128]

    pl.semaphore_wait(barrier, 46)

    def kv_copy(i):
        unit, half = (u + i // 2) % 8, (yh + i) % 2
        to_cam = (c + 9 - 2 * (unit // 4)) % 8
        to_frame = (unit // 2) * 4 + half * 2 + unit % 2
        return remote(kv_send.at[unit], kv_recv.at[f], kv_ss.at[i], kv_rs.at[f],
                      cam=to_cam, frame=to_frame)

    each(16, lambda i: kv_copy(i).start())

    loads[2].wait()
    for side in range(2):
        cut = strip(q_in, side)
        for h in range(4):
            q_send[side * 4 + h] = cut[:, h * 128:(h + 1) * 128]

    def half_copy(send, recv, ss, rs, i):
        unit = (u + i) % 8
        return remote(send.at[unit], recv.at[u], ss.at[unit], rs.at[u], frame=frame_of(unit))

    def own_copy(send, recv, rs):
        return pltpu.make_async_copy(send.at[u], recv.at[u], rs.at[u])

    own_copy(q_send, q_recv, q_rs).start()
    each(7, lambda i: half_copy(q_send, q_recv, q_ss, q_rs, i + 1).start())
    loads[3].wait()
    g_copy = remote(gfull.at[hh], gfull.at[hh], g_ss, g_rs, head=1 - hh)
    g_copy.start()

    def arrived(ref, sem):
        pltpu.make_async_copy(ref, ref, sem).wait()

    def kv_arrive(i):
        arrived(kv_recv.at[i], kv_rs.at[i])
        cols = pl.ds(pl.multiple_of(i * 128, 128), 128)
        kt[:, cols] = transposed(kv_recv[i, 0]).astype(BF)
        vt[:, cols] = transposed(kv_recv[i, 1]).astype(BF)

    each(16, kv_arrive)

    def send_block(send, recv, ss, rs, unit):
        @pl.when(unit == u)
        def _():
            own_copy(send, recv, rs).start()

        @pl.when(unit != u)
        def _():
            remote(send.at[unit], recv.at[u], ss.at[unit], rs.at[u],
                   frame=frame_of(unit)).start()

    def forward(i):
        b = (x + i) % 4
        for t in range(2):
            arrived(q_recv.at[2 * b + t], q_rs.at[2 * b + t])
        queries = q_recv[pl.ds(2 * b, 2)].reshape(256, 128)
        scores = dot_nt(kv_recv[:, 0].reshape(2048, 128), queries)
        top = jnp.max(scores, axis=0, keepdims=True)
        weights = jnp.exp2((scores - top) * (scale * LOG2E))
        inverse = 1.0 / jnp.sum(weights, axis=0, keepdims=True)
        weights = weights.astype(BF)
        probs[b] = weights
        out_t = dot(vt[...], weights) * inverse
        o_t[b] = out_t
        rl[b] = inverse
        att_send[pl.ds(2 * b, 2)] = out_t.T.astype(BF).reshape(2, 128, 128)
        for t in range(2):
            send_block(att_send, att_recv, att_ss, att_rs, 2 * b + t)

    each(4, forward)

    arrived(gfull.at[1 - hh], g_rs)
    loads[4].wait()
    grad_attn = dot_nt(gfull[0], w[:, :1024]) + dot_nt(gfull[1], w[:, 1024:])
    grad_attn = grad_attn.astype(BF)
    for fr in range(2):
        for s in range(2):
            for h in range(4):
                do_send[s * 4 + h, fr * 64:(fr + 1) * 64] = grad_attn[
                    fr * 128 + s * 64:fr * 128 + s * 64 + 64, h * 128:(h + 1) * 128]
    own_copy(do_send, do_recv, do_rs).start()
    each(7, lambda i: half_copy(do_send, do_recv, do_ss, do_rs, i + 1).start())

    each(8, lambda i: arrived(att_recv.at[i], att_rs.at[i]))
    for fr in range(2):
        for s in range(2):
            for h in range(4):
                a_rows[fr * 128 + s * 64:fr * 128 + s * 64 + 64, h * 128:(h + 1) * 128] = att_recv[
                    s * 4 + h, fr * 64:(fr + 1) * 64]
    for fr in range(2):
        for h in range(4):
            a_t[h * 128:(h + 1) * 128, fr * 128:(fr + 1) * 128] = transposed(
                a_rows[fr * 128:(fr + 1) * 128, h * 128:(h + 1) * 128]).astype(BF)

    theirs = a_t[pl.ds(pl.multiple_of((1 - k) * 256, 256), 256), :]
    for j in range(2):
        core_send[j] = dot(theirs, gfull[j]).astype(BF)
        remote(core_send.at[j], core_recv.at[j], core_ss.at[j], core_rs.at[j],
               frame=other_core).start()

    lo_send[...] = dot(
        a_rows[...], w[:, pl.ds(pl.multiple_of((1 - hh) * 1024, 1024), 1024)]).astype(BF)
    lo_copy = remote(lo_send, lo_recv, lo_ss, lo_rs, head=1 - hh)
    lo_copy.start()

    mine = a_t[pl.ds(pl.multiple_of(k * 256, 256), 256), :]
    for j in range(2):
        own[:, j * 1024:(j + 1) * 1024] = dot(mine, gfull[j])
    for j in range(2):
        arrived(core_recv.at[j], core_rs.at[j])
        own[:, j * 1024:(j + 1) * 1024] += core_recv[j].astype(F32)

    def rows_of(chunk, half):
        return own[pl.ds(pl.multiple_of(chunk * 64 + half * 32, 32), 32), :]

    def x_copy(slot, to_x):
        return remote(x_send.at[slot], x_recv.at[slot], x_ss.at[slot], x_rs.at[slot],
                      frame=frame_x(to_x))

    for slot, (chunk, half, to_x) in enumerate(((xo, 0, xp), (xo, 1, xm), (xp, 1, xp), (xm, 0, xm))):
        x_send[slot] = rows_of(chunk, half).astype(BF)
        x_copy(slot, to_x).start()

    def backward(i):
        b = (x + i) % 4
        for t in range(2):
            arrived(do_recv.at[2 * b + t], do_rs.at[2 * b + t])
        queries = q_recv[pl.ds(2 * b, 2)].reshape(256, 128)
        weights = probs[b]
        grad_t = transposed(do_recv[pl.ds(2 * b, 2)].reshape(256, 128)) * rl[b]
        delta = jnp.sum(grad_t * o_t[b], axis=0, keepdims=True)
        grads = grad_t.T.astype(BF)
        grad_probs = dot(kv_recv[:, 1].reshape(2048, 128), grad_t.astype(BF))
        grad_scores = (weights.astype(F32) * (grad_probs - delta)).astype(BF)
        grad_q_t = dot(kt[...], grad_scores) * scale
        dq_send[pl.ds(2 * b, 2)] = grad_q_t.T.astype(BF).reshape(2, 128, 128)
        for t in range(2):
            send_block(dq_send, dq_out, dq_ss, dq_rs, 2 * b + t)
        dk_acc[...] += dot(grad_scores, queries)
        dv_acc[...] += dot(weights, grads)

    dk_acc[...] = jnp.zeros_like(dk_acc)
    dv_acc[...] = jnp.zeros_like(dv_acc)
    each(2, backward)

    for slot, (chunk, half, to_x) in enumerate(((xp, 0, xp), (xm, 1, xm))):
        arrived(x_recv.at[slot], x_rs.at[slot])
        x_send[4 + slot] = (rows_of(chunk, half) + x_recv[slot].astype(F32)).astype(BF)
        x_copy(4 + slot, to_x).start()

    each(2, lambda i: backward(i + 2))
    dkv_send[:, 0] = (dk_acc[...] * scale).astype(BF).reshape(16, 128, 128)
    dkv_send[:, 1] = dv_acc[...].astype(BF).reshape(16, 128, 128)

    def dkv_copy(i):
        to_frame = (f + i) % 16
        to_cam = (c + 7 + 2 * (x // 2)) % 8
        return remote(dkv_send.at[to_frame], dkv_out.at[yh, u], dkv_ss.at[i],
                      dkv_rs.at[yh * 8 + u], cam=to_cam, frame=to_frame)

    for slot in range(2, 6):
        arrived(x_recv.at[slot], x_rs.at[slot])
    vx[0:32] = rows_of(x, 0) + x_recv[3].astype(F32) + x_recv[4].astype(F32)
    vx[32:64] = rows_of(x, 1) + x_recv[2].astype(F32) + x_recv[5].astype(F32)
    for i in range(8):
        z_send[i] = vx[:, i * 256:(i + 1) * 256].astype(BF)

    def z_copy(i):
        to = (c + i) % 8
        return remote(z_send.at[to], z_recv.at[c], z_ss.at[to], z_rs.at[c], cam=to)

    each(7, lambda i: z_copy(i + 1).start())
    each(16, lambda i: dkv_copy(i).start())

    here = dot(a_rows[...], w[:, pl.ds(pl.multiple_of(hh * 1024, 1024), 1024)])
    lo_copy.wait()
    lo_out[...] = (here + lo_recv[...].astype(F32)).astype(BF)

    total = vx[:, pl.ds(pl.multiple_of(c * 256, 256), 256)]
    for i in range(1, 8):
        frm = (c + i) % 8
        arrived(z_recv.at[frm], z_rs.at[frm])
        total = total + z_recv[frm].astype(F32)
    y_send[...] = total.astype(BF)
    y_copy = remote(y_send, y_recv, y_ss, y_rs, frame=other_half)
    y_copy.start()
    y_copy.wait()
    gw_out[k, x, c] = (y_send[...].astype(F32) + y_recv[...].astype(F32)).astype(BF)

    def zg_copy(i):
        return remote(gw_out.at[k, x, c], gw_out.at[k, x, c], zg_ss.at[i], zg_rs.at[c],
                      cam=(c + i) % 8)

    def xg_copy(z, side):
        return remote(gw_out.at[k, x, z], gw_out.at[k, x, z], xg_ss.at[side, z], xg_rs.at[side, z],
                      frame=frame_x(xp if side == 0 else xm))

    def xf_copy(z):
        odd = z % 2
        src = gw_out.at[k, (x + 3 + 2 * odd) % 4, z]
        return remote(src, src, xf_ss.at[z], xf_rs.at[z], frame=frame_x((x + 1 + 2 * odd) % 4))

    def cg_copy(to_x, slot):
        part = gw_out.at[k, to_x]
        return remote(part, part, cg_ss.at[slot], cg_rs.at[slot], frame=other_core)

    each(7, lambda i: zg_copy(i + 1).start())
    order = (0, 1, 7, 2, 6, 3, 5, 4)
    for d in order:
        z = (c + d) % 8
        if d:
            arrived(gw_out.at[k, x, z], zg_rs.at[z])
        xg_copy(z, 0).start()
        xg_copy(z, 1).start()
    cg_copy(x, 0).start()
    for d in order:
        z = (c + d) % 8
        arrived(gw_out.at[k, xm, z], xg_rs.at[0, z])
        arrived(gw_out.at[k, xp, z], xg_rs.at[1, z])
        xf_copy(z).start()
    cg_copy(xm, 1).start()
    cg_copy(xp, 2).start()
    each(8, lambda z: arrived(gw_out.at[k, xo, z], xf_rs.at[z]))
    cg_copy(xo, 3).start()

    each(8, lambda i: arrived(dq_out.at[i], dq_rs.at[i]))
    each(16, lambda i: arrived(dkv_out.at[i // 8, i % 8], dkv_rs.at[i]))
    for slot, at in enumerate((x, xm, xp, xo)):
        arrived(gw_out.at[1 - k, at], cg_rs.at[slot])

    g_copy.wait_send()
    each(16, lambda i: kv_copy(i).wait_send())

    def sent(send, recv, ss, rs):
        each(7, lambda i: half_copy(send, recv, ss, rs, i + 1).wait_send())

    sent(q_send, q_recv, q_ss, q_rs)
    sent(do_send, do_recv, do_ss, do_rs)
    sent(att_send, att_recv, att_ss, att_rs)
    sent(dq_send, dq_out, dq_ss, dq_rs)
    each(16, lambda i: dkv_copy(i).wait_send())
    for j in range(2):
        remote(core_send.at[j], core_recv.at[j], core_ss.at[j], core_rs.at[j],
               frame=other_core).wait_send()
    for slot, to_x in enumerate((xp, xm, xp, xm, xp, xm)):
        x_copy(slot, to_x).wait_send()
    each(7, lambda i: z_copy(i + 1).wait_send())
    each(7, lambda i: zg_copy(i + 1).wait_send())
    for z in range(8):
        xg_copy(z, 0).wait_send()
        xg_copy(z, 1).wait_send()
        xf_copy(z).wait_send()
    for slot, at in enumerate((x, xm, xp, xo)):
        cg_copy(at, slot).wait_send()


def place_kernel(cam, offs, dq, dkv, gw, gq_hbm, gk_hbm, gv_hbm, gw_hbm, grid, rows, sem):
    c = cam[0]
    off = (offs[(c + 7) % 8, 1], offs[c, 0])
    sel = [selector_t(o) for o in off]
    copies = []
    for n, out in enumerate((gq_hbm, gk_hbm, gv_hbm)):
        for side in range(2):
            for h in range(4):
                unit = side * 4 + h
                if n == 0:
                    placed = dot(sel[side], dq[unit])
                else:
                    unit = (1 - side) * 4 + h
                    placed = dot(sel[side], dkv[0, unit, n - 1]) + dot(sel[side], dkv[1, unit, n - 1])
                grid[n, :, :, side * 32:(side + 1) * 32, h * 128:(h + 1) * 128] = placed.reshape(
                    2, 4, 32, 128)
        copies.append(pltpu.make_async_copy(grid.at[n], out, sem.at[n]))
        copies[-1].start()
    for r in range(8):
        for z in range(8):
            rows[r * 64:(r + 1) * 64, z * 256:(z + 1) * 256] = gw[r // 4, r % 4, z].astype(F32)
        if r % 2:
            part = pl.ds((r - 1) * 64, 128)
            copies.append(pltpu.make_async_copy(rows.at[part], gw_hbm.at[part], sem.at[3 + r // 2]))
            copies[-1].start()
    for copy in copies:
        copy.wait()


def on_device(queries, keys, values, offsets, w_out, grad_out):
    field = queries.shape[1:]
    dma = pltpu.SemaphoreType.DMA
    any_spec = pl.BlockSpec(memory_space=pl.ANY)
    vmem = pl.BlockSpec(memory_space=pltpu.VMEM)
    smem = pl.BlockSpec(memory_space=pltpu.SMEM)
    tile = (128, 128)

    def buf(*shape):
        return pltpu.VMEM(shape, BF)

    layer, dq, dkv, gw = pl.pallas_call(
        main_kernel,
        out_shape=(
            jax.ShapeDtypeStruct((256, 1024), BF),
            jax.ShapeDtypeStruct((8,) + tile, BF),
            jax.ShapeDtypeStruct((2, 8, 2) + tile, BF),
            jax.ShapeDtypeStruct((2, 4, 8, 64, 256), BF),
        ),
        in_specs=[smem] + [any_spec] * 5,
        out_specs=(vmem,) * 4,
        scratch_shapes=[
            buf(*field), buf(*field), buf(*field), buf(512, 2048), buf(2, 256, 1024),
            buf(8, *tile), buf(8, 2, *tile), buf(8, *tile),
            buf(8, *tile), buf(16, 2, *tile), buf(8, *tile),
            buf(128, 2048), buf(128, 2048), buf(4, 2048, 256),
            pltpu.VMEM((4, 128, 256), F32), pltpu.VMEM((4, 1, 256), F32),
            buf(8, *tile), buf(8, *tile), buf(8, *tile),
            pltpu.VMEM((2048, 128), F32), pltpu.VMEM((2048, 128), F32), buf(16, 2, *tile),
            buf(256, 512), buf(512, 256), buf(2, 256, 1024), buf(2, 256, 1024),
            pltpu.VMEM((256, 2048), F32), buf(256, 1024), buf(256, 1024),
            buf(6, 32, 2048), buf(6, 32, 2048), pltpu.VMEM((64, 2048), F32),
            buf(8, 64, 256), buf(8, 64, 256), buf(64, 256), buf(64, 256),
            dma((5,)), dma, dma, dma((8,)), dma((8,)), dma((16,)), dma((16,)), dma((8,)), dma((8,)),
            dma((8,)), dma((8,)), dma((8,)), dma((8,)), dma((16,)), dma((16,)),
            dma((2,)), dma((2,)), dma, dma,
            dma((6,)), dma((6,)), dma((8,)), dma((8,)), dma, dma, dma((8,)), dma((8,)),
            dma((2, 8)), dma((2, 8)), dma((8,)), dma((8,)),
            dma((4,)), dma((4,)),
        ],
        compiler_params=pltpu.CompilerParams(
            collective_id=0, has_side_effects=True, vmem_limit_bytes=56 * 1024 * 1024),
        cost_estimate=pl.CostEstimate(
            flops=5 * 10**9, bytes_accessed=10 * 2**20, transcendentals=2 * 2**20),
        name="strip_attention",
    )(offsets, queries.reshape(field), keys.reshape(field), values.reshape(field), w_out,
      grad_out.reshape(256, 1024))

    grid = jax.ShapeDtypeStruct(field, F32)
    gq, gk, gv, gwo = pl.pallas_call(
        place_kernel,
        out_shape=(grid, grid, grid, jax.ShapeDtypeStruct((512, 2048), F32)),
        in_specs=[smem, smem, vmem, vmem, vmem],
        out_specs=(any_spec,) * 4,
        scratch_shapes=[
            pltpu.VMEM((3,) + field, F32), pltpu.VMEM((512, 2048), F32), dma((7,))],
        compiler_params=pltpu.CompilerParams(vmem_limit_bytes=48 * 1024 * 1024),
        cost_estimate=pl.CostEstimate(
            flops=10**8, bytes_accessed=10 * 2**20, transcendentals=0),
        name="place_gradients",
    )(lax.axis_index("cam").reshape(1), offsets, dq, dkv, gw)
    shape = queries.shape
    return (layer.reshape(grad_out.shape), gq.reshape(shape), gk.reshape(shape), gv.reshape(shape),
            gwo)


def solution(mesh):
    field = P("cam", "frame", None, None, "head")
    rows = P("cam", "frame", None, None, None, "head")
    return jax.shard_map(
        on_device,
        mesh=mesh,
        in_specs=(field, field, field, P(), P("head", None), rows),
        out_specs=(rows, field, field, field, P("head", None)),
        check_vma=False,
    )
```

```python
import functools

import jax
import jax.numpy as jnp
from jax import lax
from jax.experimental import pallas as pl
from jax.experimental.pallas import tpu as pltpu
from jax.sharding import PartitionSpec as P

HD = 128
BF = jnp.bfloat16
F32 = jnp.float32
MESH = pl.DeviceIdType.MESH
LOG2E = 1.4426950408889634
NT = (((1,), (1,)), ((), ()))


def dot(a, b):
    return jnp.dot(a, b, preferred_element_type=F32)


def dot_nt(a, b):
    return lax.dot_general(a, b, NT, preferred_element_type=F32)


def each(count, fn):
    def step(i, carry):
        fn(i)
        return carry

    lax.fori_loop(0, count, step, 0)


def transposed(block):
    return block.astype(F32).T


def selector(off):
    rows = lax.broadcasted_iota(jnp.int32, (128, 256), 0)
    cols = lax.broadcasted_iota(jnp.int32, (128, 256), 1)
    hit = cols == rows + (lax.shift_right_logical(rows, 4) * 16 + off)
    return jnp.where(hit, 1.0, 0.0).astype(BF)


def selector_t(off):
    rows = lax.broadcasted_iota(jnp.int32, (256, 128), 1)
    cols = lax.broadcasted_iota(jnp.int32, (256, 128), 0)
    hit = cols == rows + (lax.shift_right_logical(rows, 4) * 16 + off)
    return jnp.where(hit, 1.0, 0.0).astype(BF)


def main_kernel(
    offs_hbm, q_hbm, k_hbm, v_hbm, w_hbm, g_hbm,
    lo_hbm, dq_hbm, dkv_hbm, gw_hbm,
    offs, q_in, k_in, v_in, w, gfull,
    q_send, kv_send, do_send, q_recv, kv_recv, do_recv,
    kt, vt, probs, o_t, rl,
    att_send, att_recv, dq_send, dq_recv, dk_acc, dv_acc, dkv_send, dkv_recv,
    a_rows, a_t, core_send, core_recv, own, lo_send, lo_recv, lo_done,
    x_send, x_recv, z_send, z_recv, y_send, y_recv, gw,
    in_sem, out_sem, g_ss, g_rs, q_ss, q_rs, kv_ss, kv_rs, do_ss, do_rs,
    att_ss, att_rs, dq_ss, dq_rs, dkv_ss, dkv_rs, core_ss, core_rs, lo_ss, lo_rs,
    x_ss, x_rs, z_ss, z_rs, y_ss, y_rs, zg_ss, zg_rs, xg_ss, xg_rs, cg_ss, cg_rs,
):
    c = lax.axis_index("cam")
    f = lax.axis_index("frame")
    hh = lax.axis_index("head")
    x, yh, k = f // 4, (f // 2) % 2, f % 2
    u = x * 2 + k
    scale = HD ** (-0.5)

    def frame_of(unit):
        return (unit // 2) * 4 + yh * 2 + unit % 2

    def frame_x(to_x):
        return to_x * 4 + yh * 2 + k

    def remote(src, dst, ss, rs, **where):
        return pltpu.make_async_remote_copy(
            src_ref=src, dst_ref=dst, send_sem=ss, recv_sem=rs,
            device_id=where, device_id_type=MESH)

    other_core = x * 4 + yh * 2 + 1 - k
    other_half = x * 4 + (1 - yh) * 2 + k

    barrier = pltpu.get_barrier_semaphore()

    def greet(**where):
        pl.semaphore_signal(barrier, inc=1, device_id=where, device_id_type=MESH)

    def greet_cams(i):
        greet(cam=(c + 1) % 8, frame=i)
        greet(cam=(c + 7) % 8, frame=i)

    loads = [
        pltpu.make_async_copy(src, dst, in_sem.at[i])
        for i, (src, dst) in enumerate(
            ((k_hbm, k_in), (v_hbm, v_in), (q_hbm, q_in), (g_hbm, gfull.at[hh]), (w_hbm, w),
             (offs_hbm, offs)))
    ]
    for load in loads:
        load.start()
    each(16, greet_cams)
    each(7, lambda i: greet(frame=frame_of((u + 1 + i) % 8)))
    each(5, lambda i: greet(cam=(c + 2 + i) % 8))
    greet(frame=other_half)
    greet(head=1 - hh)

    loads[5].wait()
    off = (offs[1, (c + 7) % 8], offs[0, c])
    sel = [selector(o) for o in off]

    def strip(ref, side):
        window = ref[:, :, side * 32:(side + 1) * 32, :].reshape(256, 512)
        return dot(sel[side], window).astype(BF)

    for i, ref in enumerate((k_in, v_in)):
        loads[i].wait()
        for side in range(2):
            cut = strip(ref, side)
            for h in range(4):
                kv_send[h * 2 + 1 - side, i] = cut[:, h * 128:(h + 1) * 128]

    pl.semaphore_wait(barrier, 46)

    def kv_copy(i):
        unit, half = (u + i) % 8, (yh + 1 + i // 8) % 2
        to_cam = (c + 9 - 2 * (unit % 2)) % 8
        to_frame = (unit // 2) * 4 + half * 2 + unit % 2
        return remote(kv_send.at[unit], kv_recv.at[f], kv_ss.at[i], kv_rs.at[f],
                      cam=to_cam, frame=to_frame)

    each(16, lambda i: kv_copy(i).start())

    loads[2].wait()
    for side in range(2):
        cut = strip(q_in, side)
        for h in range(4):
            q_send[h * 2 + side] = cut[:, h * 128:(h + 1) * 128]

    def half_copy(send, recv, ss, rs, i):
        unit = (u + i) % 8
        return remote(send.at[unit], recv.at[u], ss.at[unit], rs.at[u], frame=frame_of(unit))

    def own_copy(send, recv, rs):
        return pltpu.make_async_copy(send.at[u], recv.at[u], rs.at[u])

    own_copy(q_send, q_recv, q_rs).start()
    each(7, lambda i: half_copy(q_send, q_recv, q_ss, q_rs, i + 1).start())
    loads[3].wait()
    g_copy = remote(gfull.at[hh], gfull.at[hh], g_ss, g_rs, head=1 - hh)
    g_copy.start()

    def arrived(ref, sem):
        pltpu.make_async_copy(ref, ref, sem).wait()

    def kv_arrive(i):
        arrived(kv_recv.at[i], kv_rs.at[i])
        cols = pl.ds(pl.multiple_of(i * 128, 128), 128)
        vt[:, cols] = transposed(kv_recv[i, 1]).astype(BF)

    each(16, kv_arrive)

    def send_block(send, recv, ss, rs, unit):
        @pl.when(unit == u)
        def _():
            own_copy(send, recv, rs).start()

        @pl.when(unit != u)
        def _():
            remote(send.at[unit], recv.at[u], ss.at[unit], rs.at[u],
                   frame=frame_of(unit)).start()

    def forward(i):
        b = (x + i) % 4
        for t in range(2):
            arrived(q_recv.at[2 * b + t], q_rs.at[2 * b + t])
        queries = q_recv[pl.ds(2 * b, 2)].reshape(256, 128)
        scores = dot_nt(kv_recv[:, 0].reshape(2048, 128), queries)
        top = jnp.max(scores, axis=0, keepdims=True)
        weights = jnp.exp2((scores - top) * (scale * LOG2E))
        inverse = 1.0 / jnp.sum(weights, axis=0, keepdims=True)
        weights = weights.astype(BF)
        probs[b] = weights
        out_t = dot(vt[...], weights) * inverse
        o_t[b] = out_t
        rl[b] = inverse
        att_send[pl.ds(2 * b, 2)] = out_t.T.astype(BF).reshape(2, 128, 128)
        for t in range(2):
            send_block(att_send, att_recv, att_ss, att_rs, 2 * b + t)

    each(4, forward)

    arrived(gfull.at[1 - hh], g_rs)
    loads[4].wait()
    grad_attn = dot_nt(gfull[0], w[:, :1024]) + dot_nt(gfull[1], w[:, 1024:])
    grad_attn = grad_attn.astype(BF)
    for fr in range(2):
        for s in range(2):
            for h in range(4):
                do_send[h * 2 + s, fr * 64:(fr + 1) * 64] = grad_attn[
                    fr * 128 + s * 64:fr * 128 + s * 64 + 64, h * 128:(h + 1) * 128]
    own_copy(do_send, do_recv, do_rs).start()
    each(7, lambda i: half_copy(do_send, do_recv, do_ss, do_rs, i + 1).start())

    def key_turn(i):
        kt[:, pl.ds(pl.multiple_of(i * 128, 128), 128)] = transposed(kv_recv[i, 0]).astype(BF)

    each(16, key_turn)
    each(8, lambda i: arrived(att_recv.at[i], att_rs.at[i]))
    for fr in range(2):
        for s in range(2):
            for h in range(4):
                a_rows[fr * 128 + s * 64:fr * 128 + s * 64 + 64, h * 128:(h + 1) * 128] = att_recv[
                    h * 2 + s, fr * 64:(fr + 1) * 64]
    for fr in range(2):
        for h in range(4):
            a_t[h * 128:(h + 1) * 128, fr * 128:(fr + 1) * 128] = transposed(
                a_rows[fr * 128:(fr + 1) * 128, h * 128:(h + 1) * 128]).astype(BF)

    theirs = a_t[pl.ds(pl.multiple_of((1 - k) * 256, 256), 256), :]
    for j in range(2):
        core_send[:, j * 1024:(j + 1) * 1024] = dot(theirs, gfull[j]).astype(BF)

    def core_copy(p):
        part = pl.ds(p * 64, 64)
        return remote(core_send.at[part], core_recv.at[part], core_ss.at[p], core_rs.at[p],
                      frame=other_core)

    for p in range(4):
        core_copy(p).start()
    mine = a_t[pl.ds(pl.multiple_of(k * 256, 256), 256), :]
    for j in range(2):
        own[:, j * 1024:(j + 1) * 1024] = dot(mine, gfull[j])

    def x_copy(p, i):
        to = (x + i) % 4
        return remote(x_send.at[p, to], x_recv.at[p, x], x_ss.at[p, i - 1], x_rs.at[p],
                      frame=frame_x(to))

    for p in range(4):
        part = pl.ds(p * 64, 64)
        arrived(core_recv.at[part], core_rs.at[p])
        piece = own[part, :] + core_recv[part, :].astype(F32)
        own[part, :] = piece
        x_send[p] = piece.astype(BF).reshape(4, 16, 2048)
        for i in (1, 3, 2):
            x_copy(p, i).start()

    lo_send[...] = dot(
        a_rows[...], w[:, pl.ds(pl.multiple_of((1 - hh) * 1024, 1024), 1024)]).astype(BF)
    lo_copy = remote(lo_send, lo_recv, lo_ss, lo_rs, head=1 - hh)
    lo_copy.start()

    def backward(i):
        b = (x + i) % 4
        for t in range(2):
            arrived(do_recv.at[2 * b + t], do_rs.at[2 * b + t])
        queries = q_recv[pl.ds(2 * b, 2)].reshape(256, 128)
        weights = probs[b]
        grad_t = transposed(do_recv[pl.ds(2 * b, 2)].reshape(256, 128)) * rl[b]
        delta = jnp.sum(grad_t * o_t[b], axis=0, keepdims=True)
        grads = grad_t.T.astype(BF)
        grad_probs = dot(kv_recv[:, 1].reshape(2048, 128), grad_t.astype(BF))
        grad_scores = (weights.astype(F32) * (grad_probs - delta)).astype(BF)
        grad_q_t = dot(kt[...], grad_scores) * scale
        dq_send[pl.ds(2 * b, 2)] = grad_q_t.T.astype(BF).reshape(2, 128, 128)
        for t in range(2):
            send_block(dq_send, dq_recv, dq_ss, dq_rs, 2 * b + t)
        dk_acc[...] += dot(grad_scores, queries)
        dv_acc[...] += dot(weights, grads)

    dk_acc[...] = jnp.zeros_like(dk_acc)
    dv_acc[...] = jnp.zeros_like(dv_acc)
    each(2, backward)

    def z_copy(p, i):
        to = (c + i) % 8
        return remote(z_send.at[p, to], z_recv.at[p, c], z_ss.at[p], z_rs.at[p], cam=to)

    def x_total(p):
        arrived(x_recv.at[p, pl.ds(0, 3)], x_rs.at[p])
        total = own[pl.ds(pl.multiple_of(p * 64 + x * 16, 16), 16), :]
        for i in range(1, 4):
            total = total + x_recv[p, (x + i) % 4].astype(F32)
        total = total.astype(BF)
        for i in range(8):
            z_send[p, i] = total[:, i * 256:(i + 1) * 256]
        each(7, lambda i: z_copy(p, i + 1).start())

    each(4, x_total)
    backward(2)

    def y_copy(p):
        return remote(y_send.at[p], y_recv.at[p], y_ss.at[p], y_rs.at[p], frame=other_half)

    def z_total(p):
        arrived(z_recv.at[p, pl.ds(0, 7)], z_rs.at[p])
        total = z_send[p, c].astype(F32)
        for i in range(1, 8):
            total = total + z_recv[p, (c + i) % 8].astype(F32)
        y_send[p] = total.astype(BF)
        y_copy(p).start()

    each(4, z_total)
    backward(3)
    dkv_send[:, 0] = (dk_acc[...] * scale).astype(BF).reshape(16, 128, 128)
    dkv_send[:, 1] = dv_acc[...].astype(BF).reshape(16, 128, 128)

    def dkv_copy(i):
        to_frame = (f + i) % 16
        return remote(dkv_send.at[to_frame], dkv_recv.at[yh, u], dkv_ss.at[i],
                      dkv_rs.at[yh * 8 + u], cam=(c + 7 + 2 * k) % 8, frame=to_frame)

    def rows_of(p, to_x):
        return pl.ds(pl.multiple_of(k * 256 + p * 64 + to_x * 16, 16), 16)

    def zg_copy(p, i):
        part = gw.at[rows_of(p, x), pl.ds(pl.multiple_of(c * 256, 256), 256)]
        return remote(part, part, zg_ss.at[p], zg_rs.at[p], cam=(c + i) % 8)

    def total_out(p):
        arrived(y_recv.at[p], y_rs.at[p])
        gw[rows_of(p, x), pl.ds(pl.multiple_of(c * 256, 256), 256)] = (
            y_send[p].astype(F32) + y_recv[p].astype(F32)).astype(BF)
        each(7, lambda i: zg_copy(p, i + 1).start())

    each(4, total_out)
    each(16, lambda i: dkv_copy(i).start())

    here = dot(a_rows[...], w[:, pl.ds(pl.multiple_of(hh * 1024, 1024), 1024)])
    lo_copy.wait()
    lo_done[...] = (here + lo_recv[...].astype(F32)).astype(BF)
    lo_write = pltpu.make_async_copy(lo_done, lo_hbm, out_sem.at[0])
    lo_write.start()

    def xg_copy(p, i):
        part = gw.at[rows_of(p, x), :]
        return remote(part, part, xg_ss.at[p], xg_rs.at[p], frame=frame_x((x + i) % 4))

    def z_gathered(p):
        arrived(z_recv.at[p, pl.ds(0, 7)], zg_rs.at[p])
        for i in (1, 3, 2):
            xg_copy(p, i).start()

    each(4, z_gathered)

    def core_rows(p, core):
        return gw.at[pl.ds(pl.multiple_of(core * 256 + p * 64, 64), 64), :]

    def cg_copy(p):
        return remote(core_rows(p, k), core_rows(p, k), cg_ss.at[p], cg_rs.at[p], frame=other_core)

    def gw_write(p, core):
        at = pl.ds(pl.multiple_of(core * 256 + p * 64, 64), 64)
        return pltpu.make_async_copy(gw.at[at], gw_hbm.at[at], out_sem.at[3 + p * 2 + core])

    def x_gathered(p):
        arrived(x_recv.at[p, pl.ds(0, 3)], xg_rs.at[p])
        cg_copy(p).start()
        gw_write(p, k).start()

    each(4, x_gathered)

    each(8, lambda i: arrived(dq_recv.at[i], dq_rs.at[i]))
    dq_write = pltpu.make_async_copy(dq_recv, dq_hbm, out_sem.at[1])
    dq_write.start()
    each(16, lambda i: arrived(dkv_recv.at[i // 8, i % 8], dkv_rs.at[i]))
    dkv_write = pltpu.make_async_copy(dkv_recv, dkv_hbm, out_sem.at[2])
    dkv_write.start()

    def core_gathered(p):
        arrived(core_rows(p, 1 - k), cg_rs.at[p])
        gw_write(p, 1 - k).start()

    each(4, core_gathered)

    g_copy.wait_send()
    each(16, lambda i: kv_copy(i).wait_send())

    def sent(send, recv, ss, rs):
        each(7, lambda i: half_copy(send, recv, ss, rs, i + 1).wait_send())

    sent(q_send, q_recv, q_ss, q_rs)
    sent(do_send, do_recv, do_ss, do_rs)
    sent(att_send, att_recv, att_ss, att_rs)
    sent(dq_send, dq_recv, dq_ss, dq_rs)
    each(16, lambda i: dkv_copy(i).wait_send())

    def pieces_sent(p):
        core_copy(p).wait_send()
        for i in (1, 2, 3):
            x_copy(p, i).wait_send()
        arrived(z_recv.at[p, pl.ds(0, 7)], z_ss.at[p])
        y_copy(p).wait_send()
        arrived(z_recv.at[p, pl.ds(0, 7)], zg_ss.at[p])
        arrived(x_recv.at[p, pl.ds(0, 3)], xg_ss.at[p])
        cg_copy(p).wait_send()
        gw_write(p, k).wait()
        gw_write(p, 1 - k).wait()

    each(4, pieces_sent)
    lo_write.wait()
    dq_write.wait()
    dkv_write.wait()


def place_kernel(
    offs_hbm, lo_hbm, dq_hbm, dkv_hbm, gw_hbm, layer_hbm, gq_hbm, gk_hbm, gv_hbm, gwo_hbm,
    offs, dq, dkv, gw, lo, grid, rows, in_sem, out_sem,
):
    c = lax.axis_index("cam")
    loads = [pltpu.make_async_copy(offs_hbm, offs, in_sem.at[0]),
             pltpu.make_async_copy(dq_hbm, dq, in_sem.at[1]),
             pltpu.make_async_copy(dkv_hbm, dkv, in_sem.at[2]),
             pltpu.make_async_copy(lo_hbm, lo, in_sem.at[3])]
    part = [pl.ds(r * 128, 128) for r in range(4)]
    loads += [pltpu.make_async_copy(gw_hbm.at[part[r]], gw.at[part[r]], in_sem.at[4 + r])
              for r in range(4)]
    for load in loads:
        load.start()
    loads[0].wait()
    off = (offs[1, (c + 7) % 8], offs[0, c])
    sel = [selector_t(o) for o in off]
    writes = []

    def write(src, dst):
        writes.append(pltpu.make_async_copy(src, dst, out_sem.at[len(writes)]))
        writes[-1].start()

    for n, out in enumerate((gq_hbm, gk_hbm, gv_hbm)):
        if n < 2:
            loads[1 + n].wait()
        for side in range(2):
            for h in range(4):
                unit = h * 2 + (side if n == 0 else 1 - side)
                if n == 0:
                    placed = dot(sel[side], dq[unit])
                else:
                    placed = dot(sel[side], dkv[0, unit, n - 1]) + dot(sel[side], dkv[1, unit, n - 1])
                grid[n, :, :, side * 32:(side + 1) * 32, h * 128:(h + 1) * 128] = placed.reshape(
                    2, 4, 32, 128)
        write(grid.at[n], out)
    loads[3].wait()
    write(lo, layer_hbm)
    for r in range(4):
        loads[4 + r].wait()
        rows[part[r], :] = gw[part[r], :].astype(F32)
        write(rows.at[part[r]], gwo_hbm.at[part[r]])
    for copy in writes:
        copy.wait()


def on_device(queries, keys, values, offsets, w_out, grad_out):
    field = queries.shape[1:]
    dma = pltpu.SemaphoreType.DMA
    any_spec = pl.BlockSpec(memory_space=pl.ANY)
    tile = (128, 128)

    def buf(*shape):
        return pltpu.VMEM(shape, BF)

    mid = [
        jax.ShapeDtypeStruct((256, 1024), BF),
        jax.ShapeDtypeStruct((8,) + tile, BF),
        jax.ShapeDtypeStruct((2, 8, 2) + tile, BF),
        jax.ShapeDtypeStruct((512, 2048), BF),
    ]
    offs = offsets.T
    parts = pl.pallas_call(
        main_kernel,
        out_shape=mid,
        in_specs=[any_spec] * 6,
        out_specs=[any_spec] * 4,
        scratch_shapes=[
            pltpu.SMEM((2, 8), jnp.int32),
            buf(*field), buf(*field), buf(*field), buf(512, 2048), buf(2, 256, 1024),
            buf(8, *tile), buf(8, 2, *tile), buf(8, *tile),
            buf(8, *tile), buf(16, 2, *tile), buf(8, *tile),
            buf(128, 2048), buf(128, 2048), buf(4, 2048, 256),
            pltpu.VMEM((4, 128, 256), F32), pltpu.VMEM((4, 1, 256), F32),
            buf(8, *tile), buf(8, *tile), buf(8, *tile), buf(8, *tile),
            pltpu.VMEM((2048, 128), F32), pltpu.VMEM((2048, 128), F32),
            buf(16, 2, *tile), buf(2, 8, 2, *tile),
            buf(256, 512), buf(512, 256), buf(256, 2048), buf(256, 2048),
            pltpu.VMEM((256, 2048), F32), buf(256, 1024), buf(256, 1024), buf(256, 1024),
            buf(4, 4, 16, 2048), buf(4, 4, 16, 2048),
            buf(4, 8, 16, 256), buf(4, 8, 16, 256), buf(4, 16, 256), buf(4, 16, 256),
            buf(512, 2048),
            dma((6,)), dma((11,)), dma, dma, dma((8,)), dma((8,)), dma((16,)), dma((16,)),
            dma((8,)), dma((8,)),
            dma((8,)), dma((8,)), dma((8,)), dma((8,)), dma((16,)), dma((16,)),
            dma((4,)), dma((4,)), dma, dma,
            dma((4, 3)), dma((4,)), dma((4,)), dma((4,)), dma((4,)), dma((4,)),
            dma((4,)), dma((4,)), dma((4,)), dma((4,)), dma((4,)), dma((4,)),
        ],
        compiler_params=pltpu.CompilerParams(
            collective_id=0, has_side_effects=True, vmem_limit_bytes=56 * 1024 * 1024),
        cost_estimate=pl.CostEstimate(
            flops=5 * 10**9, bytes_accessed=10 * 2**20, transcendentals=2 * 2**20),
        name="strip_attention",
    )(offs, queries.reshape(field), keys.reshape(field), values.reshape(field), w_out,
      grad_out.reshape(256, 1024))

    grid = jax.ShapeDtypeStruct(field, F32)
    layer, gq, gk, gv, gwo = pl.pallas_call(
        place_kernel,
        out_shape=(mid[0], grid, grid, grid, jax.ShapeDtypeStruct((512, 2048), F32)),
        in_specs=[any_spec] * 5,
        out_specs=(any_spec,) * 5,
        scratch_shapes=[
            pltpu.SMEM((2, 8), jnp.int32), buf(8, *tile), buf(2, 8, 2, *tile), buf(512, 2048),
            buf(256, 1024), pltpu.VMEM((3,) + field, F32), pltpu.VMEM((512, 2048), F32),
            dma((8,)), dma((8,))],
        compiler_params=pltpu.CompilerParams(vmem_limit_bytes=60 * 1024 * 1024),
        cost_estimate=pl.CostEstimate(
            flops=10**8, bytes_accessed=10 * 2**20, transcendentals=0),
        name="place_gradients",
    )(offs, *parts)
    shape = queries.shape
    return (layer.reshape(grad_out.shape), gq.reshape(shape), gk.reshape(shape), gv.reshape(shape),
            gwo)


def solution(mesh):
    field = P("cam", "frame", None, None, "head")
    rows = P("cam", "frame", None, None, None, "head")
    return jax.shard_map(
        on_device,
        mesh=mesh,
        in_specs=(field, field, field, P(), P("head", None), rows),
        out_specs=(rows, field, field, field, P("head", None)),
        check_vma=False,
    )
```

```python
import functools

import jax
import jax.numpy as jnp
from jax import lax
from jax.experimental import pallas as pl
from jax.experimental.pallas import tpu as pltpu
from jax.sharding import PartitionSpec as P

HD = 128
BF = jnp.bfloat16
F32 = jnp.float32
MESH = pl.DeviceIdType.MESH
LOG2E = 1.4426950408889634
NT = (((1,), (1,)), ((), ()))


def dot(a, b):
    return jnp.dot(a, b, preferred_element_type=F32)


def dot_nt(a, b):
    return lax.dot_general(a, b, NT, preferred_element_type=F32)


def each(count, fn):
    def step(i, carry):
        fn(i)
        return carry

    lax.fori_loop(0, count, step, 0)


def transposed(block):
    return block.astype(F32).T


def selector(off):
    rows = lax.broadcasted_iota(jnp.int32, (128, 256), 0)
    cols = lax.broadcasted_iota(jnp.int32, (128, 256), 1)
    hit = cols == rows + (lax.shift_right_logical(rows, 4) * 16 + off)
    return jnp.where(hit, 1.0, 0.0).astype(BF)


def selector_t(off):
    rows = lax.broadcasted_iota(jnp.int32, (256, 128), 1)
    cols = lax.broadcasted_iota(jnp.int32, (256, 128), 0)
    hit = cols == rows + (lax.shift_right_logical(rows, 4) * 16 + off)
    return jnp.where(hit, 1.0, 0.0).astype(BF)


def main_kernel(
    offs_hbm, q_hbm, k_hbm, v_hbm, w_hbm, g_hbm,
    lo_hbm, dq_hbm, dkv_hbm, gw_hbm,
    offs, q_in, k_in, v_in, w, gfull,
    q_send, kv_send, do_send, q_recv, kv_recv, do_recv,
    kt, vt, probs, o_t, rl,
    att_send, att_recv, dq_acc, dq_send, dq_recv, dk_acc, dv_acc, far_send, far_recv, dkv_send, dkv_recv,
    a_rows, a_t, core_send, core_recv, own, lo_send, lo_recv, lo_done,
    x_send, x_recv, z_send, z_recv, y_send, y_recv, gw,
    in_sem, out_sem, g_ss, g_rs, q_ss, q_rs, kv_ss, kv_rs, do_ss, do_rs,
    att_ss, att_rs, dq_ss, dq_rs, far_ss, far_rs, dkv_ss, dkv_rs, core_ss, core_rs, lo_ss, lo_rs,
    x_ss, x_rs, z_ss, z_rs, y_ss, y_rs, zg_ss, zg_rs, xg_ss, xg_rs, cg_ss, cg_rs,
):
    c = lax.axis_index("cam")
    f = lax.axis_index("frame")
    hh = lax.axis_index("head")
    x, yh, k = f // 4, (f // 2) % 2, f % 2
    u = x * 2 + k
    scale = HD ** (-0.5)

    def frame_of(unit):
        return (unit // 2) * 4 + yh * 2 + unit % 2

    def frame_x(to_x):
        return to_x * 4 + yh * 2 + k

    def remote(src, dst, ss, rs, **where):
        return pltpu.make_async_remote_copy(
            src_ref=src, dst_ref=dst, send_sem=ss, recv_sem=rs,
            device_id=where, device_id_type=MESH)

    other_core = x * 4 + yh * 2 + 1 - k
    other_half = x * 4 + (1 - yh) * 2 + k

    barrier = pltpu.get_barrier_semaphore()

    def greet(**where):
        pl.semaphore_signal(barrier, inc=1, device_id=where, device_id_type=MESH)

    def greet_cams(i):
        greet(cam=(c + 1) % 8, frame=i)
        greet(cam=(c + 7) % 8, frame=i)

    loads = [
        pltpu.make_async_copy(src, dst, in_sem.at[i])
        for i, (src, dst) in enumerate(
            ((k_hbm, k_in), (v_hbm, v_in), (q_hbm, q_in), (g_hbm, gfull.at[hh]), (w_hbm, w),
             (offs_hbm, offs)))
    ]
    for load in loads:
        load.start()
    each(16, greet_cams)
    each(7, lambda i: greet(frame=frame_of((u + 1 + i) % 8)))
    each(5, lambda i: greet(cam=(c + 2 + i) % 8))
    greet(frame=other_half)
    greet(head=1 - hh)

    loads[5].wait()
    off = (offs[1, (c + 7) % 8], offs[0, c])
    sel = [selector(o) for o in off]

    def strip(ref, side):
        window = ref[:, :, side * 32:(side + 1) * 32, :].reshape(256, 512)
        return dot(sel[side], window).astype(BF)

    for i, ref in enumerate((k_in, v_in)):
        loads[i].wait()
        for side in range(2):
            cut = strip(ref, side)
            for h in range(4):
                kv_send[h * 2 + 1 - side, i] = cut[:, h * 128:(h + 1) * 128]

    pl.semaphore_wait(barrier, 46)

    def kv_copy(i):
        unit, half = (u + i) % 8, (yh + 1 + i // 8) % 2
        to_cam = (c + 9 - 2 * (unit % 2)) % 8
        to_frame = (unit // 2) * 4 + half * 2 + unit % 2
        return remote(kv_send.at[unit], kv_recv.at[yh, u], kv_ss.at[i], kv_rs.at[yh * 8 + u],
                      cam=to_cam, frame=to_frame)

    each(16, lambda i: kv_copy(i).start())

    loads[2].wait()
    for side in range(2):
        cut = strip(q_in, side)
        for h in range(4):
            q_send[h * 2 + side] = cut[:, h * 128:(h + 1) * 128]

    def half_copy(send, recv, ss, rs, i):
        unit = (u + i) % 8
        return remote(send.at[unit], recv.at[u], ss.at[unit], rs.at[u], frame=frame_of(unit))

    def own_copy(send, recv, rs):
        return pltpu.make_async_copy(send.at[u], recv.at[u], rs.at[u])

    own_copy(q_send, q_recv, q_rs).start()
    each(7, lambda i: half_copy(q_send, q_recv, q_ss, q_rs, i + 1).start())
    loads[3].wait()
    g_copy = remote(gfull.at[hh], gfull.at[hh], g_ss, g_rs, head=1 - hh)
    g_copy.start()

    def arrived(ref, sem):
        pltpu.make_async_copy(ref, ref, sem).wait()

    def kv_arrive(i):
        half, source = i // 8, i % 8
        arrived(kv_recv.at[half, source], kv_rs.at[i])
        cols = pl.ds(pl.multiple_of(source * 128, 128), 128)
        vt[half, :, cols] = transposed(kv_recv[half, source, 1]).astype(BF)

    each(16, kv_arrive)

    def stacked(half, i):
        return kv_recv[half, :, i].reshape(1024, 128)

    def send_block(send, recv, ss, rs, unit):
        @pl.when(unit == u)
        def _():
            own_copy(send, recv, rs).start()

        @pl.when(unit != u)
        def _():
            remote(send.at[unit], recv.at[u], ss.at[unit], rs.at[u],
                   frame=frame_of(unit)).start()

    def forward(i):
        b = (x + i) % 4
        for t in range(2):
            arrived(q_recv.at[2 * b + t], q_rs.at[2 * b + t])
        queries = q_recv[pl.ds(2 * b, 2)].reshape(256, 128)
        scores = [dot_nt(stacked(half, 0), queries) for half in range(2)]
        top = jnp.maximum(jnp.max(scores[0], axis=0, keepdims=True),
                          jnp.max(scores[1], axis=0, keepdims=True))
        total, out_t = 0.0, 0.0
        for half in range(2):
            weights = jnp.exp2((scores[half] - top) * (scale * LOG2E))
            total = total + jnp.sum(weights, axis=0, keepdims=True)
            weights = weights.astype(BF)
            probs[half, b] = weights
            out_t = out_t + dot(vt[half], weights)
        inverse = 1.0 / total
        out_t = out_t * inverse
        o_t[b] = out_t
        rl[b] = inverse
        att_send[pl.ds(2 * b, 2)] = out_t.T.astype(BF).reshape(2, 128, 128)
        for t in range(2):
            send_block(att_send, att_recv, att_ss, att_rs, 2 * b + t)

    each(4, forward)

    each(8, lambda i: arrived(att_recv.at[i], att_rs.at[i]))
    for fr in range(2):
        for s in range(2):
            for h in range(4):
                a_rows[fr * 128 + s * 64:fr * 128 + s * 64 + 64, h * 128:(h + 1) * 128] = att_recv[
                    h * 2 + s, fr * 64:(fr + 1) * 64]
    for fr in range(2):
        for h in range(4):
            a_t[h * 128:(h + 1) * 128, fr * 128:(fr + 1) * 128] = transposed(
                a_rows[fr * 128:(fr + 1) * 128, h * 128:(h + 1) * 128]).astype(BF)

    features = (hh, 1 - hh)

    def core_copy(p):
        part = (p // 2, pl.ds(p % 2 * 128, 128))
        return remote(core_send.at[part], core_recv.at[part], core_ss.at[p], core_rs.at[p],
                      frame=other_core)

    def multiply(g):
        theirs = a_t[pl.ds(pl.multiple_of((1 - k) * 256, 256), 256), :]
        core_send[g] = dot(theirs, gfull[features[g]]).astype(BF)
        core_copy(2 * g).start()
        core_copy(2 * g + 1).start()
        mine = a_t[pl.ds(pl.multiple_of(k * 256, 256), 256), :]
        own[g] = dot(mine, gfull[features[g]])

    def x_copy(p, i):
        to = (x + i) % 4
        return remote(x_send.at[p, to], x_recv.at[p, x], x_ss.at[p, i - 1], x_rs.at[p],
                      frame=frame_x(to))

    def core_total(p):
        part = pl.ds(p % 2 * 128, 128)
        arrived(core_recv.at[p // 2, part], core_rs.at[p])
        piece = own[p // 2, part, :] + core_recv[p // 2, part, :].astype(F32)
        own[p // 2, part, :] = piece
        x_send[p] = piece.astype(BF).reshape(4, 32, 1024)
        for i in (1, 3, 2):
            x_copy(p, i).start()

    def z_copy(p, i):
        to = (c + i) % 8
        return remote(z_send.at[p, to], z_recv.at[p, c], z_ss.at[p], z_rs.at[p], cam=to)

    def x_total(p):
        arrived(x_recv.at[p, pl.ds(0, 3)], x_rs.at[p])
        total = own[p // 2, pl.ds(pl.multiple_of(p % 2 * 128 + x * 32, 32), 32), :]
        for i in range(1, 4):
            total = total + x_recv[p, (x + i) % 4].astype(F32)
        total = total.astype(BF)
        for i in range(8):
            z_send[p, i] = total[:, i * 128:(i + 1) * 128]
        each(7, lambda i: z_copy(p, i + 1).start())

    def y_copy(p):
        return remote(y_send.at[p], y_recv.at[p], y_ss.at[p], y_rs.at[p], frame=other_half)

    def z_total(p):
        arrived(z_recv.at[p, pl.ds(0, 7)], z_rs.at[p])
        total = z_send[p, c].astype(F32)
        for i in range(1, 8):
            total = total + z_recv[p, (c + i) % 8].astype(F32)
        y_send[p] = total.astype(BF)
        y_copy(p).start()

    def piece_at(p, core, to_x=None, z=None):
        row, rows = core * 256 + p % 2 * 128, 128
        if to_x is not None:
            row, rows = row + to_x * 32, 32
        col, cols = features[p // 2] * 1024, 1024
        if z is not None:
            col, cols = col + z * 128, 128
        return (pl.ds(pl.multiple_of(row, rows), rows), pl.ds(pl.multiple_of(col, cols), cols))

    def zg_copy(p, i):
        part = gw.at[piece_at(p, k, x, c)]
        return remote(part, part, zg_ss.at[p], zg_rs.at[p], cam=(c + i) % 8)

    def y_total(p):
        arrived(y_recv.at[p], y_rs.at[p])
        rows, cols = piece_at(p, k, x, c)
        gw[rows, cols] = (y_send[p].astype(F32) + y_recv[p].astype(F32)).astype(BF)
        each(7, lambda i: zg_copy(p, i + 1).start())

    def xg_copy(p, i):
        part = gw.at[piece_at(p, k, x)]
        return remote(part, part, xg_ss.at[p], xg_rs.at[p], frame=frame_x((x + i) % 4))

    def z_gathered(p):
        arrived(z_recv.at[p, pl.ds(0, 7)], zg_rs.at[p])
        for i in (1, 3, 2):
            xg_copy(p, i).start()

    def cg_copy(p):
        part = gw.at[piece_at(p, k)]
        return remote(part, part, cg_ss.at[p], cg_rs.at[p], frame=other_core)

    def gw_write(p, core):
        at = piece_at(p, core)
        return pltpu.make_async_copy(gw.at[at], gw_hbm.at[at], out_sem.at[3 + p * 2 + core])

    def x_gathered(p):
        arrived(x_recv.at[p, pl.ds(0, 3)], xg_rs.at[p])
        cg_copy(p).start()
        gw_write(p, k).start()

    def core_gathered(p):
        arrived(gw.at[piece_at(p, 1 - k)], cg_rs.at[p])
        gw_write(p, 1 - k).start()

    def backward(half, i):
        b = (x + i) % 4
        if half is far:
            for t in range(2):
                arrived(do_recv.at[2 * b + t], do_rs.at[2 * b + t])
        queries = q_recv[pl.ds(2 * b, 2)].reshape(256, 128)
        weights = probs[half, b]
        grad_t = transposed(do_recv[pl.ds(2 * b, 2)].reshape(256, 128)) * rl[b]
        delta = jnp.sum(grad_t * o_t[b], axis=0, keepdims=True)
        grads = grad_t.T.astype(BF)
        grad_probs = dot(stacked(half, 1), grad_t.astype(BF))
        grad_scores = (weights.astype(F32) * (grad_probs - delta)).astype(BF)
        grad_q_t = dot(kt[half], grad_scores)
        if half is far:
            dq_acc[b] = grad_q_t
        else:
            grad_q_t = (grad_q_t + dq_acc[b]) * scale
            dq_send[pl.ds(2 * b, 2)] = grad_q_t.T.astype(BF).reshape(2, 128, 128)
            for t in range(2):
                send_block(dq_send, dq_recv, dq_ss, dq_rs, 2 * b + t)
        if i == 0:
            dk_acc[...] = dot(grad_scores, queries)
            dv_acc[...] = dot(weights, grads)
        else:
            dk_acc[...] += dot(grad_scores, queries)
            dv_acc[...] += dot(weights, grads)

    def far_copy():
        return remote(far_send, far_recv, far_ss, far_rs, frame=other_half)

    def dkv_copy(i):
        source = (u + i) % 8
        return remote(dkv_send.at[source], dkv_recv.at[u], dkv_ss.at[i], dkv_rs.at[u],
                      cam=(c + 7 + 2 * k) % 8, frame=frame_of(source))

    far, near = 1 - yh, yh

    multiply(0)

    def key_turn(i):
        half, source = i // 8, i % 8
        kt[half, :, pl.ds(pl.multiple_of(source * 128, 128), 128)] = transposed(
            kv_recv[half, source, 0]).astype(BF)

    core_total(0)
    core_total(1)
    each(16, key_turn)
    arrived(gfull.at[1 - hh], g_rs)
    loads[4].wait()
    grad_attn = dot_nt(gfull[0], w[:, :1024]) + dot_nt(gfull[1], w[:, 1024:])
    grad_attn = grad_attn.astype(BF)
    for fr in range(2):
        for s in range(2):
            for h in range(4):
                do_send[h * 2 + s, fr * 64:(fr + 1) * 64] = grad_attn[
                    fr * 128 + s * 64:fr * 128 + s * 64 + 64, h * 128:(h + 1) * 128]
    own_copy(do_send, do_recv, do_rs).start()
    each(7, lambda i: half_copy(do_send, do_recv, do_ss, do_rs, i + 1).start())
    multiply(1)
    x_total(0)
    x_total(1)
    lo_send[...] = dot(
        a_rows[...], w[:, pl.ds(pl.multiple_of((1 - hh) * 1024, 1024), 1024)]).astype(BF)
    lo_copy = remote(lo_send, lo_recv, lo_ss, lo_rs, head=1 - hh)
    lo_copy.start()
    core_total(2)
    core_total(3)
    backward(far, 0)
    backward(far, 1)
    z_total(0)
    z_total(1)
    backward(far, 2)
    backward(far, 3)
    far_send[:, 0] = dk_acc[...].astype(BF).reshape(8, 128, 128)
    far_send[:, 1] = dv_acc[...].astype(BF).reshape(8, 128, 128)
    far_copy().start()
    x_total(2)
    x_total(3)
    y_total(0)
    y_total(1)
    backward(near, 0)
    backward(near, 1)
    z_total(2)
    z_total(3)
    z_gathered(0)
    z_gathered(1)
    backward(near, 2)
    backward(near, 3)
    y_total(2)
    y_total(3)
    x_gathered(0)
    x_gathered(1)
    far_copy().wait()
    for i, acc in enumerate((dk_acc, dv_acc)):
        total = acc[...].reshape(8, 128, 128) + far_recv[:, i].astype(F32)
        if i == 0:
            total = total * scale
        dkv_send[:, i] = total.astype(BF)
    each(8, lambda i: dkv_copy(i).start())
    z_gathered(2)
    z_gathered(3)

    here = dot(a_rows[...], w[:, pl.ds(pl.multiple_of(hh * 1024, 1024), 1024)])
    lo_copy.wait()
    lo_done[...] = (here + lo_recv[...].astype(F32)).astype(BF)
    lo_write = pltpu.make_async_copy(lo_done, lo_hbm, out_sem.at[0])
    lo_write.start()

    core_gathered(0)
    core_gathered(1)
    each(8, lambda i: arrived(dq_recv.at[i], dq_rs.at[i]))
    dq_write = pltpu.make_async_copy(dq_recv, dq_hbm, out_sem.at[1])
    dq_write.start()
    each(8, lambda i: arrived(dkv_recv.at[i], dkv_rs.at[i]))
    dkv_write = pltpu.make_async_copy(dkv_recv, dkv_hbm, out_sem.at[2])
    dkv_write.start()
    x_gathered(2)
    x_gathered(3)
    core_gathered(2)
    core_gathered(3)

    g_copy.wait_send()
    each(16, lambda i: kv_copy(i).wait_send())

    def sent(send, recv, ss, rs):
        each(7, lambda i: half_copy(send, recv, ss, rs, i + 1).wait_send())

    sent(q_send, q_recv, q_ss, q_rs)
    sent(do_send, do_recv, do_ss, do_rs)
    sent(att_send, att_recv, att_ss, att_rs)
    sent(dq_send, dq_recv, dq_ss, dq_rs)
    each(8, lambda i: dkv_copy(i).wait_send())
    for p in range(4):
        core_copy(p).wait_send()
        for i in (1, 2, 3):
            x_copy(p, i).wait_send()
        arrived(z_recv.at[p, pl.ds(0, 7)], z_ss.at[p])
        y_copy(p).wait_send()
        arrived(z_recv.at[p, pl.ds(0, 7)], zg_ss.at[p])
        arrived(x_recv.at[p, pl.ds(0, 3)], xg_ss.at[p])
        cg_copy(p).wait_send()
        gw_write(p, k).wait()
        gw_write(p, 1 - k).wait()
    lo_write.wait()
    dq_write.wait()
    dkv_write.wait()


def place_kernel(
    offs_hbm, lo_hbm, dq_hbm, dkv_hbm, gw_hbm, layer_hbm, gq_hbm, gk_hbm, gv_hbm, gwo_hbm,
    offs, dq, dkv, gw, lo, grid, rows, in_sem, out_sem,
):
    c = lax.axis_index("cam")
    loads = [pltpu.make_async_copy(offs_hbm, offs, in_sem.at[0]),
             pltpu.make_async_copy(dq_hbm, dq, in_sem.at[1]),
             pltpu.make_async_copy(dkv_hbm, dkv, in_sem.at[2]),
             pltpu.make_async_copy(lo_hbm, lo, in_sem.at[3])]
    part = [pl.ds(r * 128, 128) for r in range(4)]
    loads += [pltpu.make_async_copy(gw_hbm.at[part[r]], gw.at[part[r]], in_sem.at[4 + r])
              for r in range(4)]
    for load in loads:
        load.start()
    loads[0].wait()
    off = (offs[1, (c + 7) % 8], offs[0, c])
    sel = [selector_t(o) for o in off]
    writes = []

    def write(src, dst):
        writes.append(pltpu.make_async_copy(src, dst, out_sem.at[len(writes)]))
        writes[-1].start()

    for n, out in enumerate((gq_hbm, gk_hbm, gv_hbm)):
        if n < 2:
            loads[1 + n].wait()
        for side in range(2):
            for h in range(4):
                unit = h * 2 + (side if n == 0 else 1 - side)
                if n == 0:
                    placed = dot(sel[side], dq[unit])
                else:
                    placed = dot(sel[side], dkv[unit, n - 1])
                grid[n, :, :, side * 32:(side + 1) * 32, h * 128:(h + 1) * 128] = placed.reshape(
                    2, 4, 32, 128)
        write(grid.at[n], out)
    loads[3].wait()
    write(lo, layer_hbm)
    for r in range(4):
        loads[4 + r].wait()
        rows[part[r], :] = gw[part[r], :].astype(F32)
        write(rows.at[part[r]], gwo_hbm.at[part[r]])
    for copy in writes:
        copy.wait()


def on_device(queries, keys, values, offsets, w_out, grad_out):
    field = queries.shape[1:]
    dma = pltpu.SemaphoreType.DMA
    any_spec = pl.BlockSpec(memory_space=pl.ANY)
    tile = (128, 128)

    def buf(*shape):
        return pltpu.VMEM(shape, BF)

    mid = [
        jax.ShapeDtypeStruct((256, 1024), BF),
        jax.ShapeDtypeStruct((8,) + tile, BF),
        jax.ShapeDtypeStruct((8, 2) + tile, BF),
        jax.ShapeDtypeStruct((512, 2048), BF),
    ]
    offs = offsets.T
    parts = pl.pallas_call(
        main_kernel,
        out_shape=mid,
        in_specs=[any_spec] * 6,
        out_specs=[any_spec] * 4,
        scratch_shapes=[
            pltpu.SMEM((2, 8), jnp.int32),
            buf(*field), buf(*field), buf(*field), buf(512, 2048), buf(2, 256, 1024),
            buf(8, *tile), buf(8, 2, *tile), buf(8, *tile),
            buf(8, *tile), buf(2, 8, 2, *tile), buf(8, *tile),
            buf(2, 128, 1024), buf(2, 128, 1024), buf(2, 4, 1024, 256),
            pltpu.VMEM((4, 128, 256), F32), pltpu.VMEM((4, 1, 256), F32),
            buf(8, *tile), buf(8, *tile), pltpu.VMEM((4, 128, 256), F32), buf(8, *tile), buf(8, *tile),
            pltpu.VMEM((1024, 128), F32), pltpu.VMEM((1024, 128), F32),
            buf(8, 2, *tile), buf(8, 2, *tile), buf(8, 2, *tile), buf(8, 2, *tile),
            buf(256, 512), buf(512, 256), buf(2, 256, 1024), buf(2, 256, 1024),
            pltpu.VMEM((2, 256, 1024), F32), buf(256, 1024), buf(256, 1024), buf(256, 1024),
            buf(4, 4, 32, 1024), buf(4, 4, 32, 1024),
            buf(4, 8, 32, 128), buf(4, 8, 32, 128), buf(4, 32, 128), buf(4, 32, 128),
            buf(512, 2048),
            dma((6,)), dma((11,)), dma, dma, dma((8,)), dma((8,)), dma((16,)), dma((16,)),
            dma((8,)), dma((8,)),
            dma((8,)), dma((8,)), dma((8,)), dma((8,)), dma, dma, dma((8,)), dma((8,)),
            dma((4,)), dma((4,)), dma, dma,
            dma((4, 3)), dma((4,)), dma((4,)), dma((4,)), dma((4,)), dma((4,)),
            dma((4,)), dma((4,)), dma((4,)), dma((4,)), dma((4,)), dma((4,)),
        ],
        compiler_params=pltpu.CompilerParams(
            collective_id=0, has_side_effects=True, vmem_limit_bytes=56 * 1024 * 1024),
        cost_estimate=pl.CostEstimate(
            flops=5 * 10**9, bytes_accessed=10 * 2**20, transcendentals=2 * 2**20),
        name="strip_attention",
    )(offs, queries.reshape(field), keys.reshape(field), values.reshape(field), w_out,
      grad_out.reshape(256, 1024))

    grid = jax.ShapeDtypeStruct(field, F32)
    layer, gq, gk, gv, gwo = pl.pallas_call(
        place_kernel,
        out_shape=(mid[0], grid, grid, grid, jax.ShapeDtypeStruct((512, 2048), F32)),
        in_specs=[any_spec] * 5,
        out_specs=(any_spec,) * 5,
        scratch_shapes=[
            pltpu.SMEM((2, 8), jnp.int32), buf(8, *tile), buf(8, 2, *tile), buf(512, 2048),
            buf(256, 1024), pltpu.VMEM((3,) + field, F32), pltpu.VMEM((512, 2048), F32),
            dma((8,)), dma((8,))],
        compiler_params=pltpu.CompilerParams(vmem_limit_bytes=60 * 1024 * 1024),
        cost_estimate=pl.CostEstimate(
            flops=10**8, bytes_accessed=10 * 2**20, transcendentals=0),
        name="place_gradients",
    )(offs, *parts)
    shape = queries.shape
    return (layer.reshape(grad_out.shape), gq.reshape(shape), gk.reshape(shape), gv.reshape(shape),
            gwo)


def solution(mesh):
    field = P("cam", "frame", None, None, "head")
    rows = P("cam", "frame", None, None, None, "head")
    return jax.shard_map(
        on_device,
        mesh=mesh,
        in_specs=(field, field, field, P(), P("head", None), rows),
        out_specs=(rows, field, field, field, P("head", None)),
        check_vma=False,
    )
```

```python
import functools

import jax
import jax.numpy as jnp
from jax import lax
from jax.experimental import pallas as pl
from jax.experimental.pallas import tpu as pltpu
from jax.sharding import PartitionSpec as P

HD = 128
BF = jnp.bfloat16
F32 = jnp.float32
MESH = pl.DeviceIdType.MESH
LOG2E = 1.4426950408889634
NT = (((1,), (1,)), ((), ()))
PIECES = ("xz", "zx", "xz", "xz")


def dot(a, b):
    return jnp.dot(a, b, preferred_element_type=F32)


def dot_nt(a, b):
    return lax.dot_general(a, b, NT, preferred_element_type=F32)


def each(count, fn):
    def step(i, carry):
        fn(i)
        return carry

    lax.fori_loop(0, count, step, 0)


def transposed(block):
    return block.astype(F32).T


def selector(off):
    rows = lax.broadcasted_iota(jnp.int32, (128, 256), 0)
    cols = lax.broadcasted_iota(jnp.int32, (128, 256), 1)
    hit = cols == rows + (lax.shift_right_logical(rows, 4) * 16 + off)
    return jnp.where(hit, 1.0, 0.0).astype(BF)


def selector_t(off):
    rows = lax.broadcasted_iota(jnp.int32, (256, 128), 1)
    cols = lax.broadcasted_iota(jnp.int32, (256, 128), 0)
    hit = cols == rows + (lax.shift_right_logical(rows, 4) * 16 + off)
    return jnp.where(hit, 1.0, 0.0).astype(BF)


def main_kernel(
    offs_hbm, q_hbm, k_hbm, v_hbm, w_hbm, g_hbm,
    lo_hbm, dq_hbm, dkv_hbm, gw_hbm,
    offs, q_in, k_in, v_in, w, gfull,
    q_send, kv_send, do_send, q_recv, kv_recv, do_recv,
    kt, vt, probs, o_t, rl,
    att_send, att_recv, dq_acc, dq_send, dq_recv, dk_acc, dv_acc, far_send, far_recv, dkv_send, dkv_recv,
    a_rows, a_t, core_send, core_recv, own, lo_send, lo_recv, lo_done,
    out_bf, gw, first_recv, mid_sum, second_recv, y_send, y_recv,
    in_sem, out_sem, g_ss, g_rs, q_ss, q_rs, kv_ss, kv_rs, do_ss, do_rs,
    att_ss, att_rs, dq_ss, dq_rs, far_ss, far_rs, dkv_ss, dkv_rs, core_ss, core_rs, lo_ss, lo_rs,
    sum_ss, sum_rs,
):
    c = lax.axis_index("cam")
    f = lax.axis_index("frame")
    hh = lax.axis_index("head")
    x, yh, k = f >> 2, (f >> 1) & 1, f & 1
    u = x * 2 + k
    scale = HD ** (-0.5)

    def frame_of(unit):
        return (unit >> 1) * 4 + yh * 2 + (unit & 1)

    def frame_x(to_x):
        return to_x * 4 + yh * 2 + k

    def device(cam=c, frame=f, head=hh):
        return (cam, frame, head)

    def remote(src, dst, ss, rs, **where):
        return pltpu.make_async_remote_copy(
            src_ref=src, dst_ref=dst, send_sem=ss, recv_sem=rs,
            device_id=device(**where), device_id_type=MESH)

    other_core = x * 4 + yh * 2 + 1 - k
    other_half = x * 4 + (1 - yh) * 2 + k

    barrier = pltpu.get_barrier_semaphore()

    def greet(**where):
        pl.semaphore_signal(barrier, inc=1, device_id=device(**where), device_id_type=MESH)

    def greet_cams(i):
        greet(cam=(c + 1) & 7, frame=i)
        greet(cam=(c + 7) & 7, frame=i)

    loads = [
        pltpu.make_async_copy(src, dst, in_sem.at[i])
        for i, (src, dst) in enumerate(
            ((k_hbm, k_in), (v_hbm, v_in), (q_hbm, q_in), (g_hbm, gfull.at[hh]), (w_hbm, w),
             (offs_hbm, offs)))
    ]
    for load in loads:
        load.start()
    each(16, greet_cams)
    each(7, lambda i: greet(frame=frame_of((u + 1 + i) & 7)))
    each(5, lambda i: greet(cam=(c + 2 + i) & 7))
    greet(frame=other_half)
    greet(head=1 - hh)

    loads[5].wait()
    off = (offs[1, (c + 7) % 8], offs[0, c])
    sel = [selector(o) for o in off]

    def strip(ref, side):
        window = ref[:, :, side * 32:(side + 1) * 32, :].reshape(256, 512)
        return dot(sel[side], window).astype(BF)

    for i, ref in enumerate((k_in, v_in)):
        loads[i].wait()
        for side in range(2):
            cut = strip(ref, side)
            for h in range(4):
                kv_send[h * 2 + 1 - side, i] = cut[:, h * 128:(h + 1) * 128]

    loads[3].wait()
    pl.semaphore_wait(barrier, 46)
    g_copy = remote(gfull.at[hh], gfull.at[hh], g_ss, g_rs, head=1 - hh)
    g_copy.start()

    def kv_copy(i):
        unit, half = (u + i) & 7, (yh + 1 + (i >> 3)) & 1
        to_cam = (c + 9 - 2 * (unit & 1)) & 7
        to_frame = (unit >> 1) * 4 + half * 2 + (unit & 1)
        return remote(kv_send.at[unit], kv_recv.at[yh, u], kv_ss.at[i], kv_rs.at[yh * 8 + u],
                      cam=to_cam, frame=to_frame)

    each(16, lambda i: kv_copy(i).start())

    loads[2].wait()
    for side in range(2):
        cut = strip(q_in, side)
        for h in range(4):
            q_send[h * 2 + side] = cut[:, h * 128:(h + 1) * 128]

    def half_copy(send, recv, ss, rs, i):
        unit = (u + i) & 7
        return remote(send.at[unit], recv.at[u], ss.at[unit], rs.at[u], frame=frame_of(unit))

    def own_copy(send, recv, rs):
        return pltpu.make_async_copy(send.at[u], recv.at[u], rs.at[u])

    own_copy(q_send, q_recv, q_rs).start()
    each(7, lambda i: half_copy(q_send, q_recv, q_ss, q_rs, i + 1).start())

    def arrived(ref, sem):
        pltpu.make_async_copy(ref, ref, sem).wait()

    def kv_arrive(i):
        half, source = i >> 3, i & 7
        arrived(kv_recv.at[half, source], kv_rs.at[i])
        cols = pl.ds(pl.multiple_of(source * 128, 128), 128)
        vt[half, :, cols] = transposed(kv_recv[half, source, 1]).astype(BF)

    each(16, kv_arrive)

    def stacked(half, i):
        return kv_recv[half, :, i].reshape(1024, 128)

    def send_block(send, recv, ss, rs, unit):
        @pl.when(unit == u)
        def _():
            own_copy(send, recv, rs).start()

        @pl.when(unit != u)
        def _():
            remote(send.at[unit], recv.at[u], ss.at[unit], rs.at[u],
                   frame=frame_of(unit)).start()

    def forward(i):
        b = (x + i) & 3
        for t in range(2):
            arrived(q_recv.at[2 * b + t], q_rs.at[2 * b + t])
        queries = q_recv[pl.ds(2 * b, 2)].reshape(256, 128)
        scores = [dot_nt(stacked(half, 0), queries) for half in range(2)]
        top = jnp.maximum(jnp.max(scores[0], axis=0, keepdims=True),
                          jnp.max(scores[1], axis=0, keepdims=True))
        total, out_t = 0.0, 0.0
        for half in range(2):
            weights = jnp.exp2((scores[half] - top) * (scale * LOG2E))
            total = total + jnp.sum(weights, axis=0, keepdims=True)
            weights = weights.astype(BF)
            probs[half, b] = weights
            out_t = out_t + dot(vt[half], weights)
        inverse = 1.0 / total
        out_t = out_t * inverse
        o_t[b] = out_t
        rl[b] = inverse
        att_send[pl.ds(2 * b, 2)] = out_t.T.astype(BF).reshape(2, 128, 128)
        for t in range(2):
            send_block(att_send, att_recv, att_ss, att_rs, 2 * b + t)

    each(4, forward)

    arrived(gfull.at[1 - hh], g_rs)
    loads[4].wait()
    grad_attn = dot_nt(gfull[0], w[:, :1024]) + dot_nt(gfull[1], w[:, 1024:])
    grad_attn = grad_attn.astype(BF)
    for fr in range(2):
        for s in range(2):
            for h in range(4):
                do_send[h * 2 + s, fr * 64:(fr + 1) * 64] = grad_attn[
                    fr * 128 + s * 64:fr * 128 + s * 64 + 64, h * 128:(h + 1) * 128]
    own_copy(do_send, do_recv, do_rs).start()
    each(7, lambda i: half_copy(do_send, do_recv, do_ss, do_rs, i + 1).start())

    each(8, lambda i: arrived(att_recv.at[i], att_rs.at[i]))
    for fr in range(2):
        for s in range(2):
            for h in range(4):
                a_rows[fr * 128 + s * 64:fr * 128 + s * 64 + 64, h * 128:(h + 1) * 128] = att_recv[
                    h * 2 + s, fr * 64:(fr + 1) * 64]
    for fr in range(2):
        for h in range(4):
            a_t[h * 128:(h + 1) * 128, fr * 128:(fr + 1) * 128] = transposed(
                a_rows[fr * 128:(fr + 1) * 128, h * 128:(h + 1) * 128]).astype(BF)

    def core_copy(p):
        part = pl.ds(p * 64, 64)
        return remote(core_send.at[part], core_recv.at[part], core_ss.at[p], core_rs.at[p],
                      frame=other_core)

    def multiply():
        theirs = a_t[pl.ds(pl.multiple_of((1 - k) * 256, 256), 256), :]
        for j in range(2):
            core_send[:, j * 1024:(j + 1) * 1024] = dot(theirs, gfull[j]).astype(BF)
        for p in range(4):
            core_copy(p).start()
        mine = a_t[pl.ds(pl.multiple_of(k * 256, 256), 256), :]
        for j in range(2):
            own[:, j * 1024:(j + 1) * 1024] = dot(mine, gfull[j])

    def peers(axis):
        if axis == "x":
            return [((x + i) & 3, dict(frame=frame_x((x + i) & 3))) for i in (1, 3, 2)]
        return [((c + i) & 7, dict(cam=(c + i) & 7)) for i in (1, 7, 2, 6, 3, 5, 4)]

    def area(p, axes, at_x=x, at_z=c, base=0):
        rows, cols = pl.ds(base + p * 64, 64), pl.ds(0, 2048)
        if "x" in axes:
            rows = pl.ds(pl.multiple_of(base + p * 64 + at_x * 16, 16), 16)
        elif not isinstance(base, int):
            rows = pl.ds(pl.multiple_of(base + p * 64, 64), 64)
        if "z" in axes:
            cols = pl.ds(pl.multiple_of(at_z * 256, 256), 256)
        return rows, cols

    def me(axis):
        return x if axis == "x" else c

    def sum_copy(src, dst, p, step, where):
        return remote(src, dst, sum_ss.at[p, step], sum_rs.at[p, step], **where)

    def batch(recv, p, axis):
        return recv[p].at[pl.ds(0, 3 if axis == "x" else 7)]

    def first_sent(p):
        arrived(batch(first_recv, p, PIECES[p][0]), sum_ss.at[p, 0])

    def first(p):
        part = pl.ds(p * 64, 64)
        axis = PIECES[p][0]
        arrived(core_recv.at[part], core_rs.at[p])
        own[part, :] += core_recv[part, :].astype(F32)
        out_bf[part, :] = own[part, :].astype(BF)
        for to, where in peers(axis):
            src = out_bf.at[area(p, axis, to, to)]
            sum_copy(src, first_recv[p].at[me(axis)], p, 0, where).start()

    def second(p):
        axis, other = PIECES[p]
        arrived(batch(first_recv, p, axis), sum_rs.at[p, 0])
        total = own[area(p, axis)]
        for frm, _ in peers(axis):
            total = total + first_recv[p][frm].astype(F32)
        mid_sum[p][...] = total.astype(BF)
        for to, where in peers(other):
            sum_copy(mid_sum[p].at[mid_part(p, to)], second_recv[p].at[me(other)], p, 1, where).start()

    def mid_part(p, to):
        if PIECES[p][1] == "x":
            return pl.ds(pl.multiple_of(to * 16, 16), 16), pl.ds(0, 256)
        return pl.ds(0, 16), pl.ds(pl.multiple_of(to * 256, 256), 256)

    def y_copy(p):
        return sum_copy(y_send.at[p], y_recv.at[p], p, 2, dict(frame=other_half))

    def third(p):
        axis = PIECES[p][1]
        arrived(batch(second_recv, p, axis), sum_rs.at[p, 1])
        total = mid_sum[p][mid_part(p, me(axis))].astype(F32)
        for frm, _ in peers(axis):
            total = total + second_recv[p][frm].astype(F32)
        y_send[p] = total.astype(BF)
        y_copy(p).start()

    def gather(p, axes, axis, step):
        part = gw.at[area(p, axes, base=k * 256)]
        for _, where in peers(axis):
            sum_copy(part, part, p, step, where).start()

    def fourth(p):
        arrived(y_recv.at[p], sum_rs.at[p, 2])
        gw[area(p, "xz", base=k * 256)] = (
            y_send[p].astype(F32) + y_recv[p].astype(F32)).astype(BF)
        gather(p, "xz", PIECES[p][1], 3)

    def fifth(p):
        arrived(batch(second_recv, p, PIECES[p][1]), sum_rs.at[p, 3])
        gather(p, PIECES[p][0], PIECES[p][0], 4)

    def sixth(p):
        arrived(batch(first_recv, p, PIECES[p][0]), sum_rs.at[p, 4])
        part = gw.at[area(p, "", base=k * 256)]
        sum_copy(part, part, p, 5, dict(frame=other_core)).start()
        gw_write(p, k).start()

    def seventh(p):
        arrived(gw.at[area(p, "", base=(1 - k) * 256)], sum_rs.at[p, 5])
        gw_write(p, 1 - k).start()

    def gw_write(p, core):
        at = area(p, "", base=core * 256)
        return pltpu.make_async_copy(gw.at[at], gw_hbm.at[at], out_sem.at[3 + p * 2 + core])

    def backward(half, i):
        b = (x + i) & 3
        if half is far:
            for t in range(2):
                arrived(do_recv.at[2 * b + t], do_rs.at[2 * b + t])
        queries = q_recv[pl.ds(2 * b, 2)].reshape(256, 128)
        weights = probs[half, b]
        grad_t = transposed(do_recv[pl.ds(2 * b, 2)].reshape(256, 128)) * rl[b]
        delta = jnp.sum(grad_t * o_t[b], axis=0, keepdims=True)
        grads = grad_t.T.astype(BF)
        grad_probs = dot(stacked(half, 1), grad_t.astype(BF))
        grad_scores = (weights.astype(F32) * (grad_probs - delta)).astype(BF)
        grad_q_t = dot(kt[half], grad_scores)
        if half is far:
            dq_acc[b] = grad_q_t
        else:
            grad_q_t = (grad_q_t + dq_acc[b]) * scale
            dq_send[pl.ds(2 * b, 2)] = grad_q_t.T.astype(BF).reshape(2, 128, 128)
            for t in range(2):
                send_block(dq_send, dq_recv, dq_ss, dq_rs, 2 * b + t)
        if i == 0:
            dk_acc[...] = dot(grad_scores, queries)
            dv_acc[...] = dot(weights, grads)
        else:
            dk_acc[...] += dot(grad_scores, queries)
            dv_acc[...] += dot(weights, grads)

    def far_copy():
        return remote(far_send, far_recv, far_ss, far_rs, frame=other_half)

    def dkv_copy(i):
        source = (u + i) & 7
        return remote(dkv_send.at[source], dkv_recv.at[u], dkv_ss.at[i], dkv_rs.at[u],
                      cam=(c + 7 + 2 * k) & 7, frame=frame_of(source))

    far, near = 1 - yh, yh

    def key_turn(i):
        half, source = i >> 3, i & 7
        kt[half, :, pl.ds(pl.multiple_of(source * 128, 128), 128)] = transposed(
            kv_recv[half, source, 0]).astype(BF)

    multiply()
    first(0)
    first(1)
    lo_send[...] = dot(
        a_rows[...], w[:, pl.ds(pl.multiple_of((1 - hh) * 1024, 1024), 1024)]).astype(BF)
    lo_copy = remote(lo_send, lo_recv, lo_ss, lo_rs, head=1 - hh)
    lo_copy.start()
    each(16, key_turn)
    first_sent(0)
    first(2)
    backward(far, 0)
    second(0)
    backward(far, 1)
    first_sent(2)
    first(3)
    backward(far, 2)
    second(1)
    backward(far, 3)
    far_send[:, 0] = dk_acc[...].astype(BF).reshape(8, 128, 128)
    far_send[:, 1] = dv_acc[...].astype(BF).reshape(8, 128, 128)
    far_copy().start()
    second(2)
    third(0)
    backward(near, 0)
    second(3)
    third(1)
    backward(near, 1)
    third(2)
    fourth(0)
    backward(near, 2)
    third(3)
    fourth(1)
    fourth(2)
    backward(near, 3)
    fourth(3)
    fifth(0)
    fifth(1)
    far_copy().wait()
    for i, acc in enumerate((dk_acc, dv_acc)):
        total = acc[...].reshape(8, 128, 128) + far_recv[:, i].astype(F32)
        if i == 0:
            total = total * scale
        dkv_send[:, i] = total.astype(BF)
    each(8, lambda i: dkv_copy(i).start())
    fifth(2)
    fifth(3)

    here = dot(a_rows[...], w[:, pl.ds(pl.multiple_of(hh * 1024, 1024), 1024)])
    lo_copy.wait()
    lo_done[...] = (here + lo_recv[...].astype(F32)).astype(BF)
    lo_write = pltpu.make_async_copy(lo_done, lo_hbm, out_sem.at[0])
    lo_write.start()
    sixth(0)
    sixth(1)
    each(8, lambda i: arrived(dq_recv.at[i], dq_rs.at[i]))
    dq_write = pltpu.make_async_copy(dq_recv, dq_hbm, out_sem.at[1])
    dq_write.start()
    sixth(2)
    seventh(0)
    seventh(1)
    sixth(3)
    each(8, lambda i: arrived(dkv_recv.at[i], dkv_rs.at[i]))
    dkv_write = pltpu.make_async_copy(dkv_recv, dkv_hbm, out_sem.at[2])
    dkv_write.start()
    seventh(2)
    seventh(3)

    g_copy.wait_send()
    each(16, lambda i: kv_copy(i).wait_send())

    def sent(send, recv, ss, rs):
        each(7, lambda i: half_copy(send, recv, ss, rs, i + 1).wait_send())

    sent(q_send, q_recv, q_ss, q_rs)
    sent(do_send, do_recv, do_ss, do_rs)
    sent(att_send, att_recv, att_ss, att_rs)
    sent(dq_send, dq_recv, dq_ss, dq_rs)
    each(8, lambda i: dkv_copy(i).wait_send())
    first_sent(1)
    first_sent(3)
    for p in range(4):
        axis, other = PIECES[p]
        core_copy(p).wait_send()
        arrived(batch(second_recv, p, other), sum_ss.at[p, 1])
        y_copy(p).wait_send()
        arrived(batch(second_recv, p, other), sum_ss.at[p, 3])
        arrived(batch(first_recv, p, axis), sum_ss.at[p, 4])
        arrived(gw.at[area(p, "", base=k * 256)], sum_ss.at[p, 5])
        gw_write(p, k).wait()
        gw_write(p, 1 - k).wait()
    lo_write.wait()
    dq_write.wait()
    dkv_write.wait()


def place_kernel(
    offs_hbm, lo_hbm, dq_hbm, dkv_hbm, gw_hbm, layer_hbm, gq_hbm, gk_hbm, gv_hbm, gwo_hbm,
    offs, dq, dkv, gw, lo, grid, rows, in_sem, out_sem,
):
    c = lax.axis_index("cam")
    loads = [pltpu.make_async_copy(offs_hbm, offs, in_sem.at[0]),
             pltpu.make_async_copy(dq_hbm, dq, in_sem.at[1]),
             pltpu.make_async_copy(dkv_hbm, dkv, in_sem.at[2]),
             pltpu.make_async_copy(lo_hbm, lo, in_sem.at[3])]
    part = [pl.ds(r * 128, 128) for r in range(4)]
    loads += [pltpu.make_async_copy(gw_hbm.at[part[r]], gw.at[part[r]], in_sem.at[4 + r])
              for r in range(4)]
    for load in loads:
        load.start()
    loads[0].wait()
    off = (offs[1, (c + 7) % 8], offs[0, c])
    sel = [selector_t(o) for o in off]
    writes = []

    def write(src, dst):
        writes.append(pltpu.make_async_copy(src, dst, out_sem.at[len(writes)]))
        writes[-1].start()

    for n, out in enumerate((gq_hbm, gk_hbm, gv_hbm)):
        if n < 2:
            loads[1 + n].wait()
        for side in range(2):
            for h in range(4):
                unit = h * 2 + (side if n == 0 else 1 - side)
                if n == 0:
                    placed = dot(sel[side], dq[unit])
                else:
                    placed = dot(sel[side], dkv[unit, n - 1])
                grid[n, :, :, side * 32:(side + 1) * 32, h * 128:(h + 1) * 128] = placed.reshape(
                    2, 4, 32, 128)
        write(grid.at[n], out)
    loads[3].wait()
    write(lo, layer_hbm)
    for r in range(4):
        loads[4 + r].wait()
        rows[part[r], :] = gw[part[r], :].astype(F32)
        write(rows.at[part[r]], gwo_hbm.at[part[r]])
    for copy in writes:
        copy.wait()


def on_device(queries, keys, values, offsets, w_out, grad_out):
    field = queries.shape[1:]
    dma = pltpu.SemaphoreType.DMA
    any_spec = pl.BlockSpec(memory_space=pl.ANY)
    tile = (128, 128)

    def buf(*shape):
        return pltpu.VMEM(shape, BF)

    mid = [
        jax.ShapeDtypeStruct((256, 1024), BF),
        jax.ShapeDtypeStruct((8,) + tile, BF),
        jax.ShapeDtypeStruct((8, 2) + tile, BF),
        jax.ShapeDtypeStruct((512, 2048), BF),
    ]
    offs = offsets.T
    parts = pl.pallas_call(
        main_kernel,
        out_shape=mid,
        in_specs=[any_spec] * 6,
        out_specs=[any_spec] * 4,
        scratch_shapes=[
            pltpu.SMEM((2, 8), jnp.int32),
            buf(*field), buf(*field), buf(*field), buf(512, 2048), buf(2, 256, 1024),
            buf(8, *tile), buf(8, 2, *tile), buf(8, *tile),
            buf(8, *tile), buf(2, 8, 2, *tile), buf(8, *tile),
            buf(2, 128, 1024), buf(2, 128, 1024), buf(2, 4, 1024, 256),
            pltpu.VMEM((4, 128, 256), F32), pltpu.VMEM((4, 1, 256), F32),
            buf(8, *tile), buf(8, *tile), pltpu.VMEM((4, 128, 256), F32), buf(8, *tile), buf(8, *tile),
            pltpu.VMEM((1024, 128), F32), pltpu.VMEM((1024, 128), F32),
            buf(8, 2, *tile), buf(8, 2, *tile), buf(8, 2, *tile), buf(8, 2, *tile),
            buf(256, 512), buf(512, 256), buf(256, 2048), buf(256, 2048),
            pltpu.VMEM((256, 2048), F32), buf(256, 1024), buf(256, 1024), buf(256, 1024),
            buf(256, 2048), buf(512, 2048),
            [buf(4, 16, 2048) if axes == "xz" else buf(8, 64, 256) for axes in PIECES],
            [buf(16, 2048) if axes == "xz" else buf(64, 256) for axes in PIECES],
            [buf(8, 16, 256) if axes == "xz" else buf(4, 16, 256) for axes in PIECES],
            buf(4, 16, 256), buf(4, 16, 256),
            dma((6,)), dma((11,)), dma, dma, dma((8,)), dma((8,)), dma((16,)), dma((16,)),
            dma((8,)), dma((8,)),
            dma((8,)), dma((8,)), dma((8,)), dma((8,)), dma, dma, dma((8,)), dma((8,)),
            dma((4,)), dma((4,)), dma, dma,
            dma((4, 6)), dma((4, 6)),
        ],
        compiler_params=pltpu.CompilerParams(
            collective_id=0, has_side_effects=True, vmem_limit_bytes=56 * 1024 * 1024),
        cost_estimate=pl.CostEstimate(
            flops=5 * 10**9, bytes_accessed=10 * 2**20, transcendentals=2 * 2**20),
        name="strip_attention",
    )(offs, queries.reshape(field), keys.reshape(field), values.reshape(field), w_out,
      grad_out.reshape(256, 1024))

    grid = jax.ShapeDtypeStruct(field, F32)
    layer, gq, gk, gv, gwo = pl.pallas_call(
        place_kernel,
        out_shape=(mid[0], grid, grid, grid, jax.ShapeDtypeStruct((512, 2048), F32)),
        in_specs=[any_spec] * 5,
        out_specs=(any_spec,) * 5,
        scratch_shapes=[
            pltpu.SMEM((2, 8), jnp.int32), buf(8, *tile), buf(8, 2, *tile), buf(512, 2048),
            buf(256, 1024), pltpu.VMEM((3,) + field, F32), pltpu.VMEM((512, 2048), F32),
            dma((8,)), dma((8,))],
        compiler_params=pltpu.CompilerParams(vmem_limit_bytes=60 * 1024 * 1024),
        cost_estimate=pl.CostEstimate(
            flops=10**8, bytes_accessed=10 * 2**20, transcendentals=0),
        name="place_gradients",
    )(offs, *parts)
    shape = queries.shape
    return (layer.reshape(grad_out.shape), gq.reshape(shape), gk.reshape(shape), gv.reshape(shape),
            gwo)


def solution(mesh):
    field = P("cam", "frame", None, None, "head")
    rows = P("cam", "frame", None, None, None, "head")
    return jax.shard_map(
        on_device,
        mesh=mesh,
        in_specs=(field, field, field, P(), P("head", None), rows),
        out_specs=(rows, field, field, field, P("head", None)),
        check_vma=False,
    )
```

```python
import functools

import jax
import jax.numpy as jnp
from jax import lax
from jax.experimental import pallas as pl
from jax.experimental.pallas import tpu as pltpu
from jax.sharding import PartitionSpec as P

HD = 128
BF = jnp.bfloat16
F32 = jnp.float32
MESH = pl.DeviceIdType.MESH
LOG2E = 1.4426950408889634
NT = (((1,), (1,)), ((), ()))
PIECES = ("xz", "zx", "xz", "xz")


def dot(a, b):
    return jnp.dot(a, b, preferred_element_type=F32)


def dot_nt(a, b):
    return lax.dot_general(a, b, NT, preferred_element_type=F32)


def each(count, fn):
    def step(i, carry):
        fn(i)
        return carry

    lax.fori_loop(0, count, step, 0)


def transposed(block):
    return block.astype(F32).T


def selector(off):
    rows = lax.broadcasted_iota(jnp.int32, (128, 256), 0)
    cols = lax.broadcasted_iota(jnp.int32, (128, 256), 1)
    hit = cols == rows + (lax.shift_right_logical(rows, 4) * 16 + off)
    return jnp.where(hit, 1.0, 0.0).astype(BF)


def selector_t(off):
    rows = lax.broadcasted_iota(jnp.int32, (256, 128), 1)
    cols = lax.broadcasted_iota(jnp.int32, (256, 128), 0)
    hit = cols == rows + (lax.shift_right_logical(rows, 4) * 16 + off)
    return jnp.where(hit, 1.0, 0.0).astype(BF)


def main_kernel(
    offs_hbm, q_hbm, k_hbm, v_hbm, w_hbm, g_hbm,
    lo_hbm, dq_hbm, dkv_hbm, gw_hbm,
    offs, q_in, k_in, v_in, w, gfull,
    q_send, kv_send, do_send, q_recv, kv_recv, do_recv,
    kt, vt, probs, o_t, rl,
    att_send, att_recv, dq_acc, dq_send, dq_recv, dk_acc, dv_acc, far_send, far_recv, dkv_send, dkv_recv,
    a_rows, a_t, core_send, core_recv, own, lo_send, lo_recv, lo_done,
    out_bf, gw, first_recv, mid_sum, second_recv, y_send, y_recv,
    in_sem, out_sem, g_ss, g_rs, q_ss, q_rs, kv_ss, kv_rs, do_ss, do_rs,
    att_ss, att_rs, dq_ss, dq_rs, far_ss, far_rs, dkv_ss, dkv_rs, core_ss, core_rs, lo_ss, lo_rs,
    sum_ss, sum_rs,
):
    c = lax.axis_index("cam")
    f = lax.axis_index("frame")
    hh = lax.axis_index("head")
    x, yh, k = f >> 2, (f >> 1) & 1, f & 1
    u = x * 2 + k
    scale = HD ** (-0.5)

    def frame_of(unit):
        return (unit >> 1) * 4 + yh * 2 + (unit & 1)

    def frame_x(to_x):
        return to_x * 4 + yh * 2 + k

    def device(cam=c, frame=f, head=hh):
        return (cam, frame, head)

    def remote(src, dst, ss, rs, **where):
        return pltpu.make_async_remote_copy(
            src_ref=src, dst_ref=dst, send_sem=ss, recv_sem=rs,
            device_id=device(**where), device_id_type=MESH)

    other_core = x * 4 + yh * 2 + 1 - k
    other_half = x * 4 + (1 - yh) * 2 + k

    barrier = pltpu.get_barrier_semaphore()

    def greet(**where):
        pl.semaphore_signal(barrier, inc=1, device_id=device(**where), device_id_type=MESH)

    def greet_cams(i):
        greet(cam=(c + 1) & 7, frame=i)
        greet(cam=(c + 7) & 7, frame=i)

    loads = [
        pltpu.make_async_copy(src, dst, in_sem.at[i])
        for i, (src, dst) in enumerate(
            ((k_hbm, k_in), (v_hbm, v_in), (q_hbm, q_in), (g_hbm, gfull.at[hh]), (w_hbm, w),
             (offs_hbm, offs)))
    ]
    for load in loads:
        load.start()
    each(16, greet_cams)
    each(7, lambda i: greet(frame=frame_of((u + 1 + i) & 7)))
    each(5, lambda i: greet(cam=(c + 2 + i) & 7))
    greet(frame=other_half)
    greet(head=1 - hh)

    loads[5].wait()
    off = (offs[1, (c + 7) % 8], offs[0, c])
    sel = [selector(o) for o in off]

    def strip(ref, side):
        window = ref[:, :, side * 32:(side + 1) * 32, :].reshape(256, 512)
        return dot(sel[side], window).astype(BF)

    for i, ref in enumerate((k_in, v_in)):
        loads[i].wait()
        for side in range(2):
            cut = strip(ref, side)
            for h in range(4):
                kv_send[h * 2 + 1 - side, i] = cut[:, h * 128:(h + 1) * 128]

    pl.semaphore_wait(barrier, 46)

    def kv_copy(i):
        unit, half = (u + i) & 7, (yh + 1 + (i >> 3)) & 1
        to_cam = (c + 9 - 2 * (unit & 1)) & 7
        to_frame = (unit >> 1) * 4 + half * 2 + (unit & 1)
        return remote(kv_send.at[unit], kv_recv.at[yh, u], kv_ss.at[i], kv_rs.at[yh * 8 + u],
                      cam=to_cam, frame=to_frame)

    each(16, lambda i: kv_copy(i).start())

    loads[2].wait()
    for side in range(2):
        cut = strip(q_in, side)
        for h in range(4):
            q_send[h * 2 + side] = cut[:, h * 128:(h + 1) * 128]

    def half_copy(send, recv, ss, rs, i):
        unit = (u + i) & 7
        return remote(send.at[unit], recv.at[u], ss.at[unit], rs.at[u], frame=frame_of(unit))

    def own_copy(send, recv, rs):
        return pltpu.make_async_copy(send.at[u], recv.at[u], rs.at[u])

    own_copy(q_send, q_recv, q_rs).start()
    each(7, lambda i: half_copy(q_send, q_recv, q_ss, q_rs, i + 1).start())
    loads[3].wait()
    g_copy = remote(gfull.at[hh], gfull.at[hh], g_ss, g_rs, head=1 - hh)
    g_copy.start()

    def arrived(ref, sem):
        pltpu.make_async_copy(ref, ref, sem).wait()

    def kv_arrive(i):
        half, source = i >> 3, i & 7
        arrived(kv_recv.at[half, source], kv_rs.at[i])
        cols = pl.ds(pl.multiple_of(source * 128, 128), 128)
        vt[half, :, cols] = transposed(kv_recv[half, source, 1]).astype(BF)

    each(16, kv_arrive)

    def stacked(half, i):
        return kv_recv[half, :, i].reshape(1024, 128)

    def send_block(send, recv, ss, rs, unit):
        @pl.when(unit == u)
        def _():
            own_copy(send, recv, rs).start()

        @pl.when(unit != u)
        def _():
            remote(send.at[unit], recv.at[u], ss.at[unit], rs.at[u],
                   frame=frame_of(unit)).start()

    def forward(i):
        b = (x + i) & 3
        for t in range(2):
            arrived(q_recv.at[2 * b + t], q_rs.at[2 * b + t])
        queries = q_recv[pl.ds(2 * b, 2)].reshape(256, 128)
        scores = [dot_nt(stacked(half, 0), queries) for half in range(2)]
        top = jnp.maximum(jnp.max(scores[0], axis=0, keepdims=True),
                          jnp.max(scores[1], axis=0, keepdims=True))
        total, out_t = 0.0, 0.0
        for half in range(2):
            weights = jnp.exp2((scores[half] - top) * (scale * LOG2E))
            total = total + jnp.sum(weights, axis=0, keepdims=True)
            weights = weights.astype(BF)
            probs[half, b] = weights
            out_t = out_t + dot(vt[half], weights)
        inverse = 1.0 / total
        out_t = out_t * inverse
        o_t[b] = out_t
        rl[b] = inverse
        att_send[pl.ds(2 * b, 2)] = out_t.T.astype(BF).reshape(2, 128, 128)
        for t in range(2):
            send_block(att_send, att_recv, att_ss, att_rs, 2 * b + t)

    each(4, forward)

    arrived(gfull.at[1 - hh], g_rs)
    loads[4].wait()
    grad_attn = dot_nt(gfull[0], w[:, :1024]) + dot_nt(gfull[1], w[:, 1024:])
    grad_attn = grad_attn.astype(BF)
    for fr in range(2):
        for s in range(2):
            for h in range(4):
                do_send[h * 2 + s, fr * 64:(fr + 1) * 64] = grad_attn[
                    fr * 128 + s * 64:fr * 128 + s * 64 + 64, h * 128:(h + 1) * 128]
    own_copy(do_send, do_recv, do_rs).start()
    each(7, lambda i: half_copy(do_send, do_recv, do_ss, do_rs, i + 1).start())

    def key_turn(i):
        half, source = i >> 3, i & 7
        kt[half, :, pl.ds(pl.multiple_of(source * 128, 128), 128)] = transposed(
            kv_recv[half, source, 0]).astype(BF)

    each(16, key_turn)

    each(8, lambda i: arrived(att_recv.at[i], att_rs.at[i]))
    for fr in range(2):
        for s in range(2):
            for h in range(4):
                a_rows[fr * 128 + s * 64:fr * 128 + s * 64 + 64, h * 128:(h + 1) * 128] = att_recv[
                    h * 2 + s, fr * 64:(fr + 1) * 64]
    for fr in range(2):
        for h in range(4):
            a_t[h * 128:(h + 1) * 128, fr * 128:(fr + 1) * 128] = transposed(
                a_rows[fr * 128:(fr + 1) * 128, h * 128:(h + 1) * 128]).astype(BF)

    def core_copy(p):
        part = pl.ds(p * 64, 64)
        return remote(core_send.at[part], core_recv.at[part], core_ss.at[p], core_rs.at[p],
                      frame=other_core)

    def multiply():
        theirs = a_t[pl.ds(pl.multiple_of((1 - k) * 256, 256), 256), :]
        for j in range(2):
            core_send[:, j * 1024:(j + 1) * 1024] = dot(theirs, gfull[j]).astype(BF)
        for p in range(4):
            core_copy(p).start()
        mine = a_t[pl.ds(pl.multiple_of(k * 256, 256), 256), :]
        for j in range(2):
            own[:, j * 1024:(j + 1) * 1024] = dot(mine, gfull[j])

    def peers(axis):
        if axis == "x":
            return [((x + i) & 3, dict(frame=frame_x((x + i) & 3))) for i in (1, 3, 2)]
        return [((c + i) & 7, dict(cam=(c + i) & 7)) for i in (1, 7, 2, 6, 3, 5, 4)]

    def area(p, axes, at_x=x, at_z=c, base=0):
        rows, cols = pl.ds(base + p * 64, 64), pl.ds(0, 2048)
        if "x" in axes:
            rows = pl.ds(pl.multiple_of(base + p * 64 + at_x * 16, 16), 16)
        elif not isinstance(base, int):
            rows = pl.ds(pl.multiple_of(base + p * 64, 64), 64)
        if "z" in axes:
            cols = pl.ds(pl.multiple_of(at_z * 256, 256), 256)
        return rows, cols

    def me(axis):
        return x if axis == "x" else c

    def sum_copy(src, dst, p, step, where):
        return remote(src, dst, sum_ss.at[p, step], sum_rs.at[p, step], **where)

    def batch(recv, p, axis):
        return recv[p].at[pl.ds(0, 3 if axis == "x" else 7)]

    def first_sent(p):
        arrived(batch(first_recv, p, PIECES[p][0]), sum_ss.at[p, 0])

    def first(p):
        part = pl.ds(p * 64, 64)
        axis = PIECES[p][0]
        arrived(core_recv.at[part], core_rs.at[p])
        own[part, :] += core_recv[part, :].astype(F32)
        out_bf[part, :] = own[part, :].astype(BF)
        for to, where in peers(axis):
            src = out_bf.at[area(p, axis, to, to)]
            sum_copy(src, first_recv[p].at[me(axis)], p, 0, where).start()

    def second(p):
        axis, other = PIECES[p]
        arrived(batch(first_recv, p, axis), sum_rs.at[p, 0])
        total = own[area(p, axis)]
        for frm, _ in peers(axis):
            total = total + first_recv[p][frm].astype(F32)
        mid_sum[p][...] = total.astype(BF)
        for to, where in peers(other):
            sum_copy(mid_sum[p].at[mid_part(p, to)], second_recv[p].at[me(other)], p, 1, where).start()

    def mid_part(p, to):
        if PIECES[p][1] == "x":
            return pl.ds(pl.multiple_of(to * 16, 16), 16), pl.ds(0, 256)
        return pl.ds(0, 16), pl.ds(pl.multiple_of(to * 256, 256), 256)

    def y_copy(p):
        return sum_copy(y_send.at[p], y_recv.at[p], p, 2, dict(frame=other_half))

    def third(p):
        axis = PIECES[p][1]
        arrived(batch(second_recv, p, axis), sum_rs.at[p, 1])
        total = mid_sum[p][mid_part(p, me(axis))].astype(F32)
        for frm, _ in peers(axis):
            total = total + second_recv[p][frm].astype(F32)
        y_send[p] = total.astype(BF)
        y_copy(p).start()

    def gather(p, axes, axis, step):
        part = gw.at[area(p, axes, base=k * 256)]
        for _, where in peers(axis):
            sum_copy(part, part, p, step, where).start()

    def fourth(p):
        arrived(y_recv.at[p], sum_rs.at[p, 2])
        gw[area(p, "xz", base=k * 256)] = (
            y_send[p].astype(F32) + y_recv[p].astype(F32)).astype(BF)
        gather(p, "xz", PIECES[p][1], 3)

    def fifth(p):
        arrived(batch(second_recv, p, PIECES[p][1]), sum_rs.at[p, 3])
        gather(p, PIECES[p][0], PIECES[p][0], 4)

    def sixth(p):
        arrived(batch(first_recv, p, PIECES[p][0]), sum_rs.at[p, 4])
        part = gw.at[area(p, "", base=k * 256)]
        sum_copy(part, part, p, 5, dict(frame=other_core)).start()
        gw_write(p, k).start()

    def seventh(p):
        arrived(gw.at[area(p, "", base=(1 - k) * 256)], sum_rs.at[p, 5])
        gw_write(p, 1 - k).start()

    def gw_write(p, core):
        at = area(p, "", base=core * 256)
        return pltpu.make_async_copy(gw.at[at], gw_hbm.at[at], out_sem.at[3 + p * 2 + core])

    def backward(half, i):
        b = (x + i) & 3
        if half is far:
            for t in range(2):
                arrived(do_recv.at[2 * b + t], do_rs.at[2 * b + t])
        queries = q_recv[pl.ds(2 * b, 2)].reshape(256, 128)
        weights = probs[half, b]
        grad_t = transposed(do_recv[pl.ds(2 * b, 2)].reshape(256, 128)) * rl[b]
        delta = jnp.sum(grad_t * o_t[b], axis=0, keepdims=True)
        grads = grad_t.T.astype(BF)
        grad_probs = dot(stacked(half, 1), grad_t.astype(BF))
        grad_scores = (weights.astype(F32) * (grad_probs - delta)).astype(BF)
        grad_q_t = dot(kt[half], grad_scores)
        if half is far:
            dq_acc[b] = grad_q_t
        else:
            grad_q_t = (grad_q_t + dq_acc[b]) * scale
            dq_send[pl.ds(2 * b, 2)] = grad_q_t.T.astype(BF).reshape(2, 128, 128)
            for t in range(2):
                send_block(dq_send, dq_recv, dq_ss, dq_rs, 2 * b + t)
        if i == 0:
            dk_acc[...] = dot(grad_scores, queries)
            dv_acc[...] = dot(weights, grads)
        else:
            dk_acc[...] += dot(grad_scores, queries)
            dv_acc[...] += dot(weights, grads)

    def far_copy():
        return remote(far_send, far_recv, far_ss, far_rs, frame=other_half)

    def dkv_copy(i):
        source = (u + i) & 7
        return remote(dkv_send.at[source], dkv_recv.at[u], dkv_ss.at[i], dkv_rs.at[u],
                      cam=(c + 7 + 2 * k) & 7, frame=frame_of(source))

    far, near = 1 - yh, yh

    multiply()
    for i in range(4):
        backward(far, i)
    far_send[:, 0] = dk_acc[...].astype(BF).reshape(8, 128, 128)
    far_send[:, 1] = dv_acc[...].astype(BF).reshape(8, 128, 128)
    far_copy().start()
    first(0)
    first(1)
    backward(near, 0)
    first_sent(0)
    first(2)
    backward(near, 1)
    second(0)
    first_sent(2)
    first(3)
    backward(near, 2)
    second(1)
    backward(near, 3)
    second(2)
    third(0)
    second(3)
    third(1)
    third(2)
    fourth(0)
    third(3)
    fourth(1)
    fourth(2)
    fourth(3)
    lo_send[...] = dot(
        a_rows[...], w[:, pl.ds(pl.multiple_of((1 - hh) * 1024, 1024), 1024)]).astype(BF)
    lo_copy = remote(lo_send, lo_recv, lo_ss, lo_rs, head=1 - hh)
    lo_copy.start()
    fifth(0)
    fifth(1)
    far_copy().wait()
    for i, acc in enumerate((dk_acc, dv_acc)):
        total = acc[...].reshape(8, 128, 128) + far_recv[:, i].astype(F32)
        if i == 0:
            total = total * scale
        dkv_send[:, i] = total.astype(BF)
    each(8, lambda i: dkv_copy(i).start())
    fifth(2)
    fifth(3)

    lo_done[...] = dot(
        a_rows[...], w[:, pl.ds(pl.multiple_of(hh * 1024, 1024), 1024)])
    each(8, lambda i: arrived(dq_recv.at[i], dq_rs.at[i]))
    dq_write = pltpu.make_async_copy(dq_recv, dq_hbm, out_sem.at[1])
    dq_write.start()
    sixth(0)
    sixth(1)
    sixth(2)
    sixth(3)
    each(8, lambda i: arrived(dkv_recv.at[i], dkv_rs.at[i]))
    dkv_write = pltpu.make_async_copy(dkv_recv, dkv_hbm, out_sem.at[2])
    dkv_write.start()
    lo_copy.wait()
    lo_send[...] = (lo_done[...] + lo_recv[...].astype(F32)).astype(BF)
    lo_write = pltpu.make_async_copy(lo_send, lo_hbm, out_sem.at[0])
    lo_write.start()
    for p in range(4):
        seventh(p)

    g_copy.wait_send()
    each(16, lambda i: kv_copy(i).wait_send())

    def sent(send, recv, ss, rs):
        each(7, lambda i: half_copy(send, recv, ss, rs, i + 1).wait_send())

    sent(q_send, q_recv, q_ss, q_rs)
    sent(do_send, do_recv, do_ss, do_rs)
    sent(att_send, att_recv, att_ss, att_rs)
    sent(dq_send, dq_recv, dq_ss, dq_rs)
    each(8, lambda i: dkv_copy(i).wait_send())
    first_sent(1)
    first_sent(3)
    for p in range(4):
        axis, other = PIECES[p]
        core_copy(p).wait_send()
        arrived(batch(second_recv, p, other), sum_ss.at[p, 1])
        y_copy(p).wait_send()
        arrived(batch(second_recv, p, other), sum_ss.at[p, 3])
        arrived(batch(first_recv, p, axis), sum_ss.at[p, 4])
        arrived(gw.at[area(p, "", base=k * 256)], sum_ss.at[p, 5])
        gw_write(p, k).wait()
        gw_write(p, 1 - k).wait()
    lo_write.wait()
    dq_write.wait()
    dkv_write.wait()


def place_kernel(
    offs_hbm, lo_hbm, dq_hbm, dkv_hbm, gw_hbm, layer_hbm, gq_hbm, gk_hbm, gv_hbm, gwo_hbm,
    offs, dq, dkv, gw, lo, grid, rows, in_sem, out_sem,
):
    c = lax.axis_index("cam")
    loads = [pltpu.make_async_copy(offs_hbm, offs, in_sem.at[0]),
             pltpu.make_async_copy(dq_hbm, dq, in_sem.at[1]),
             pltpu.make_async_copy(dkv_hbm, dkv, in_sem.at[2]),
             pltpu.make_async_copy(lo_hbm, lo, in_sem.at[3])]
    part = [pl.ds(r * 128, 128) for r in range(4)]
    loads += [pltpu.make_async_copy(gw_hbm.at[part[r]], gw.at[part[r]], in_sem.at[4 + r])
              for r in range(4)]
    for load in loads:
        load.start()
    loads[0].wait()
    off = (offs[1, (c + 7) % 8], offs[0, c])
    sel = [selector_t(o) for o in off]
    writes = []

    def write(src, dst):
        writes.append(pltpu.make_async_copy(src, dst, out_sem.at[len(writes)]))
        writes[-1].start()

    for n, out in enumerate((gq_hbm, gk_hbm, gv_hbm)):
        if n < 2:
            loads[1 + n].wait()
        for side in range(2):
            for h in range(4):
                unit = h * 2 + (side if n == 0 else 1 - side)
                if n == 0:
                    placed = dot(sel[side], dq[unit])
                else:
                    placed = dot(sel[side], dkv[unit, n - 1])
                grid[n, :, :, side * 32:(side + 1) * 32, h * 128:(h + 1) * 128] = placed.reshape(
                    2, 4, 32, 128)
        write(grid.at[n], out)
    loads[3].wait()
    write(lo, layer_hbm)
    for r in range(4):
        loads[4 + r].wait()
        rows[part[r], :] = gw[part[r], :].astype(F32)
        write(rows.at[part[r]], gwo_hbm.at[part[r]])
    for copy in writes:
        copy.wait()


def on_device(queries, keys, values, offsets, w_out, grad_out):
    field = queries.shape[1:]
    dma = pltpu.SemaphoreType.DMA
    any_spec = pl.BlockSpec(memory_space=pl.ANY)
    tile = (128, 128)

    def buf(*shape):
        return pltpu.VMEM(shape, BF)

    mid = [
        jax.ShapeDtypeStruct((256, 1024), BF),
        jax.ShapeDtypeStruct((8,) + tile, BF),
        jax.ShapeDtypeStruct((8, 2) + tile, BF),
        jax.ShapeDtypeStruct((512, 2048), BF),
    ]
    offs = offsets.T
    parts = pl.pallas_call(
        main_kernel,
        out_shape=mid,
        in_specs=[any_spec] * 6,
        out_specs=[any_spec] * 4,
        scratch_shapes=[
            pltpu.SMEM((2, 8), jnp.int32),
            buf(*field), buf(*field), buf(*field), buf(512, 2048), buf(2, 256, 1024),
            buf(8, *tile), buf(8, 2, *tile), buf(8, *tile),
            buf(8, *tile), buf(2, 8, 2, *tile), buf(8, *tile),
            buf(2, 128, 1024), buf(2, 128, 1024), buf(2, 4, 1024, 256),
            pltpu.VMEM((4, 128, 256), F32), pltpu.VMEM((4, 1, 256), F32),
            buf(8, *tile), buf(8, *tile), pltpu.VMEM((4, 128, 256), F32), buf(8, *tile), buf(8, *tile),
            pltpu.VMEM((1024, 128), F32), pltpu.VMEM((1024, 128), F32),
            buf(8, 2, *tile), buf(8, 2, *tile), buf(8, 2, *tile), buf(8, 2, *tile),
            buf(256, 512), buf(512, 256), buf(256, 2048), buf(256, 2048),
            pltpu.VMEM((256, 2048), F32), buf(256, 1024), buf(256, 1024), pltpu.VMEM((256, 1024), F32),
            buf(256, 2048), buf(512, 2048),
            [buf(4, 16, 2048) if axes == "xz" else buf(8, 64, 256) for axes in PIECES],
            [buf(16, 2048) if axes == "xz" else buf(64, 256) for axes in PIECES],
            [buf(8, 16, 256) if axes == "xz" else buf(4, 16, 256) for axes in PIECES],
            buf(4, 16, 256), buf(4, 16, 256),
            dma((6,)), dma((11,)), dma, dma, dma((8,)), dma((8,)), dma((16,)), dma((16,)),
            dma((8,)), dma((8,)),
            dma((8,)), dma((8,)), dma((8,)), dma((8,)), dma, dma, dma((8,)), dma((8,)),
            dma((4,)), dma((4,)), dma, dma,
            dma((4, 6)), dma((4, 6)),
        ],
        compiler_params=pltpu.CompilerParams(
            collective_id=0, has_side_effects=True, vmem_limit_bytes=56 * 1024 * 1024),
        cost_estimate=pl.CostEstimate(
            flops=5 * 10**9, bytes_accessed=10 * 2**20, transcendentals=2 * 2**20),
        name="strip_attention",
    )(offs, queries.reshape(field), keys.reshape(field), values.reshape(field), w_out,
      grad_out.reshape(256, 1024))

    grid = jax.ShapeDtypeStruct(field, F32)
    layer, gq, gk, gv, gwo = pl.pallas_call(
        place_kernel,
        out_shape=(mid[0], grid, grid, grid, jax.ShapeDtypeStruct((512, 2048), F32)),
        in_specs=[any_spec] * 5,
        out_specs=(any_spec,) * 5,
        scratch_shapes=[
            pltpu.SMEM((2, 8), jnp.int32), buf(8, *tile), buf(8, 2, *tile), buf(512, 2048),
            buf(256, 1024), pltpu.VMEM((3,) + field, F32), pltpu.VMEM((512, 2048), F32),
            dma((8,)), dma((8,))],
        compiler_params=pltpu.CompilerParams(vmem_limit_bytes=60 * 1024 * 1024),
        cost_estimate=pl.CostEstimate(
            flops=10**8, bytes_accessed=10 * 2**20, transcendentals=0),
        name="place_gradients",
    )(offs, *parts)
    shape = queries.shape
    return (layer.reshape(grad_out.shape), gq.reshape(shape), gk.reshape(shape), gv.reshape(shape),
            gwo)


def solution(mesh):
    field = P("cam", "frame", None, None, "head")
    rows = P("cam", "frame", None, None, None, "head")
    return jax.shard_map(
        on_device,
        mesh=mesh,
        in_specs=(field, field, field, P(), P("head", None), rows),
        out_specs=(rows, field, field, field, P("head", None)),
        check_vma=False,
    )
```

```python
import functools

import jax
import jax.numpy as jnp
from jax import lax
from jax.experimental import pallas as pl
from jax.experimental.pallas import tpu as pltpu
from jax.sharding import PartitionSpec as P

HD = 128
BF = jnp.bfloat16
F32 = jnp.float32
MESH = pl.DeviceIdType.MESH
LOG2E = 1.4426950408889634
NT = (((1,), (1,)), ((), ()))
PIECES = ("xz", "zx", "xz", "xz")


def dot(a, b):
    return jnp.dot(a, b, preferred_element_type=F32)


def dot_nt(a, b):
    return lax.dot_general(a, b, NT, preferred_element_type=F32)


def each(count, fn):
    def step(i, carry):
        fn(i)
        return carry

    lax.fori_loop(0, count, step, 0)


def transposed(block):
    return block.astype(F32).T


def selector(off):
    rows = lax.broadcasted_iota(jnp.int32, (128, 256), 0)
    cols = lax.broadcasted_iota(jnp.int32, (128, 256), 1)
    hit = cols == rows + (lax.shift_right_logical(rows, 4) * 16 + off)
    return jnp.where(hit, 1.0, 0.0).astype(BF)


def selector_t(off):
    rows = lax.broadcasted_iota(jnp.int32, (256, 128), 1)
    cols = lax.broadcasted_iota(jnp.int32, (256, 128), 0)
    hit = cols == rows + (lax.shift_right_logical(rows, 4) * 16 + off)
    return jnp.where(hit, 1.0, 0.0).astype(BF)


def main_kernel(
    offs_hbm, q_hbm, k_hbm, v_hbm, w_hbm, g_hbm,
    lo_hbm, dq_hbm, dkv_hbm, gw_hbm,
    offs, q_in, k_in, v_in, w, gfull,
    q_send, kv_send, do_send, q_recv, kv_recv, do_recv,
    kt, vt, probs, o_t, rl,
    att_send, att_recv, dq_acc, dq_send, dq_recv, dk_acc, dv_acc, far_send, far_recv, dkv_send, dkv_recv,
    a_rows, a_t, core_send, core_recv, own, lo_send, lo_recv, lo_done,
    out_bf, gw, first_recv, mid_sum, second_recv, y_send, y_recv,
    in_sem, out_sem, g_ss, g_rs, q_ss, q_rs, kv_ss, kv_rs, hand_ss, hand_rs, do_ss, do_rs,
    att_ss, att_rs, dq_ss, dq_rs, far_ss, far_rs, dkv_ss, dkv_rs, core_ss, core_rs, lo_ss, lo_rs,
    sum_ss, sum_rs,
):
    c = lax.axis_index("cam")
    f = lax.axis_index("frame")
    hh = lax.axis_index("head")
    x, yh, k = f >> 2, (f >> 1) & 1, f & 1
    u = x * 2 + yh
    scale = HD ** (-0.5)

    def frame_of(unit):
        return unit * 2 + k

    def frame_x(to_x):
        return to_x * 4 + yh * 2 + k

    def device(cam=c, frame=f, head=hh):
        return (cam, frame, head)

    def remote(src, dst, ss, rs, **where):
        return pltpu.make_async_remote_copy(
            src_ref=src, dst_ref=dst, send_sem=ss, recv_sem=rs,
            device_id=device(**where), device_id_type=MESH)

    other_core = x * 4 + yh * 2 + 1 - k
    other_half = x * 4 + (1 - yh) * 2 + k

    barrier = pltpu.get_barrier_semaphore()

    def greet(**where):
        pl.semaphore_signal(barrier, inc=1, device_id=device(**where), device_id_type=MESH)

    def greet_cams(i):
        greet(cam=(c + 1) & 7, frame=frame_of(i))
        greet(cam=(c + 7) & 7, frame=frame_of(i))

    loads = [
        pltpu.make_async_copy(src, dst, in_sem.at[i])
        for i, (src, dst) in enumerate(
            ((k_hbm, k_in), (v_hbm, v_in), (q_hbm, q_in), (g_hbm, gfull.at[hh]), (w_hbm, w),
             (offs_hbm, offs)))
    ]
    for load in loads:
        load.start()
    each(8, greet_cams)
    each(7, lambda i: greet(frame=frame_of((u + 1 + i) & 7)))
    each(5, lambda i: greet(cam=(c + 2 + i) & 7))
    greet(frame=other_core)
    greet(head=1 - hh)

    loads[5].wait()
    off = (offs[1, (c + 7) % 8], offs[0, c])
    sel = [selector(o) for o in off]

    def strip(ref, side):
        window = ref[:, :, side * 32:(side + 1) * 32, :].reshape(256, 512)
        return dot(sel[side], window).astype(BF)

    for i, ref in enumerate((k_in, v_in)):
        loads[i].wait()
        for side in range(2):
            cut = strip(ref, side)
            for h in range(4):
                kv_send[h * 2 + 1 - side, i] = cut[:, h * 128:(h + 1) * 128]

    pl.semaphore_wait(barrier, 30)

    def kv_copy(i):
        unit = (u + i) & 7
        return remote(kv_send.at[unit], kv_recv.at[k, u], kv_ss.at[i], kv_rs.at[u],
                      cam=(c + 9 - 2 * (unit & 1)) & 7, frame=frame_of(unit))

    each(8, lambda i: kv_copy(i).start())

    loads[2].wait()
    for side in range(2):
        cut = strip(q_in, side)
        for h in range(4):
            q_send[h * 2 + side] = cut[:, h * 128:(h + 1) * 128]

    def half_copy(send, recv, ss, rs, i):
        unit = (u + i) & 7
        return remote(send.at[unit], recv.at[u], ss.at[unit], rs.at[u], frame=frame_of(unit))

    def own_copy(send, recv, rs):
        return pltpu.make_async_copy(send.at[u], recv.at[u], rs.at[u])

    own_copy(q_send, q_recv, q_rs).start()
    each(7, lambda i: half_copy(q_send, q_recv, q_ss, q_rs, i + 1).start())
    loads[3].wait()
    g_copy = remote(gfull.at[hh], gfull.at[hh], g_ss, g_rs, head=1 - hh)
    g_copy.start()

    def arrived(ref, sem):
        pltpu.make_async_copy(ref, ref, sem).wait()

    def turn(turned, half, source, i):
        cols = pl.ds(pl.multiple_of(source * 128, 128), 128)
        turned[half, :, cols] = transposed(kv_recv[half, source, i]).astype(BF)

    def hand_copy(source):
        part = kv_recv.at[k, source]
        return remote(part, part, hand_ss.at[source], hand_rs.at[source], frame=other_core)

    def kv_arrive(i):
        source = (u + 8 - i) & 7
        arrived(kv_recv.at[k, source], kv_rs.at[source])
        hand_copy(source).start()
        turn(vt, k, source, 1)

    def kv_handed(i):
        source = (u + 8 - i) & 7
        arrived(kv_recv.at[1 - k, source], hand_rs.at[source])
        turn(vt, 1 - k, source, 1)

    each(8, kv_arrive)
    each(8, kv_handed)

    def stacked(half, i):
        return kv_recv[half, :, i].reshape(1024, 128)

    def send_block(send, recv, ss, rs, unit):
        @pl.when(unit == u)
        def _():
            own_copy(send, recv, rs).start()

        @pl.when(unit != u)
        def _():
            remote(send.at[unit], recv.at[u], ss.at[unit], rs.at[u],
                   frame=frame_of(unit)).start()

    def forward(i):
        b = (x + i) & 3
        for t in range(2):
            arrived(q_recv.at[2 * b + t], q_rs.at[2 * b + t])
        queries = q_recv[pl.ds(2 * b, 2)].reshape(256, 128)
        scores = [dot_nt(stacked(half, 0), queries) for half in range(2)]
        top = jnp.maximum(jnp.max(scores[0], axis=0, keepdims=True),
                          jnp.max(scores[1], axis=0, keepdims=True))
        total, out_t = 0.0, 0.0
        for half in range(2):
            weights = jnp.exp2((scores[half] - top) * (scale * LOG2E))
            total = total + jnp.sum(weights, axis=0, keepdims=True)
            weights = weights.astype(BF)
            probs[half, b] = weights
            out_t = out_t + dot(vt[half], weights)
        inverse = 1.0 / total
        out_t = out_t * inverse
        o_t[b] = out_t
        rl[b] = inverse
        att_send[pl.ds(2 * b, 2)] = out_t.T.astype(BF).reshape(2, 128, 128)
        for t in range(2):
            send_block(att_send, att_recv, att_ss, att_rs, 2 * b + t)

    each(4, forward)

    arrived(gfull.at[1 - hh], g_rs)
    loads[4].wait()
    grad_attn = dot_nt(gfull[0], w[:, :1024]) + dot_nt(gfull[1], w[:, 1024:])
    grad_attn = grad_attn.astype(BF)
    for fr in range(2):
        for s in range(2):
            for h in range(4):
                do_send[h * 2 + s, fr * 64:(fr + 1) * 64] = grad_attn[
                    fr * 128 + s * 64:fr * 128 + s * 64 + 64, h * 128:(h + 1) * 128]
    own_copy(do_send, do_recv, do_rs).start()
    each(7, lambda i: half_copy(do_send, do_recv, do_ss, do_rs, i + 1).start())

    each(16, lambda i: turn(kt, i >> 3, i & 7, 0))

    each(8, lambda i: arrived(att_recv.at[i], att_rs.at[i]))
    for fr in range(2):
        for s in range(2):
            for h in range(4):
                a_rows[fr * 128 + s * 64:fr * 128 + s * 64 + 64, h * 128:(h + 1) * 128] = att_recv[
                    h * 2 + s, fr * 64:(fr + 1) * 64]
    for fr in range(2):
        for h in range(4):
            a_t[h * 128:(h + 1) * 128, fr * 128:(fr + 1) * 128] = transposed(
                a_rows[fr * 128:(fr + 1) * 128, h * 128:(h + 1) * 128]).astype(BF)

    def core_copy(p):
        part = pl.ds(p * 64, 64)
        return remote(core_send.at[part], core_recv.at[part], core_ss.at[p], core_rs.at[p],
                      frame=other_core)

    def multiply():
        theirs = a_t[pl.ds(pl.multiple_of((1 - k) * 256, 256), 256), :]
        for j in range(2):
            core_send[:, j * 1024:(j + 1) * 1024] = dot(theirs, gfull[j]).astype(BF)
        for p in range(4):
            core_copy(p).start()
        mine = a_t[pl.ds(pl.multiple_of(k * 256, 256), 256), :]
        for j in range(2):
            own[:, j * 1024:(j + 1) * 1024] = dot(mine, gfull[j])

    def peers(axis):
        if axis == "x":
            return [((x + i) & 3, dict(frame=frame_x((x + i) & 3))) for i in (1, 3, 2)]
        return [((c + i) & 7, dict(cam=(c + i) & 7)) for i in (1, 7, 2, 6, 3, 5, 4)]

    def area(p, axes, at_x=x, at_z=c, base=0):
        rows, cols = pl.ds(base + p * 64, 64), pl.ds(0, 2048)
        if "x" in axes:
            rows = pl.ds(pl.multiple_of(base + p * 64 + at_x * 16, 16), 16)
        elif not isinstance(base, int):
            rows = pl.ds(pl.multiple_of(base + p * 64, 64), 64)
        if "z" in axes:
            cols = pl.ds(pl.multiple_of(at_z * 256, 256), 256)
        return rows, cols

    def me(axis):
        return x if axis == "x" else c

    def sum_copy(src, dst, p, step, where):
        return remote(src, dst, sum_ss.at[p, step], sum_rs.at[p, step], **where)

    def batch(recv, p, axis):
        return recv[p].at[pl.ds(0, 3 if axis == "x" else 7)]

    def first_sent(p):
        arrived(batch(first_recv, p, PIECES[p][0]), sum_ss.at[p, 0])

    def first(p):
        part = pl.ds(p * 64, 64)
        axis = PIECES[p][0]
        arrived(core_recv.at[part], core_rs.at[p])
        own[part, :] += core_recv[part, :].astype(F32)
        out_bf[part, :] = own[part, :].astype(BF)
        for to, where in peers(axis):
            src = out_bf.at[area(p, axis, to, to)]
            sum_copy(src, first_recv[p].at[me(axis)], p, 0, where).start()

    def second(p):
        axis, other = PIECES[p]
        arrived(batch(first_recv, p, axis), sum_rs.at[p, 0])
        total = own[area(p, axis)]
        for frm, _ in peers(axis):
            total = total + first_recv[p][frm].astype(F32)
        mid_sum[p][...] = total.astype(BF)
        for to, where in peers(other):
            sum_copy(mid_sum[p].at[mid_part(p, to)], second_recv[p].at[me(other)], p, 1, where).start()

    def mid_part(p, to):
        if PIECES[p][1] == "x":
            return pl.ds(pl.multiple_of(to * 16, 16), 16), pl.ds(0, 256)
        return pl.ds(0, 16), pl.ds(pl.multiple_of(to * 256, 256), 256)

    def y_copy(p):
        return sum_copy(y_send.at[p], y_recv.at[p], p, 2, dict(frame=other_half))

    def third(p):
        axis = PIECES[p][1]
        arrived(batch(second_recv, p, axis), sum_rs.at[p, 1])
        total = mid_sum[p][mid_part(p, me(axis))].astype(F32)
        for frm, _ in peers(axis):
            total = total + second_recv[p][frm].astype(F32)
        y_send[p] = total.astype(BF)
        y_copy(p).start()

    def gather(p, axes, axis, step):
        part = gw.at[area(p, axes, base=k * 256)]
        for _, where in peers(axis):
            sum_copy(part, part, p, step, where).start()

    def fourth(p):
        arrived(y_recv.at[p], sum_rs.at[p, 2])
        gw[area(p, "xz", base=k * 256)] = (
            y_send[p].astype(F32) + y_recv[p].astype(F32)).astype(BF)
        gather(p, "xz", PIECES[p][1], 3)

    def fifth(p):
        arrived(batch(second_recv, p, PIECES[p][1]), sum_rs.at[p, 3])
        gather(p, PIECES[p][0], PIECES[p][0], 4)

    def sixth(p):
        arrived(batch(first_recv, p, PIECES[p][0]), sum_rs.at[p, 4])
        part = gw.at[area(p, "", base=k * 256)]
        sum_copy(part, part, p, 5, dict(frame=other_core)).start()
        gw_write(p, k).start()

    def seventh(p):
        arrived(gw.at[area(p, "", base=(1 - k) * 256)], sum_rs.at[p, 5])
        gw_write(p, 1 - k).start()

    def gw_write(p, core):
        at = area(p, "", base=core * 256)
        return pltpu.make_async_copy(gw.at[at], gw_hbm.at[at], out_sem.at[3 + p * 2 + core])

    def backward(half, i):
        b = (x + i) & 3
        if half is far:
            for t in range(2):
                arrived(do_recv.at[2 * b + t], do_rs.at[2 * b + t])
        queries = q_recv[pl.ds(2 * b, 2)].reshape(256, 128)
        weights = probs[half, b]
        grad_t = transposed(do_recv[pl.ds(2 * b, 2)].reshape(256, 128)) * rl[b]
        delta = jnp.sum(grad_t * o_t[b], axis=0, keepdims=True)
        grads = grad_t.T.astype(BF)
        grad_probs = dot(stacked(half, 1), grad_t.astype(BF))
        grad_scores = (weights.astype(F32) * (grad_probs - delta)).astype(BF)
        grad_q_t = dot(kt[half], grad_scores)
        if half is far:
            dq_acc[b] = grad_q_t
        else:
            grad_q_t = (grad_q_t + dq_acc[b]) * scale
            dq_send[pl.ds(2 * b, 2)] = grad_q_t.T.astype(BF).reshape(2, 128, 128)
            for t in range(2):
                send_block(dq_send, dq_recv, dq_ss, dq_rs, 2 * b + t)
        if i == 0:
            dk_acc[...] = dot(grad_scores, queries)
            dv_acc[...] = dot(weights, grads)
        else:
            dk_acc[...] += dot(grad_scores, queries)
            dv_acc[...] += dot(weights, grads)

    def far_copy():
        return remote(far_send, far_recv, far_ss, far_rs, frame=other_core)

    def dkv_copy(i):
        source = (u + i) & 7
        return remote(dkv_send.at[source], dkv_recv.at[u], dkv_ss.at[i], dkv_rs.at[u],
                      cam=(c + 7 + 2 * yh) & 7, frame=frame_of(source))

    far, near = 1 - k, k

    multiply()
    first(0)
    first(1)
    for i in range(4):
        backward(far, i)
    far_send[:, 0] = dk_acc[...].astype(BF).reshape(8, 128, 128)
    far_send[:, 1] = dv_acc[...].astype(BF).reshape(8, 128, 128)
    far_copy().start()
    first_sent(0)
    first(2)
    backward(near, 0)
    second(0)
    backward(near, 1)
    first_sent(2)
    first(3)
    backward(near, 2)
    second(1)
    backward(near, 3)
    far_copy().wait()
    for i, acc in enumerate((dk_acc, dv_acc)):
        total = acc[...].reshape(8, 128, 128) + far_recv[:, i].astype(F32)
        if i == 0:
            total = total * scale
        dkv_send[:, i] = total.astype(BF)
    each(8, lambda i: dkv_copy(i).start())
    second(2)
    third(0)
    second(3)
    third(1)
    third(2)
    fourth(0)
    third(3)
    fourth(1)
    fourth(2)
    fourth(3)
    lo_send[...] = dot(
        a_rows[...], w[:, pl.ds(pl.multiple_of((1 - hh) * 1024, 1024), 1024)]).astype(BF)
    lo_copy = remote(lo_send, lo_recv, lo_ss, lo_rs, head=1 - hh)
    lo_copy.start()
    fifth(0)
    fifth(1)
    fifth(2)
    fifth(3)

    lo_done[...] = dot(
        a_rows[...], w[:, pl.ds(pl.multiple_of(hh * 1024, 1024), 1024)])
    each(8, lambda i: arrived(dq_recv.at[i], dq_rs.at[i]))
    dq_write = pltpu.make_async_copy(dq_recv, dq_hbm, out_sem.at[1])
    dq_write.start()
    each(8, lambda i: arrived(dkv_recv.at[i], dkv_rs.at[i]))
    dkv_write = pltpu.make_async_copy(dkv_recv, dkv_hbm, out_sem.at[2])
    dkv_write.start()
    g_copy.wait_send()
    each(8, lambda i: kv_copy(i).wait_send())
    each(8, lambda i: hand_copy(i).wait_send())

    def sent(send, recv, ss, rs):
        each(7, lambda i: half_copy(send, recv, ss, rs, i + 1).wait_send())

    sent(q_send, q_recv, q_ss, q_rs)
    sent(do_send, do_recv, do_ss, do_rs)
    sent(att_send, att_recv, att_ss, att_rs)
    sent(dq_send, dq_recv, dq_ss, dq_rs)
    each(8, lambda i: dkv_copy(i).wait_send())
    first_sent(1)
    first_sent(3)
    for p in range(4):
        core_copy(p).wait_send()
        arrived(batch(second_recv, p, PIECES[p][1]), sum_ss.at[p, 1])
        y_copy(p).wait_send()
        arrived(batch(second_recv, p, PIECES[p][1]), sum_ss.at[p, 3])
    sixth(0)
    sixth(1)
    sixth(2)
    sixth(3)
    lo_copy.wait()
    lo_send[...] = (lo_done[...] + lo_recv[...].astype(F32)).astype(BF)
    lo_write = pltpu.make_async_copy(lo_send, lo_hbm, out_sem.at[0])
    lo_write.start()
    for p in range(4):
        seventh(p)

    for p in range(4):
        arrived(batch(first_recv, p, PIECES[p][0]), sum_ss.at[p, 4])
        arrived(gw.at[area(p, "", base=k * 256)], sum_ss.at[p, 5])
        gw_write(p, k).wait()
        gw_write(p, 1 - k).wait()
    lo_write.wait()
    dq_write.wait()
    dkv_write.wait()


def place_kernel(
    offs_hbm, lo_hbm, dq_hbm, dkv_hbm, gw_hbm, layer_hbm, gq_hbm, gk_hbm, gv_hbm, gwo_hbm,
    offs, dq, dkv, gw, lo, grid, rows, in_sem, out_sem,
):
    c = lax.axis_index("cam")
    loads = [pltpu.make_async_copy(offs_hbm, offs, in_sem.at[0]),
             pltpu.make_async_copy(dq_hbm, dq, in_sem.at[1]),
             pltpu.make_async_copy(dkv_hbm, dkv, in_sem.at[2]),
             pltpu.make_async_copy(lo_hbm, lo, in_sem.at[3])]
    part = [pl.ds(r * 128, 128) for r in range(4)]
    loads += [pltpu.make_async_copy(gw_hbm.at[part[r]], gw.at[part[r]], in_sem.at[4 + r])
              for r in range(4)]
    for load in loads:
        load.start()
    loads[0].wait()
    off = (offs[1, (c + 7) % 8], offs[0, c])
    sel = [selector_t(o) for o in off]
    writes = []

    def write(src, dst):
        writes.append(pltpu.make_async_copy(src, dst, out_sem.at[len(writes)]))
        writes[-1].start()

    for n, out in enumerate((gq_hbm, gk_hbm, gv_hbm)):
        if n < 2:
            loads[1 + n].wait()
        for side in range(2):
            for h in range(4):
                unit = h * 2 + (side if n == 0 else 1 - side)
                if n == 0:
                    placed = dot(sel[side], dq[unit])
                else:
                    placed = dot(sel[side], dkv[unit, n - 1])
                grid[n, :, :, side * 32:(side + 1) * 32, h * 128:(h + 1) * 128] = placed.reshape(
                    2, 4, 32, 128)
        write(grid.at[n], out)
    loads[3].wait()
    write(lo, layer_hbm)
    for r in range(4):
        loads[4 + r].wait()
        rows[part[r], :] = gw[part[r], :].astype(F32)
        write(rows.at[part[r]], gwo_hbm.at[part[r]])
    for copy in writes:
        copy.wait()


def on_device(queries, keys, values, offsets, w_out, grad_out):
    field = queries.shape[1:]
    dma = pltpu.SemaphoreType.DMA
    any_spec = pl.BlockSpec(memory_space=pl.ANY)
    tile = (128, 128)

    def buf(*shape):
        return pltpu.VMEM(shape, BF)

    mid = [
        jax.ShapeDtypeStruct((256, 1024), BF),
        jax.ShapeDtypeStruct((8,) + tile, BF),
        jax.ShapeDtypeStruct((8, 2) + tile, BF),
        jax.ShapeDtypeStruct((512, 2048), BF),
    ]
    offs = offsets.T
    parts = pl.pallas_call(
        main_kernel,
        out_shape=mid,
        in_specs=[any_spec] * 6,
        out_specs=[any_spec] * 4,
        scratch_shapes=[
            pltpu.SMEM((2, 8), jnp.int32),
            buf(*field), buf(*field), buf(*field), buf(512, 2048), buf(2, 256, 1024),
            buf(8, *tile), buf(8, 2, *tile), buf(8, *tile),
            buf(8, *tile), buf(2, 8, 2, *tile), buf(8, *tile),
            buf(2, 128, 1024), buf(2, 128, 1024), buf(2, 4, 1024, 256),
            pltpu.VMEM((4, 128, 256), F32), pltpu.VMEM((4, 1, 256), F32),
            buf(8, *tile), buf(8, *tile), pltpu.VMEM((4, 128, 256), F32), buf(8, *tile), buf(8, *tile),
            pltpu.VMEM((1024, 128), F32), pltpu.VMEM((1024, 128), F32),
            buf(8, 2, *tile), buf(8, 2, *tile), buf(8, 2, *tile), buf(8, 2, *tile),
            buf(256, 512), buf(512, 256), buf(256, 2048), buf(256, 2048),
            pltpu.VMEM((256, 2048), F32), buf(256, 1024), buf(256, 1024), pltpu.VMEM((256, 1024), F32),
            buf(256, 2048), buf(512, 2048),
            [buf(4, 16, 2048) if axes == "xz" else buf(8, 64, 256) for axes in PIECES],
            [buf(16, 2048) if axes == "xz" else buf(64, 256) for axes in PIECES],
            [buf(8, 16, 256) if axes == "xz" else buf(4, 16, 256) for axes in PIECES],
            buf(4, 16, 256), buf(4, 16, 256),
            dma((6,)), dma((11,)), dma, dma, dma((8,)), dma((8,)), dma((8,)), dma((8,)),
            dma((8,)), dma((8,)),
            dma((8,)), dma((8,)),
            dma((8,)), dma((8,)), dma((8,)), dma((8,)), dma, dma, dma((8,)), dma((8,)),
            dma((4,)), dma((4,)), dma, dma,
            dma((4, 6)), dma((4, 6)),
        ],
        compiler_params=pltpu.CompilerParams(
            collective_id=0, has_side_effects=True, vmem_limit_bytes=56 * 1024 * 1024),
        cost_estimate=pl.CostEstimate(
            flops=5 * 10**9, bytes_accessed=10 * 2**20, transcendentals=2 * 2**20),
        name="strip_attention",
    )(offs, queries.reshape(field), keys.reshape(field), values.reshape(field), w_out,
      grad_out.reshape(256, 1024))

    grid = jax.ShapeDtypeStruct(field, F32)
    layer, gq, gk, gv, gwo = pl.pallas_call(
        place_kernel,
        out_shape=(mid[0], grid, grid, grid, jax.ShapeDtypeStruct((512, 2048), F32)),
        in_specs=[any_spec] * 5,
        out_specs=(any_spec,) * 5,
        scratch_shapes=[
            pltpu.SMEM((2, 8), jnp.int32), buf(8, *tile), buf(8, 2, *tile), buf(512, 2048),
            buf(256, 1024), pltpu.VMEM((3,) + field, F32), pltpu.VMEM((512, 2048), F32),
            dma((8,)), dma((8,))],
        compiler_params=pltpu.CompilerParams(vmem_limit_bytes=60 * 1024 * 1024),
        cost_estimate=pl.CostEstimate(
            flops=10**8, bytes_accessed=10 * 2**20, transcendentals=0),
        name="place_gradients",
    )(offs, *parts)
    shape = queries.shape
    return (layer.reshape(grad_out.shape), gq.reshape(shape), gk.reshape(shape), gv.reshape(shape),
            gwo)


def solution(mesh):
    field = P("cam", "frame", None, None, "head")
    rows = P("cam", "frame", None, None, None, "head")
    return jax.shard_map(
        on_device,
        mesh=mesh,
        in_specs=(field, field, field, P(), P("head", None), rows),
        out_specs=(rows, field, field, field, P("head", None)),
        check_vma=False,
    )
```

```python
import functools

import jax
import jax.numpy as jnp
from jax import lax
from jax.experimental import pallas as pl
from jax.experimental.pallas import tpu as pltpu
from jax.sharding import PartitionSpec as P

HD = 128
BF = jnp.bfloat16
F32 = jnp.float32
MESH = pl.DeviceIdType.MESH
LOG2E = 1.4426950408889634
NT = (((1,), (1,)), ((), ()))
PIECES = ("xz", "zx", "xz", "xz")


def dot(a, b):
    return jnp.dot(a, b, preferred_element_type=F32)


def dot_nt(a, b):
    return lax.dot_general(a, b, NT, preferred_element_type=F32)


def each(count, fn):
    def step(i, carry):
        fn(i)
        return carry

    lax.fori_loop(0, count, step, 0)


def transposed(block):
    return block.astype(F32).T


def selector(off):
    rows = lax.broadcasted_iota(jnp.int32, (128, 256), 0)
    cols = lax.broadcasted_iota(jnp.int32, (128, 256), 1)
    hit = cols == rows + (lax.shift_right_logical(rows, 4) * 16 + off)
    return jnp.where(hit, 1.0, 0.0).astype(BF)


def selector_t(off):
    rows = lax.broadcasted_iota(jnp.int32, (256, 128), 1)
    cols = lax.broadcasted_iota(jnp.int32, (256, 128), 0)
    hit = cols == rows + (lax.shift_right_logical(rows, 4) * 16 + off)
    return jnp.where(hit, 1.0, 0.0).astype(BF)


def main_kernel(
    offs_hbm, q_hbm, k_hbm, v_hbm, w_hbm, g_hbm,
    lo_hbm, dq_hbm, dkv_hbm, gw_hbm,
    offs, q_in, k_in, v_in, w, gfull,
    q_send, kv_send, do_send, q_recv, kv_recv, do_recv,
    kt, vt, probs, o_t, rl,
    att_send, att_recv, dq_acc, dq_send, dq_recv, dk_acc, dv_acc, far_send, far_recv, dkv_send, dkv_recv,
    a_rows, a_t, core_send, core_recv, own, lo_send, lo_recv, lo_done,
    out_bf, gw, first_recv, mid_sum, second_recv, y_send, y_recv,
    in_sem, out_sem, g_ss, g_rs, q_ss, q_rs, kv_ss, kv_rs, hand_ss, hand_rs, do_ss, do_rs,
    att_ss, att_rs, dq_ss, dq_rs, far_ss, far_rs, dkv_ss, dkv_rs, core_ss, core_rs, lo_ss, lo_rs,
    sum_ss, sum_rs,
):
    c = lax.axis_index("cam")
    f = lax.axis_index("frame")
    hh = lax.axis_index("head")
    x, yh, k = f >> 2, (f >> 1) & 1, f & 1
    u = x * 2 + yh
    scale = HD ** (-0.5)

    def frame_of(unit):
        return unit * 2 + k

    def frame_x(to_x):
        return to_x * 4 + yh * 2 + k

    def device(cam=c, frame=f, head=hh):
        return (cam, frame, head)

    def remote(src, dst, ss, rs, **where):
        return pltpu.make_async_remote_copy(
            src_ref=src, dst_ref=dst, send_sem=ss, recv_sem=rs,
            device_id=device(**where), device_id_type=MESH)

    other_core = x * 4 + yh * 2 + 1 - k
    other_half = x * 4 + (1 - yh) * 2 + k

    barrier = pltpu.get_barrier_semaphore()

    def greet(**where):
        pl.semaphore_signal(barrier, inc=1, device_id=device(**where), device_id_type=MESH)

    def greet_cams(i):
        greet(cam=(c + 1) & 7, frame=frame_of(i))
        greet(cam=(c + 7) & 7, frame=frame_of(i))

    loads = [
        pltpu.make_async_copy(src, dst, in_sem.at[i])
        for i, (src, dst) in enumerate(
            ((k_hbm, k_in), (v_hbm, v_in), (q_hbm, q_in), (g_hbm, gfull.at[hh]), (w_hbm, w),
             (offs_hbm, offs)))
    ]
    for load in loads:
        load.start()
    each(8, greet_cams)
    each(7, lambda i: greet(frame=frame_of((u + 1 + i) & 7)))
    each(5, lambda i: greet(cam=(c + 2 + i) & 7))
    greet(frame=other_core)
    greet(head=1 - hh)

    loads[5].wait()
    off = (offs[1, (c + 7) % 8], offs[0, c])
    sel = [selector(o) for o in off]

    def strip(ref, side):
        window = ref[:, :, side * 32:(side + 1) * 32, :].reshape(256, 512)
        return dot(sel[side], window).astype(BF)

    for i, ref in enumerate((k_in, v_in)):
        loads[i].wait()
        for side in range(2):
            cut = strip(ref, side)
            for h in range(4):
                kv_send[h * 2 + 1 - side, i] = cut[:, h * 128:(h + 1) * 128]

    pl.semaphore_wait(barrier, 30)

    def kv_copy(i):
        unit = (u + i) & 7
        return remote(kv_send.at[unit], kv_recv.at[k, u], kv_ss.at[i], kv_rs.at[u],
                      cam=(c + 9 - 2 * (unit & 1)) & 7, frame=frame_of(unit))

    each(8, lambda i: kv_copy(i).start())
    loads[3].wait()
    g_copy = remote(gfull.at[hh], gfull.at[hh], g_ss, g_rs, head=1 - hh)
    g_copy.start()

    loads[2].wait()
    for side in range(2):
        cut = strip(q_in, side)
        for h in range(4):
            q_send[h * 2 + side] = cut[:, h * 128:(h + 1) * 128]

    def half_copy(send, recv, ss, rs, i):
        unit = (u + i) & 7
        return remote(send.at[unit], recv.at[u], ss.at[unit], rs.at[u], frame=frame_of(unit))

    def own_copy(send, recv, rs):
        return pltpu.make_async_copy(send.at[u], recv.at[u], rs.at[u])

    own_copy(q_send, q_recv, q_rs).start()
    each(7, lambda i: half_copy(q_send, q_recv, q_ss, q_rs, i + 1).start())

    def arrived(ref, sem):
        pltpu.make_async_copy(ref, ref, sem).wait()

    def turn(turned, half, source, i):
        cols = pl.ds(pl.multiple_of(source * 128, 128), 128)
        turned[half, :, cols] = transposed(kv_recv[half, source, i]).astype(BF)

    def hand_copy(source):
        part = kv_recv.at[k, source]
        return remote(part, part, hand_ss.at[source], hand_rs.at[source], frame=other_core)

    def kv_arrive(i):
        source = (u + 8 - i) & 7
        arrived(kv_recv.at[k, source], kv_rs.at[source])
        hand_copy(source).start()
        turn(vt, k, source, 1)

    def kv_handed(i):
        source = (u + 8 - i) & 7
        arrived(kv_recv.at[1 - k, source], hand_rs.at[source])
        turn(vt, 1 - k, source, 1)

    each(8, kv_arrive)
    each(8, kv_handed)

    def stacked(half, i):
        return kv_recv[half, :, i].reshape(1024, 128)

    def send_block(send, recv, ss, rs, unit):
        @pl.when(unit == u)
        def _():
            own_copy(send, recv, rs).start()

        @pl.when(unit != u)
        def _():
            remote(send.at[unit], recv.at[u], ss.at[unit], rs.at[u],
                   frame=frame_of(unit)).start()

    def forward(i):
        b = (x + i) & 3
        for t in range(2):
            arrived(q_recv.at[2 * b + t], q_rs.at[2 * b + t])
        queries = q_recv[pl.ds(2 * b, 2)].reshape(256, 128)
        scores = [dot_nt(stacked(half, 0), queries) for half in range(2)]
        top = jnp.maximum(jnp.max(scores[0], axis=0, keepdims=True),
                          jnp.max(scores[1], axis=0, keepdims=True))
        total, out_t = 0.0, 0.0
        for half in range(2):
            weights = jnp.exp2((scores[half] - top) * (scale * LOG2E))
            total = total + jnp.sum(weights, axis=0, keepdims=True)
            weights = weights.astype(BF)
            probs[half, b] = weights
            out_t = out_t + dot(vt[half], weights)
        inverse = 1.0 / total
        out_t = out_t * inverse
        o_t[b] = out_t
        rl[b] = inverse
        att_send[pl.ds(2 * b, 2)] = out_t.T.astype(BF).reshape(2, 128, 128)
        for t in range(2):
            send_block(att_send, att_recv, att_ss, att_rs, 2 * b + t)

    each(4, forward)

    each(16, lambda i: turn(kt, i >> 3, i & 7, 0))

    each(8, lambda i: arrived(att_recv.at[i], att_rs.at[i]))
    for fr in range(2):
        for s in range(2):
            for h in range(4):
                a_rows[fr * 128 + s * 64:fr * 128 + s * 64 + 64, h * 128:(h + 1) * 128] = att_recv[
                    h * 2 + s, fr * 64:(fr + 1) * 64]
    for fr in range(2):
        for h in range(4):
            a_t[h * 128:(h + 1) * 128, fr * 128:(fr + 1) * 128] = transposed(
                a_rows[fr * 128:(fr + 1) * 128, h * 128:(h + 1) * 128]).astype(BF)

    def core_copy(p):
        part = pl.ds(p * 64, 64)
        return remote(core_send.at[part], core_recv.at[part], core_ss.at[p], core_rs.at[p],
                      frame=other_core)

    columns = [pl.ds(pl.multiple_of(i * 1024, 1024), 1024) for i in (hh, 1 - hh)]

    def multiply(i):
        theirs = a_t[pl.ds(pl.multiple_of((1 - k) * 256, 256), 256), :]
        mine = a_t[pl.ds(pl.multiple_of(k * 256, 256), 256), :]
        features = gfull[hh if i == 0 else 1 - hh]
        core_send[:, columns[i]] = dot(theirs, features).astype(BF)
        if i == 1:
            for p in range(4):
                core_copy(p).start()
        own[:, columns[i]] = dot(mine, features)

    def cotangent():
        grad_attn = lo_done[:, :512] + dot_nt(gfull[1 - hh], w[:, columns[1]])
        grad_attn = grad_attn.astype(BF)
        for fr in range(2):
            for s in range(2):
                for h in range(4):
                    do_send[h * 2 + s, fr * 64:(fr + 1) * 64] = grad_attn[
                        fr * 128 + s * 64:fr * 128 + s * 64 + 64, h * 128:(h + 1) * 128]
        own_copy(do_send, do_recv, do_rs).start()
        each(7, lambda i: half_copy(do_send, do_recv, do_ss, do_rs, i + 1).start())

    def peers(axis):
        if axis == "x":
            return [((x + i) & 3, dict(frame=frame_x((x + i) & 3))) for i in (1, 3, 2)]
        return [((c + i) & 7, dict(cam=(c + i) & 7)) for i in (1, 7, 2, 6, 3, 5, 4)]

    def area(p, axes, at_x=x, at_z=c, base=0):
        rows, cols = pl.ds(base + p * 64, 64), pl.ds(0, 2048)
        if "x" in axes:
            rows = pl.ds(pl.multiple_of(base + p * 64 + at_x * 16, 16), 16)
        elif not isinstance(base, int):
            rows = pl.ds(pl.multiple_of(base + p * 64, 64), 64)
        if "z" in axes:
            cols = pl.ds(pl.multiple_of(at_z * 256, 256), 256)
        return rows, cols

    def me(axis):
        return x if axis == "x" else c

    def sum_copy(src, dst, p, step, where):
        return remote(src, dst, sum_ss.at[p, step], sum_rs.at[p, step], **where)

    def batch(recv, p, axis):
        return recv[p].at[pl.ds(0, 3 if axis == "x" else 7)]

    def first_sent(p):
        arrived(batch(first_recv, p, PIECES[p][0]), sum_ss.at[p, 0])

    def first(p):
        part = pl.ds(p * 64, 64)
        axis = PIECES[p][0]
        arrived(core_recv.at[part], core_rs.at[p])
        own[part, :] += core_recv[part, :].astype(F32)
        out_bf[part, :] = own[part, :].astype(BF)
        for to, where in peers(axis):
            src = out_bf.at[area(p, axis, to, to)]
            sum_copy(src, first_recv[p].at[me(axis)], p, 0, where).start()

    def second(p):
        axis, other = PIECES[p]
        arrived(batch(first_recv, p, axis), sum_rs.at[p, 0])
        total = own[area(p, axis)]
        for frm, _ in peers(axis):
            total = total + first_recv[p][frm].astype(F32)
        mid_sum[p][...] = total.astype(BF)
        for to, where in peers(other):
            sum_copy(mid_sum[p].at[mid_part(p, to)], second_recv[p].at[me(other)], p, 1, where).start()

    def mid_part(p, to):
        if PIECES[p][1] == "x":
            return pl.ds(pl.multiple_of(to * 16, 16), 16), pl.ds(0, 256)
        return pl.ds(0, 16), pl.ds(pl.multiple_of(to * 256, 256), 256)

    def y_copy(p):
        return sum_copy(y_send.at[p], y_recv.at[p], p, 2, dict(frame=other_half))

    def third(p):
        axis = PIECES[p][1]
        arrived(batch(second_recv, p, axis), sum_rs.at[p, 1])
        total = mid_sum[p][mid_part(p, me(axis))].astype(F32)
        for frm, _ in peers(axis):
            total = total + second_recv[p][frm].astype(F32)
        y_send[p] = total.astype(BF)
        y_copy(p).start()

    def gather(p, axes, axis, step):
        part = gw.at[area(p, axes, base=k * 256)]
        for _, where in peers(axis):
            sum_copy(part, part, p, step, where).start()

    def fourth(p):
        arrived(y_recv.at[p], sum_rs.at[p, 2])
        gw[area(p, "xz", base=k * 256)] = (
            y_send[p].astype(F32) + y_recv[p].astype(F32)).astype(BF)
        gather(p, "xz", PIECES[p][1], 3)

    def fifth(p):
        arrived(batch(second_recv, p, PIECES[p][1]), sum_rs.at[p, 3])
        gather(p, PIECES[p][0], PIECES[p][0], 4)

    def sixth(p):
        arrived(batch(first_recv, p, PIECES[p][0]), sum_rs.at[p, 4])
        part = gw.at[area(p, "", base=k * 256)]
        sum_copy(part, part, p, 5, dict(frame=other_core)).start()
        gw_write(p, k).start()

    def seventh(p):
        arrived(gw.at[area(p, "", base=(1 - k) * 256)], sum_rs.at[p, 5])
        gw_write(p, 1 - k).start()

    def gw_write(p, core):
        at = area(p, "", base=core * 256)
        return pltpu.make_async_copy(gw.at[at], gw_hbm.at[at], out_sem.at[3 + p * 2 + core])

    def backward(half, i):
        b = (x + i) & 3
        if half is far:
            for t in range(2):
                arrived(do_recv.at[2 * b + t], do_rs.at[2 * b + t])
        queries = q_recv[pl.ds(2 * b, 2)].reshape(256, 128)
        weights = probs[half, b]
        grad_t = transposed(do_recv[pl.ds(2 * b, 2)].reshape(256, 128)) * rl[b]
        delta = jnp.sum(grad_t * o_t[b], axis=0, keepdims=True)
        grads = grad_t.T.astype(BF)
        grad_probs = dot(stacked(half, 1), grad_t.astype(BF))
        grad_scores = (weights.astype(F32) * (grad_probs - delta)).astype(BF)
        grad_q_t = dot(kt[half], grad_scores)
        if half is far:
            dq_acc[b] = grad_q_t
        else:
            grad_q_t = (grad_q_t + dq_acc[b]) * scale
            dq_send[pl.ds(2 * b, 2)] = grad_q_t.T.astype(BF).reshape(2, 128, 128)
            for t in range(2):
                send_block(dq_send, dq_recv, dq_ss, dq_rs, 2 * b + t)
        if i == 0:
            dk_acc[...] = dot(grad_scores, queries)
            dv_acc[...] = dot(weights, grads)
        else:
            dk_acc[...] += dot(grad_scores, queries)
            dv_acc[...] += dot(weights, grads)

    def far_copy():
        return remote(far_send, far_recv, far_ss, far_rs, frame=other_core)

    def dkv_copy(i):
        source = (u + i) & 7
        return remote(dkv_send.at[source], dkv_recv.at[u], dkv_ss.at[i], dkv_rs.at[u],
                      cam=(c + 7 + 2 * yh) & 7, frame=frame_of(source))

    far, near = 1 - k, k

    loads[4].wait()
    lo_done[:, :512] = dot_nt(gfull[hh], w[:, columns[0]])
    multiply(0)
    arrived(gfull.at[1 - hh], g_rs)
    multiply(1)
    cotangent()
    first(0)
    first(1)
    for i in range(4):
        backward(far, i)
    far_send[:, 0] = dk_acc[...].astype(BF).reshape(8, 128, 128)
    far_send[:, 1] = dv_acc[...].astype(BF).reshape(8, 128, 128)
    far_copy().start()
    first_sent(0)
    first(2)
    backward(near, 0)
    second(0)
    backward(near, 1)
    first_sent(2)
    first(3)
    backward(near, 2)
    second(1)
    backward(near, 3)
    far_copy().wait()
    for i, acc in enumerate((dk_acc, dv_acc)):
        total = acc[...].reshape(8, 128, 128) + far_recv[:, i].astype(F32)
        if i == 0:
            total = total * scale
        dkv_send[:, i] = total.astype(BF)
    each(8, lambda i: dkv_copy(i).start())
    second(2)
    third(0)
    second(3)
    third(1)
    third(2)
    fourth(0)
    third(3)
    fourth(1)
    fourth(2)
    fourth(3)
    lo_send[...] = dot(
        a_rows[...], w[:, pl.ds(pl.multiple_of((1 - hh) * 1024, 1024), 1024)]).astype(BF)
    lo_copy = remote(lo_send, lo_recv, lo_ss, lo_rs, head=1 - hh)
    lo_copy.start()
    fifth(0)
    fifth(1)
    fifth(2)
    fifth(3)

    lo_done[...] = dot(
        a_rows[...], w[:, pl.ds(pl.multiple_of(hh * 1024, 1024), 1024)])
    each(8, lambda i: arrived(dq_recv.at[i], dq_rs.at[i]))
    dq_write = pltpu.make_async_copy(dq_recv, dq_hbm, out_sem.at[1])
    dq_write.start()
    each(8, lambda i: arrived(dkv_recv.at[i], dkv_rs.at[i]))
    dkv_write = pltpu.make_async_copy(dkv_recv, dkv_hbm, out_sem.at[2])
    dkv_write.start()
    g_copy.wait_send()
    each(8, lambda i: kv_copy(i).wait_send())
    each(8, lambda i: hand_copy(i).wait_send())

    def sent(send, recv, ss, rs):
        each(7, lambda i: half_copy(send, recv, ss, rs, i + 1).wait_send())

    sent(q_send, q_recv, q_ss, q_rs)
    sent(do_send, do_recv, do_ss, do_rs)
    sent(att_send, att_recv, att_ss, att_rs)
    sent(dq_send, dq_recv, dq_ss, dq_rs)
    each(8, lambda i: dkv_copy(i).wait_send())
    first_sent(1)
    first_sent(3)
    for p in range(4):
        core_copy(p).wait_send()
        arrived(batch(second_recv, p, PIECES[p][1]), sum_ss.at[p, 1])
        y_copy(p).wait_send()
        arrived(batch(second_recv, p, PIECES[p][1]), sum_ss.at[p, 3])
    sixth(0)
    sixth(1)
    sixth(2)
    sixth(3)
    lo_copy.wait()
    lo_send[...] = (lo_done[...] + lo_recv[...].astype(F32)).astype(BF)
    lo_write = pltpu.make_async_copy(lo_send, lo_hbm, out_sem.at[0])
    lo_write.start()
    for p in range(4):
        seventh(p)

    for p in range(4):
        arrived(batch(first_recv, p, PIECES[p][0]), sum_ss.at[p, 4])
        arrived(gw.at[area(p, "", base=k * 256)], sum_ss.at[p, 5])
        gw_write(p, k).wait()
        gw_write(p, 1 - k).wait()
    lo_write.wait()
    dq_write.wait()
    dkv_write.wait()


def place_kernel(
    offs_hbm, lo_hbm, dq_hbm, dkv_hbm, gw_hbm, layer_hbm, gq_hbm, gk_hbm, gv_hbm, gwo_hbm,
    offs, dq, dkv, gw, lo, grid, rows, in_sem, out_sem,
):
    c = lax.axis_index("cam")
    loads = [pltpu.make_async_copy(offs_hbm, offs, in_sem.at[0]),
             pltpu.make_async_copy(dq_hbm, dq, in_sem.at[1]),
             pltpu.make_async_copy(dkv_hbm, dkv, in_sem.at[2]),
             pltpu.make_async_copy(lo_hbm, lo, in_sem.at[3])]
    part = [pl.ds(r * 128, 128) for r in range(4)]
    loads += [pltpu.make_async_copy(gw_hbm.at[part[r]], gw.at[part[r]], in_sem.at[4 + r])
              for r in range(4)]
    for load in loads:
        load.start()
    loads[0].wait()
    off = (offs[1, (c + 7) % 8], offs[0, c])
    sel = [selector_t(o) for o in off]
    writes = []

    def write(src, dst):
        writes.append(pltpu.make_async_copy(src, dst, out_sem.at[len(writes)]))
        writes[-1].start()

    for n, out in enumerate((gq_hbm, gk_hbm, gv_hbm)):
        if n < 2:
            loads[1 + n].wait()
        for side in range(2):
            for h in range(4):
                unit = h * 2 + (side if n == 0 else 1 - side)
                if n == 0:
                    placed = dot(sel[side], dq[unit])
                else:
                    placed = dot(sel[side], dkv[unit, n - 1])
                grid[n, :, :, side * 32:(side + 1) * 32, h * 128:(h + 1) * 128] = placed.reshape(
                    2, 4, 32, 128)
        write(grid.at[n], out)
    loads[3].wait()
    write(lo, layer_hbm)
    for r in range(4):
        loads[4 + r].wait()
        rows[part[r], :] = gw[part[r], :].astype(F32)
        write(rows.at[part[r]], gwo_hbm.at[part[r]])
    for copy in writes:
        copy.wait()


def on_device(queries, keys, values, offsets, w_out, grad_out):
    field = queries.shape[1:]
    dma = pltpu.SemaphoreType.DMA
    any_spec = pl.BlockSpec(memory_space=pl.ANY)
    tile = (128, 128)

    def buf(*shape):
        return pltpu.VMEM(shape, BF)

    mid = [
        jax.ShapeDtypeStruct((256, 1024), BF),
        jax.ShapeDtypeStruct((8,) + tile, BF),
        jax.ShapeDtypeStruct((8, 2) + tile, BF),
        jax.ShapeDtypeStruct((512, 2048), BF),
    ]
    offs = offsets.T
    parts = pl.pallas_call(
        main_kernel,
        out_shape=mid,
        in_specs=[any_spec] * 6,
        out_specs=[any_spec] * 4,
        scratch_shapes=[
            pltpu.SMEM((2, 8), jnp.int32),
            buf(*field), buf(*field), buf(*field), buf(512, 2048), buf(2, 256, 1024),
            buf(8, *tile), buf(8, 2, *tile), buf(8, *tile),
            buf(8, *tile), buf(2, 8, 2, *tile), buf(8, *tile),
            buf(2, 128, 1024), buf(2, 128, 1024), buf(2, 4, 1024, 256),
            pltpu.VMEM((4, 128, 256), F32), pltpu.VMEM((4, 1, 256), F32),
            buf(8, *tile), buf(8, *tile), pltpu.VMEM((4, 128, 256), F32), buf(8, *tile), buf(8, *tile),
            pltpu.VMEM((1024, 128), F32), pltpu.VMEM((1024, 128), F32),
            buf(8, 2, *tile), buf(8, 2, *tile), buf(8, 2, *tile), buf(8, 2, *tile),
            buf(256, 512), buf(512, 256), buf(256, 2048), buf(256, 2048),
            pltpu.VMEM((256, 2048), F32), buf(256, 1024), buf(256, 1024), pltpu.VMEM((256, 1024), F32),
            buf(256, 2048), buf(512, 2048),
            [buf(4, 16, 2048) if axes == "xz" else buf(8, 64, 256) for axes in PIECES],
            [buf(16, 2048) if axes == "xz" else buf(64, 256) for axes in PIECES],
            [buf(8, 16, 256) if axes == "xz" else buf(4, 16, 256) for axes in PIECES],
            buf(4, 16, 256), buf(4, 16, 256),
            dma((6,)), dma((11,)), dma, dma, dma((8,)), dma((8,)), dma((8,)), dma((8,)),
            dma((8,)), dma((8,)),
            dma((8,)), dma((8,)),
            dma((8,)), dma((8,)), dma((8,)), dma((8,)), dma, dma, dma((8,)), dma((8,)),
            dma((4,)), dma((4,)), dma, dma,
            dma((4, 6)), dma((4, 6)),
        ],
        compiler_params=pltpu.CompilerParams(
            collective_id=0, has_side_effects=True, vmem_limit_bytes=56 * 1024 * 1024),
        cost_estimate=pl.CostEstimate(
            flops=5 * 10**9, bytes_accessed=10 * 2**20, transcendentals=2 * 2**20),
        name="strip_attention",
    )(offs, queries.reshape(field), keys.reshape(field), values.reshape(field), w_out,
      grad_out.reshape(256, 1024))

    grid = jax.ShapeDtypeStruct(field, F32)
    layer, gq, gk, gv, gwo = pl.pallas_call(
        place_kernel,
        out_shape=(mid[0], grid, grid, grid, jax.ShapeDtypeStruct((512, 2048), F32)),
        in_specs=[any_spec] * 5,
        out_specs=(any_spec,) * 5,
        scratch_shapes=[
            pltpu.SMEM((2, 8), jnp.int32), buf(8, *tile), buf(8, 2, *tile), buf(512, 2048),
            buf(256, 1024), pltpu.VMEM((3,) + field, F32), pltpu.VMEM((512, 2048), F32),
            dma((8,)), dma((8,))],
        compiler_params=pltpu.CompilerParams(vmem_limit_bytes=60 * 1024 * 1024),
        cost_estimate=pl.CostEstimate(
            flops=10**8, bytes_accessed=10 * 2**20, transcendentals=0),
        name="place_gradients",
    )(offs, *parts)
    shape = queries.shape
    return (layer.reshape(grad_out.shape), gq.reshape(shape), gk.reshape(shape), gv.reshape(shape),
            gwo)


def solution(mesh):
    field = P("cam", "frame", None, None, "head")
    rows = P("cam", "frame", None, None, None, "head")
    return jax.shard_map(
        on_device,
        mesh=mesh,
        in_specs=(field, field, field, P(), P("head", None), rows),
        out_specs=(rows, field, field, field, P("head", None)),
        check_vma=False,
    )
```

```python
import functools

import jax
import jax.numpy as jnp
from jax import lax
from jax.experimental import pallas as pl
from jax.experimental.pallas import tpu as pltpu
from jax.sharding import PartitionSpec as P

HD = 128
BF = jnp.bfloat16
F32 = jnp.float32
MESH = pl.DeviceIdType.MESH
LOG2E = 1.4426950408889634
NT = (((1,), (1,)), ((), ()))
PIECES = ("xz", "zx", "xz")
ROWS = (64, 64, 128)
START = (0, 64, 128)


def dot(a, b):
    return jnp.dot(a, b, preferred_element_type=F32)


def dot_nt(a, b):
    return lax.dot_general(a, b, NT, preferred_element_type=F32)


def each(count, fn):
    def step(i, carry):
        fn(i)
        return carry

    lax.fori_loop(0, count, step, 0)


def transposed(block):
    return block.astype(F32).T


def selector(off):
    rows = lax.broadcasted_iota(jnp.int32, (128, 256), 0)
    cols = lax.broadcasted_iota(jnp.int32, (128, 256), 1)
    hit = cols == rows + (lax.shift_right_logical(rows, 4) * 16 + off)
    return jnp.where(hit, 1.0, 0.0).astype(BF)


def selector_t(off):
    rows = lax.broadcasted_iota(jnp.int32, (256, 128), 1)
    cols = lax.broadcasted_iota(jnp.int32, (256, 128), 0)
    hit = cols == rows + (lax.shift_right_logical(rows, 4) * 16 + off)
    return jnp.where(hit, 1.0, 0.0).astype(BF)


def main_kernel(
    offs_hbm, q_hbm, k_hbm, v_hbm, w_hbm, g_hbm,
    lo_hbm, dq_hbm, dkv_hbm, gw_hbm,
    offs, q_in, k_in, v_in, w, gfull,
    q_send, kv_send, do_send, q_recv, kv_recv, do_recv,
    kt, vt, probs, o_t, rl,
    att_send, att_recv, dq_acc, dq_send, dq_recv, dk_acc, dv_acc, far_send, far_recv, dkv_send, dkv_recv,
    a_rows, a_t, core_send, core_recv, own, lo_send, lo_recv, lo_done,
    out_bf, gw, first_recv, mid_sum, second_recv, y_send, y_recv,
    in_sem, out_sem, g_ss, g_rs, q_ss, q_rs, kv_ss, kv_rs, hand_ss, hand_rs, do_ss, do_rs,
    att_ss, att_rs, dq_ss, dq_rs, far_ss, far_rs, dkv_ss, dkv_rs, core_ss, core_rs, lo_ss, lo_rs,
    sum_ss, sum_rs,
):
    c = lax.axis_index("cam")
    f = lax.axis_index("frame")
    hh = lax.axis_index("head")
    x, yh, k = f >> 2, (f >> 1) & 1, f & 1
    u = x * 2 + yh
    scale = HD ** (-0.5)

    def frame_of(unit):
        return unit * 2 + k

    def frame_x(to_x):
        return to_x * 4 + yh * 2 + k

    def device(cam=c, frame=f, head=hh):
        return (cam, frame, head)

    def remote(src, dst, ss, rs, **where):
        return pltpu.make_async_remote_copy(
            src_ref=src, dst_ref=dst, send_sem=ss, recv_sem=rs,
            device_id=device(**where), device_id_type=MESH)

    other_core = x * 4 + yh * 2 + 1 - k
    other_half = x * 4 + (1 - yh) * 2 + k

    barrier = pltpu.get_barrier_semaphore()

    def greet(**where):
        pl.semaphore_signal(barrier, inc=1, device_id=device(**where), device_id_type=MESH)

    def greet_cams(i):
        greet(cam=(c + 1) & 7, frame=frame_of(i))
        greet(cam=(c + 7) & 7, frame=frame_of(i))

    loads = [
        pltpu.make_async_copy(src, dst, in_sem.at[i])
        for i, (src, dst) in enumerate(
            ((k_hbm, k_in), (v_hbm, v_in), (q_hbm, q_in), (g_hbm, gfull.at[hh]), (w_hbm, w),
             (offs_hbm, offs)))
    ]
    for load in loads:
        load.start()
    each(8, greet_cams)
    each(7, lambda i: greet(frame=frame_of((u + 1 + i) & 7)))
    each(5, lambda i: greet(cam=(c + 2 + i) & 7))
    greet(frame=other_core)
    greet(head=1 - hh)

    loads[5].wait()
    off = (offs[1, (c + 7) % 8], offs[0, c])
    sel = [selector(o) for o in off]

    def strip(ref, side):
        window = ref[:, :, side * 32:(side + 1) * 32, :].reshape(256, 512)
        return dot(sel[side], window).astype(BF)

    for i, ref in enumerate((k_in, v_in)):
        loads[i].wait()
        for side in range(2):
            cut = strip(ref, side)
            for h in range(4):
                kv_send[h * 2 + 1 - side, i] = cut[:, h * 128:(h + 1) * 128]

    pl.semaphore_wait(barrier, 30)

    def kv_copy(i):
        unit = (u + i) & 7
        return remote(kv_send.at[unit], kv_recv.at[k, u], kv_ss.at[i], kv_rs.at[u],
                      cam=(c + 9 - 2 * (unit & 1)) & 7, frame=frame_of(unit))

    each(8, lambda i: kv_copy(i).start())

    loads[2].wait()
    for side in range(2):
        cut = strip(q_in, side)
        for h in range(4):
            q_send[h * 2 + side] = cut[:, h * 128:(h + 1) * 128]

    def half_copy(send, recv, ss, rs, i):
        unit = (u + i) & 7
        return remote(send.at[unit], recv.at[u], ss.at[unit], rs.at[u], frame=frame_of(unit))

    def own_copy(send, recv, rs):
        return pltpu.make_async_copy(send.at[u], recv.at[u], rs.at[u])

    own_copy(q_send, q_recv, q_rs).start()
    each(7, lambda i: half_copy(q_send, q_recv, q_ss, q_rs, i + 1).start())
    loads[3].wait()
    g_copy = remote(gfull.at[hh], gfull.at[hh], g_ss, g_rs, head=1 - hh)
    g_copy.start()

    def arrived(ref, sem):
        pltpu.make_async_copy(ref, ref, sem).wait()

    def turn(turned, half, source, i):
        cols = pl.ds(pl.multiple_of(source * 128, 128), 128)
        turned[half, :, cols] = transposed(kv_recv[half, source, i]).astype(BF)

    def hand_copy(source):
        part = kv_recv.at[k, source]
        return remote(part, part, hand_ss.at[source], hand_rs.at[source], frame=other_core)

    def kv_arrive(i):
        source = (u + 8 - i) & 7
        arrived(kv_recv.at[k, source], kv_rs.at[source])
        hand_copy(source).start()
        turn(vt, k, source, 1)

    def kv_handed(i):
        source = (u + 8 - i) & 7
        arrived(kv_recv.at[1 - k, source], hand_rs.at[source])
        turn(vt, 1 - k, source, 1)

    each(8, kv_arrive)
    each(8, kv_handed)

    def stacked(half, i):
        return kv_recv[half, :, i].reshape(1024, 128)

    def send_block(send, recv, ss, rs, unit):
        @pl.when(unit == u)
        def _():
            own_copy(send, recv, rs).start()

        @pl.when(unit != u)
        def _():
            remote(send.at[unit], recv.at[u], ss.at[unit], rs.at[u],
                   frame=frame_of(unit)).start()

    def forward(i):
        b = (x + i) & 3
        for t in range(2):
            arrived(q_recv.at[2 * b + t], q_rs.at[2 * b + t])
        queries = q_recv[pl.ds(2 * b, 2)].reshape(256, 128)
        scores = [dot_nt(stacked(half, 0), queries) for half in range(2)]
        top = jnp.maximum(jnp.max(scores[0], axis=0, keepdims=True),
                          jnp.max(scores[1], axis=0, keepdims=True))
        total, out_t = 0.0, 0.0
        for half in range(2):
            weights = jnp.exp2((scores[half] - top) * (scale * LOG2E))
            total = total + jnp.sum(weights, axis=0, keepdims=True)
            weights = weights.astype(BF)
            probs[half, b] = weights
            out_t = out_t + dot(vt[half], weights)
        inverse = 1.0 / total
        out_t = out_t * inverse
        o_t[b] = out_t
        rl[b] = inverse
        att_send[pl.ds(2 * b, 2)] = out_t.T.astype(BF).reshape(2, 128, 128)
        for t in range(2):
            send_block(att_send, att_recv, att_ss, att_rs, 2 * b + t)

    each(4, forward)

    each(16, lambda i: turn(kt, i >> 3, i & 7, 0))

    each(8, lambda i: arrived(att_recv.at[i], att_rs.at[i]))
    for fr in range(2):
        for s in range(2):
            for h in range(4):
                a_rows[fr * 128 + s * 64:fr * 128 + s * 64 + 64, h * 128:(h + 1) * 128] = att_recv[
                    h * 2 + s, fr * 64:(fr + 1) * 64]
    for fr in range(2):
        for h in range(4):
            a_t[h * 128:(h + 1) * 128, fr * 128:(fr + 1) * 128] = transposed(
                a_rows[fr * 128:(fr + 1) * 128, h * 128:(h + 1) * 128]).astype(BF)

    def core_copy(p):
        part = pl.ds(START[p], ROWS[p])
        return remote(core_send.at[part], core_recv.at[part], core_ss.at[p], core_rs.at[p],
                      frame=other_core)

    columns = [pl.ds(pl.multiple_of(i * 1024, 1024), 1024) for i in (hh, 1 - hh)]

    def multiply(i):
        theirs = a_t[pl.ds(pl.multiple_of((1 - k) * 256, 256), 256), :]
        mine = a_t[pl.ds(pl.multiple_of(k * 256, 256), 256), :]
        features = gfull[hh if i == 0 else 1 - hh]
        core_send[:, columns[i]] = dot(theirs, features).astype(BF)
        if i == 1:
            for p in range(3):
                core_copy(p).start()
        own[:, columns[i]] = dot(mine, features)

    def cotangent():
        grad_attn = lo_done[:, :512] + dot_nt(gfull[1 - hh], w[:, columns[1]])
        grad_attn = grad_attn.astype(BF)
        for fr in range(2):
            for s in range(2):
                for h in range(4):
                    do_send[h * 2 + s, fr * 64:(fr + 1) * 64] = grad_attn[
                        fr * 128 + s * 64:fr * 128 + s * 64 + 64, h * 128:(h + 1) * 128]
        own_copy(do_send, do_recv, do_rs).start()
        each(7, lambda i: half_copy(do_send, do_recv, do_ss, do_rs, i + 1).start())

    def peers(axis):
        if axis == "x":
            return [((x + i) & 3, dict(frame=frame_x((x + i) & 3))) for i in (1, 3, 2)]
        return [((c + i) & 7, dict(cam=(c + i) & 7)) for i in (1, 7, 2, 6, 3, 5, 4)]

    def area(p, axes, at_x=x, at_z=c, base=0):
        first_row, count = base + START[p], ROWS[p]
        rows, cols = pl.ds(first_row, count), pl.ds(0, 2048)
        if "x" in axes:
            rows = pl.ds(pl.multiple_of(first_row + at_x * (count // 4), 16), count // 4)
        elif not isinstance(base, int):
            rows = pl.ds(pl.multiple_of(first_row, 64), count)
        if "z" in axes:
            cols = pl.ds(pl.multiple_of(at_z * 256, 256), 256)
        return rows, cols

    def me(axis):
        return x if axis == "x" else c

    def sum_copy(src, dst, p, step, where):
        return remote(src, dst, sum_ss.at[p, step], sum_rs.at[p, step], **where)

    def batch(recv, p, axis):
        return recv[p].at[pl.ds(0, 3 if axis == "x" else 7)]

    def first_sent(p):
        arrived(batch(first_recv, p, PIECES[p][0]), sum_ss.at[p, 0])

    def first(p):
        part = pl.ds(START[p], ROWS[p])
        axis = PIECES[p][0]
        arrived(core_recv.at[part], core_rs.at[p])
        own[part, :] += core_recv[part, :].astype(F32)
        out_bf[part, :] = own[part, :].astype(BF)
        for to, where in peers(axis):
            src = out_bf.at[area(p, axis, to, to)]
            sum_copy(src, first_recv[p].at[me(axis)], p, 0, where).start()

    def second(p):
        axis, other = PIECES[p]
        arrived(batch(first_recv, p, axis), sum_rs.at[p, 0])
        total = own[area(p, axis)]
        for frm, _ in peers(axis):
            total = total + first_recv[p][frm].astype(F32)
        mid_sum[p][...] = total.astype(BF)
        for to, where in peers(other):
            sum_copy(mid_sum[p].at[mid_part(p, to)], second_recv[p].at[me(other)], p, 1, where).start()

    def mid_part(p, to):
        if PIECES[p][1] == "x":
            return pl.ds(pl.multiple_of(to * 16, 16), 16), pl.ds(0, 256)
        return pl.ds(0, ROWS[p] // 4), pl.ds(pl.multiple_of(to * 256, 256), 256)

    def y_copy(p):
        return sum_copy(y_send[p], y_recv[p], p, 2, dict(frame=other_half))

    def third(p):
        axis = PIECES[p][1]
        arrived(batch(second_recv, p, axis), sum_rs.at[p, 1])
        total = mid_sum[p][mid_part(p, me(axis))].astype(F32)
        for frm, _ in peers(axis):
            total = total + second_recv[p][frm].astype(F32)
        y_send[p][...] = total.astype(BF)
        y_copy(p).start()

    def gather(p, axes, axis, step):
        part = gw.at[area(p, axes, base=k * 256)]
        for _, where in peers(axis):
            sum_copy(part, part, p, step, where).start()

    def fourth(p):
        arrived(y_recv[p], sum_rs.at[p, 2])
        gw[area(p, "xz", base=k * 256)] = (
            y_send[p][...].astype(F32) + y_recv[p][...].astype(F32)).astype(BF)
        gather(p, "xz", PIECES[p][1], 3)

    def fifth(p):
        arrived(batch(second_recv, p, PIECES[p][1]), sum_rs.at[p, 3])
        gather(p, PIECES[p][0], PIECES[p][0], 4)

    def sixth(p):
        arrived(batch(first_recv, p, PIECES[p][0]), sum_rs.at[p, 4])
        part = gw.at[area(p, "", base=k * 256)]
        sum_copy(part, part, p, 5, dict(frame=other_core)).start()
        gw_write(p, k).start()

    def seventh(p):
        arrived(gw.at[area(p, "", base=(1 - k) * 256)], sum_rs.at[p, 5])
        gw_write(p, 1 - k).start()

    def gw_write(p, core):
        at = area(p, "", base=core * 256)
        return pltpu.make_async_copy(gw.at[at], gw_hbm.at[at], out_sem.at[3 + p * 2 + core])

    def backward(half, i):
        b = (x + i) & 3
        if half is far:
            for t in range(2):
                arrived(do_recv.at[2 * b + t], do_rs.at[2 * b + t])
        queries = q_recv[pl.ds(2 * b, 2)].reshape(256, 128)
        weights = probs[half, b]
        grad_t = transposed(do_recv[pl.ds(2 * b, 2)].reshape(256, 128)) * rl[b]
        delta = jnp.sum(grad_t * o_t[b], axis=0, keepdims=True)
        grads = grad_t.T.astype(BF)
        grad_probs = dot(stacked(half, 1), grad_t.astype(BF))
        grad_scores = (weights.astype(F32) * (grad_probs - delta)).astype(BF)
        grad_q_t = dot(kt[half], grad_scores)
        if half is far:
            dq_acc[b] = grad_q_t
        else:
            grad_q_t = (grad_q_t + dq_acc[b]) * scale
            dq_send[pl.ds(2 * b, 2)] = grad_q_t.T.astype(BF).reshape(2, 128, 128)
            for t in range(2):
                send_block(dq_send, dq_recv, dq_ss, dq_rs, 2 * b + t)
        if i == 0:
            dk_acc[...] = dot(grad_scores, queries)
            dv_acc[...] = dot(weights, grads)
        else:
            dk_acc[...] += dot(grad_scores, queries)
            dv_acc[...] += dot(weights, grads)

    def far_copy():
        return remote(far_send, far_recv, far_ss, far_rs, frame=other_core)

    def dkv_copy(i):
        source = (u + i) & 7
        return remote(dkv_send.at[source], dkv_recv.at[u], dkv_ss.at[i], dkv_rs.at[u],
                      cam=(c + 7 + 2 * yh) & 7, frame=frame_of(source))

    far, near = 1 - k, k

    loads[4].wait()
    lo_done[:, :512] = dot_nt(gfull[hh], w[:, columns[0]])
    multiply(0)
    arrived(gfull.at[1 - hh], g_rs)
    multiply(1)
    cotangent()
    first(0)
    first(1)
    first(2)
    lo_send[...] = dot(
        a_rows[...], w[:, pl.ds(pl.multiple_of((1 - hh) * 1024, 1024), 1024)]).astype(BF)
    lo_copy = remote(lo_send, lo_recv, lo_ss, lo_rs, head=1 - hh)
    lo_copy.start()
    backward(far, 0)
    backward(far, 1)
    backward(far, 2)
    backward(far, 3)
    far_send[:, 0] = dk_acc[...].astype(BF).reshape(8, 128, 128)
    far_send[:, 1] = dv_acc[...].astype(BF).reshape(8, 128, 128)
    far_copy().start()
    second(0)
    second(1)
    backward(near, 0)
    second(2)
    backward(near, 1)
    third(0)
    third(1)
    backward(near, 2)
    backward(near, 3)
    far_copy().wait()
    for i, acc in enumerate((dk_acc, dv_acc)):
        total = acc[...].reshape(8, 128, 128) + far_recv[:, i].astype(F32)
        if i == 0:
            total = total * scale
        dkv_send[:, i] = total.astype(BF)
    each(8, lambda i: dkv_copy(i).start())
    fourth(0)
    fourth(1)
    third(2)
    fourth(2)
    fifth(0)
    fifth(1)
    fifth(2)

    lo_done[...] = dot(
        a_rows[...], w[:, pl.ds(pl.multiple_of(hh * 1024, 1024), 1024)])
    each(8, lambda i: arrived(dq_recv.at[i], dq_rs.at[i]))
    dq_write = pltpu.make_async_copy(dq_recv, dq_hbm, out_sem.at[1])
    dq_write.start()
    each(8, lambda i: arrived(dkv_recv.at[i], dkv_rs.at[i]))
    dkv_write = pltpu.make_async_copy(dkv_recv, dkv_hbm, out_sem.at[2])
    dkv_write.start()
    g_copy.wait_send()
    each(8, lambda i: kv_copy(i).wait_send())
    each(8, lambda i: hand_copy(i).wait_send())

    def sent(send, recv, ss, rs):
        each(7, lambda i: half_copy(send, recv, ss, rs, i + 1).wait_send())

    sent(q_send, q_recv, q_ss, q_rs)
    sent(do_send, do_recv, do_ss, do_rs)
    sent(att_send, att_recv, att_ss, att_rs)
    sent(dq_send, dq_recv, dq_ss, dq_rs)
    each(8, lambda i: dkv_copy(i).wait_send())
    for p in range(3):
        first_sent(p)
    for p in range(3):
        core_copy(p).wait_send()
        arrived(batch(second_recv, p, PIECES[p][1]), sum_ss.at[p, 1])
        y_copy(p).wait_send()
        arrived(batch(second_recv, p, PIECES[p][1]), sum_ss.at[p, 3])
    sixth(0)
    sixth(1)
    sixth(2)
    lo_copy.wait()
    lo_send[...] = (lo_done[...] + lo_recv[...].astype(F32)).astype(BF)
    lo_write = pltpu.make_async_copy(lo_send, lo_hbm, out_sem.at[0])
    lo_write.start()
    for p in range(3):
        seventh(p)

    for p in range(3):
        arrived(batch(first_recv, p, PIECES[p][0]), sum_ss.at[p, 4])
        arrived(gw.at[area(p, "", base=k * 256)], sum_ss.at[p, 5])
        gw_write(p, k).wait()
        gw_write(p, 1 - k).wait()
    lo_write.wait()
    dq_write.wait()
    dkv_write.wait()


def place_kernel(
    offs_hbm, lo_hbm, dq_hbm, dkv_hbm, gw_hbm, layer_hbm, gq_hbm, gk_hbm, gv_hbm, gwo_hbm,
    offs, dq, dkv, gw, lo, grid, rows, in_sem, out_sem,
):
    c = lax.axis_index("cam")
    loads = [pltpu.make_async_copy(offs_hbm, offs, in_sem.at[0]),
             pltpu.make_async_copy(dq_hbm, dq, in_sem.at[1]),
             pltpu.make_async_copy(dkv_hbm, dkv, in_sem.at[2]),
             pltpu.make_async_copy(lo_hbm, lo, in_sem.at[3])]
    part = [pl.ds(r * 128, 128) for r in range(4)]
    loads += [pltpu.make_async_copy(gw_hbm.at[part[r]], gw.at[part[r]], in_sem.at[4 + r])
              for r in range(4)]
    for load in loads:
        load.start()
    loads[0].wait()
    off = (offs[1, (c + 7) % 8], offs[0, c])
    sel = [selector_t(o) for o in off]
    writes = []

    def write(src, dst):
        writes.append(pltpu.make_async_copy(src, dst, out_sem.at[len(writes)]))
        writes[-1].start()

    for n, out in enumerate((gq_hbm, gk_hbm, gv_hbm)):
        if n < 2:
            loads[1 + n].wait()
        for side in range(2):
            for h in range(4):
                unit = h * 2 + (side if n == 0 else 1 - side)
                if n == 0:
                    placed = dot(sel[side], dq[unit])
                else:
                    placed = dot(sel[side], dkv[unit, n - 1])
                grid[n, :, :, side * 32:(side + 1) * 32, h * 128:(h + 1) * 128] = placed.reshape(
                    2, 4, 32, 128)
        write(grid.at[n], out)
    loads[3].wait()
    write(lo, layer_hbm)
    for r in range(4):
        loads[4 + r].wait()
        rows[part[r], :] = gw[part[r], :].astype(F32)
        write(rows.at[part[r]], gwo_hbm.at[part[r]])
    for copy in writes:
        copy.wait()


def on_device(queries, keys, values, offsets, w_out, grad_out):
    field = queries.shape[1:]
    dma = pltpu.SemaphoreType.DMA
    any_spec = pl.BlockSpec(memory_space=pl.ANY)
    tile = (128, 128)

    def buf(*shape):
        return pltpu.VMEM(shape, BF)

    mid = [
        jax.ShapeDtypeStruct((256, 1024), BF),
        jax.ShapeDtypeStruct((8,) + tile, BF),
        jax.ShapeDtypeStruct((8, 2) + tile, BF),
        jax.ShapeDtypeStruct((512, 2048), BF),
    ]
    offs = offsets.T
    parts = pl.pallas_call(
        main_kernel,
        out_shape=mid,
        in_specs=[any_spec] * 6,
        out_specs=[any_spec] * 4,
        scratch_shapes=[
            pltpu.SMEM((2, 8), jnp.int32),
            buf(*field), buf(*field), buf(*field), buf(512, 2048), buf(2, 256, 1024),
            buf(8, *tile), buf(8, 2, *tile), buf(8, *tile),
            buf(8, *tile), buf(2, 8, 2, *tile), buf(8, *tile),
            buf(2, 128, 1024), buf(2, 128, 1024), buf(2, 4, 1024, 256),
            pltpu.VMEM((4, 128, 256), F32), pltpu.VMEM((4, 1, 256), F32),
            buf(8, *tile), buf(8, *tile), pltpu.VMEM((4, 128, 256), F32), buf(8, *tile), buf(8, *tile),
            pltpu.VMEM((1024, 128), F32), pltpu.VMEM((1024, 128), F32),
            buf(8, 2, *tile), buf(8, 2, *tile), buf(8, 2, *tile), buf(8, 2, *tile),
            buf(256, 512), buf(512, 256), buf(256, 2048), buf(256, 2048),
            pltpu.VMEM((256, 2048), F32), buf(256, 1024), buf(256, 1024), pltpu.VMEM((256, 1024), F32),
            buf(256, 2048), buf(512, 2048),
            [buf(4, n // 4, 2048) if axes == "xz" else buf(8, n, 256) for axes, n in zip(PIECES, ROWS)],
            [buf(n // 4, 2048) if axes == "xz" else buf(n, 256) for axes, n in zip(PIECES, ROWS)],
            [buf(8 if axes == "xz" else 4, n // 4, 256) for axes, n in zip(PIECES, ROWS)],
            [buf(n // 4, 256) for n in ROWS], [buf(n // 4, 256) for n in ROWS],
            dma((6,)), dma((11,)), dma, dma, dma((8,)), dma((8,)), dma((8,)), dma((8,)),
            dma((8,)), dma((8,)),
            dma((8,)), dma((8,)),
            dma((8,)), dma((8,)), dma((8,)), dma((8,)), dma, dma, dma((8,)), dma((8,)),
            dma((4,)), dma((4,)), dma, dma,
            dma((4, 6)), dma((4, 6)),
        ],
        compiler_params=pltpu.CompilerParams(
            collective_id=0, has_side_effects=True, vmem_limit_bytes=56 * 1024 * 1024),
        cost_estimate=pl.CostEstimate(
            flops=5 * 10**9, bytes_accessed=10 * 2**20, transcendentals=2 * 2**20),
        name="strip_attention",
    )(offs, queries.reshape(field), keys.reshape(field), values.reshape(field), w_out,
      grad_out.reshape(256, 1024))

    grid = jax.ShapeDtypeStruct(field, F32)
    layer, gq, gk, gv, gwo = pl.pallas_call(
        place_kernel,
        out_shape=(mid[0], grid, grid, grid, jax.ShapeDtypeStruct((512, 2048), F32)),
        in_specs=[any_spec] * 5,
        out_specs=(any_spec,) * 5,
        scratch_shapes=[
            pltpu.SMEM((2, 8), jnp.int32), buf(8, *tile), buf(8, 2, *tile), buf(512, 2048),
            buf(256, 1024), pltpu.VMEM((3,) + field, F32), pltpu.VMEM((512, 2048), F32),
            dma((8,)), dma((8,))],
        compiler_params=pltpu.CompilerParams(vmem_limit_bytes=60 * 1024 * 1024),
        cost_estimate=pl.CostEstimate(
            flops=10**8, bytes_accessed=10 * 2**20, transcendentals=0),
        name="place_gradients",
    )(offs, *parts)
    shape = queries.shape
    return (layer.reshape(grad_out.shape), gq.reshape(shape), gk.reshape(shape), gv.reshape(shape),
            gwo)


def solution(mesh):
    field = P("cam", "frame", None, None, "head")
    rows = P("cam", "frame", None, None, None, "head")
    return jax.shard_map(
        on_device,
        mesh=mesh,
        in_specs=(field, field, field, P(), P("head", None), rows),
        out_specs=(rows, field, field, field, P("head", None)),
        check_vma=False,
    )
```

```python
import functools

import jax
import jax.numpy as jnp
from jax import lax
from jax.experimental import pallas as pl
from jax.experimental.pallas import tpu as pltpu
from jax.sharding import PartitionSpec as P

HD = 128
BF = jnp.bfloat16
F32 = jnp.float32
MESH = pl.DeviceIdType.MESH
LOG2E = 1.4426950408889634
NT = (((1,), (1,)), ((), ()))
PIECES = ("xz", "zx", "xz")
ROWS = (64, 64, 128)
START = (0, 64, 128)


def dot(a, b):
    return jnp.dot(a, b, preferred_element_type=F32)


def dot_nt(a, b):
    return lax.dot_general(a, b, NT, preferred_element_type=F32)


def each(count, fn):
    def step(i, carry):
        fn(i)
        return carry

    lax.fori_loop(0, count, step, 0)


def transposed(block):
    return block.astype(F32).T


def selector(off):
    rows = lax.broadcasted_iota(jnp.int32, (128, 256), 0)
    cols = lax.broadcasted_iota(jnp.int32, (128, 256), 1)
    hit = cols == rows + (lax.shift_right_logical(rows, 4) * 16 + off)
    return jnp.where(hit, 1.0, 0.0).astype(BF)


def selector_t(off):
    rows = lax.broadcasted_iota(jnp.int32, (256, 128), 1)
    cols = lax.broadcasted_iota(jnp.int32, (256, 128), 0)
    hit = cols == rows + (lax.shift_right_logical(rows, 4) * 16 + off)
    return jnp.where(hit, 1.0, 0.0).astype(BF)


def main_kernel(
    offs_hbm, q_hbm, k_hbm, v_hbm, w_hbm, g_hbm,
    lo_hbm, dq_hbm, dkv_hbm, gw_hbm,
    offs, q_in, k_in, v_in, w, gfull,
    q_send, kv_send, do_send, q_recv, kv_recv, do_recv,
    kt, vt, probs, o_t, rl, grads_t,
    att_send, att_recv, dq_acc, dq_send, dq_recv, dk_acc, dv_acc, far_send, far_recv, dkv_send, dkv_recv,
    a_rows, a_t, core_send, core_recv, own, lo_send, lo_recv, lo_done,
    out_bf, gw, first_recv, mid_sum, second_recv, y_send, y_recv,
    in_sem, out_sem, g_ss, g_rs, q_ss, q_rs, kv_ss, kv_rs, hand_ss, hand_rs, do_ss, do_rs,
    att_ss, att_rs, dq_ss, dq_rs, far_ss, far_rs, dkv_ss, dkv_rs, core_ss, core_rs, lo_ss, lo_rs,
    sum_ss, sum_rs,
):
    c = lax.axis_index("cam")
    f = lax.axis_index("frame")
    hh = lax.axis_index("head")
    x, yh, k = f >> 2, (f >> 1) & 1, f & 1
    u = x * 2 + yh
    scale = HD ** (-0.5)

    def frame_of(unit):
        return unit * 2 + k

    def frame_x(to_x):
        return to_x * 4 + yh * 2 + k

    def device(cam=c, frame=f, head=hh):
        return (cam, frame, head)

    def remote(src, dst, ss, rs, **where):
        return pltpu.make_async_remote_copy(
            src_ref=src, dst_ref=dst, send_sem=ss, recv_sem=rs,
            device_id=device(**where), device_id_type=MESH)

    other_core = x * 4 + yh * 2 + 1 - k
    other_half = x * 4 + (1 - yh) * 2 + k

    barrier = pltpu.get_barrier_semaphore()

    def greet(**where):
        pl.semaphore_signal(barrier, inc=1, device_id=device(**where), device_id_type=MESH)

    def greet_cams(i):
        greet(cam=(c + 1) & 7, frame=frame_of(i))
        greet(cam=(c + 7) & 7, frame=frame_of(i))

    loads = [
        pltpu.make_async_copy(src, dst, in_sem.at[i])
        for i, (src, dst) in enumerate(
            ((k_hbm, k_in), (v_hbm, v_in), (q_hbm, q_in), (g_hbm, gfull.at[hh]), (w_hbm, w),
             (offs_hbm, offs)))
    ]
    for load in loads:
        load.start()
    each(8, greet_cams)
    each(7, lambda i: greet(frame=frame_of((u + 1 + i) & 7)))
    each(5, lambda i: greet(cam=(c + 2 + i) & 7))
    greet(frame=other_core)
    greet(head=1 - hh)

    loads[5].wait()
    off = (offs[1, (c + 7) % 8], offs[0, c])
    sel = [selector(o) for o in off]

    def strip(ref, side):
        window = ref[:, :, side * 32:(side + 1) * 32, :].reshape(256, 512)
        return dot(sel[side], window).astype(BF)

    for i, ref in enumerate((k_in, v_in)):
        loads[i].wait()
        for side in range(2):
            cut = strip(ref, side)
            for h in range(4):
                kv_send[h * 2 + 1 - side, i] = cut[:, h * 128:(h + 1) * 128]

    pl.semaphore_wait(barrier, 30)

    def kv_copy(i):
        unit = (u + i) & 7
        return remote(kv_send.at[unit], kv_recv.at[k, u], kv_ss.at[i], kv_rs.at[u],
                      cam=(c + 9 - 2 * (unit & 1)) & 7, frame=frame_of(unit))

    each(8, lambda i: kv_copy(i).start())

    loads[2].wait()
    for side in range(2):
        cut = strip(q_in, side)
        for h in range(4):
            q_send[h * 2 + side] = cut[:, h * 128:(h + 1) * 128]

    def half_copy(send, recv, ss, rs, i):
        unit = (u + i) & 7
        return remote(send.at[unit], recv.at[u], ss.at[unit], rs.at[u], frame=frame_of(unit))

    def own_copy(send, recv, rs):
        return pltpu.make_async_copy(send.at[u], recv.at[u], rs.at[u])

    own_copy(q_send, q_recv, q_rs).start()
    each(7, lambda i: half_copy(q_send, q_recv, q_ss, q_rs, i + 1).start())
    loads[3].wait()
    g_copy = remote(gfull.at[hh], gfull.at[hh], g_ss, g_rs, head=1 - hh)
    g_copy.start()

    def arrived(ref, sem):
        pltpu.make_async_copy(ref, ref, sem).wait()

    def turn(turned, half, source, i):
        cols = pl.ds(pl.multiple_of(source * 128, 128), 128)
        turned[half, :, cols] = transposed(kv_recv[half, source, i]).astype(BF)

    def hand_copy(source):
        part = kv_recv.at[k, source]
        return remote(part, part, hand_ss.at[source], hand_rs.at[source], frame=other_core)

    def kv_arrive(i):
        source = (u + 8 - i) & 7
        arrived(kv_recv.at[k, source], kv_rs.at[source])
        hand_copy(source).start()
        turn(vt, k, source, 1)

    def kv_handed(i):
        source = (u + 8 - i) & 7
        arrived(kv_recv.at[1 - k, source], hand_rs.at[source])
        turn(vt, 1 - k, source, 1)

    each(8, kv_arrive)
    each(8, kv_handed)

    def stacked(half, i):
        return kv_recv[half, :, i].reshape(1024, 128)

    def send_block(send, recv, ss, rs, unit):
        @pl.when(unit == u)
        def _():
            own_copy(send, recv, rs).start()

        @pl.when(unit != u)
        def _():
            remote(send.at[unit], recv.at[u], ss.at[unit], rs.at[u],
                   frame=frame_of(unit)).start()

    def forward(i):
        b = (x + i) & 3
        for t in range(2):
            arrived(q_recv.at[2 * b + t], q_rs.at[2 * b + t])
        queries = q_recv[pl.ds(2 * b, 2)].reshape(256, 128)
        scores = [dot_nt(stacked(half, 0), queries) for half in range(2)]
        top = jnp.maximum(jnp.max(scores[0], axis=0, keepdims=True),
                          jnp.max(scores[1], axis=0, keepdims=True))
        total, out_t = 0.0, 0.0
        for half in range(2):
            weights = jnp.exp2((scores[half] - top) * (scale * LOG2E))
            total = total + jnp.sum(weights, axis=0, keepdims=True)
            weights = weights.astype(BF)
            probs[half, b] = weights
            out_t = out_t + dot(vt[half], weights)
        inverse = 1.0 / total
        out_t = out_t * inverse
        o_t[b] = out_t
        rl[b] = inverse
        att_send[pl.ds(2 * b, 2)] = out_t.T.astype(BF).reshape(2, 128, 128)
        for t in range(2):
            send_block(att_send, att_recv, att_ss, att_rs, 2 * b + t)

    each(4, forward)

    each(16, lambda i: turn(kt, i >> 3, i & 7, 0))

    each(8, lambda i: arrived(att_recv.at[i], att_rs.at[i]))
    for fr in range(2):
        for s in range(2):
            for h in range(4):
                a_rows[fr * 128 + s * 64:fr * 128 + s * 64 + 64, h * 128:(h + 1) * 128] = att_recv[
                    h * 2 + s, fr * 64:(fr + 1) * 64]
    for fr in range(2):
        for h in range(4):
            a_t[h * 128:(h + 1) * 128, fr * 128:(fr + 1) * 128] = transposed(
                a_rows[fr * 128:(fr + 1) * 128, h * 128:(h + 1) * 128]).astype(BF)

    def core_copy(p):
        part = pl.ds(START[p], ROWS[p])
        return remote(core_send.at[part], core_recv.at[part], core_ss.at[p], core_rs.at[p],
                      frame=other_core)

    columns = [pl.ds(pl.multiple_of(i * 1024, 1024), 1024) for i in (hh, 1 - hh)]

    def multiply(i):
        theirs = a_t[pl.ds(pl.multiple_of((1 - k) * 256, 256), 256), :]
        mine = a_t[pl.ds(pl.multiple_of(k * 256, 256), 256), :]
        features = gfull[hh if i == 0 else 1 - hh]
        core_send[:, columns[i]] = dot(theirs, features).astype(BF)
        if i == 1:
            for p in range(3):
                core_copy(p).start()
        own[:, columns[i]] = dot(mine, features)

    def cotangent():
        grad_attn = lo_done[:, :512] + dot_nt(gfull[1 - hh], w[:, columns[1]])
        grad_attn = grad_attn.astype(BF)
        for fr in range(2):
            for s in range(2):
                for h in range(4):
                    do_send[h * 2 + s, fr * 64:(fr + 1) * 64] = grad_attn[
                        fr * 128 + s * 64:fr * 128 + s * 64 + 64, h * 128:(h + 1) * 128]
        own_copy(do_send, do_recv, do_rs).start()
        each(7, lambda i: half_copy(do_send, do_recv, do_ss, do_rs, i + 1).start())

    def peers(axis):
        if axis == "x":
            return [((x + i) & 3, dict(frame=frame_x((x + i) & 3))) for i in (1, 3, 2)]
        return [((c + i) & 7, dict(cam=(c + i) & 7)) for i in (1, 7, 2, 6, 3, 5, 4)]

    def area(p, axes, at_x=x, at_z=c, base=0):
        first_row, count = base + START[p], ROWS[p]
        rows, cols = pl.ds(first_row, count), pl.ds(0, 2048)
        if "x" in axes:
            rows = pl.ds(pl.multiple_of(first_row + at_x * (count // 4), 16), count // 4)
        elif not isinstance(base, int):
            rows = pl.ds(pl.multiple_of(first_row, 64), count)
        if "z" in axes:
            cols = pl.ds(pl.multiple_of(at_z * 256, 256), 256)
        return rows, cols

    def me(axis):
        return x if axis == "x" else c

    def sum_copy(src, dst, p, step, where):
        return remote(src, dst, sum_ss.at[p, step], sum_rs.at[p, step], **where)

    def batch(recv, p, axis):
        return recv[p].at[pl.ds(0, 3 if axis == "x" else 7)]

    def first_sent(p):
        arrived(batch(first_recv, p, PIECES[p][0]), sum_ss.at[p, 0])

    def first(p):
        part = pl.ds(START[p], ROWS[p])
        axis = PIECES[p][0]
        arrived(core_recv.at[part], core_rs.at[p])
        own[part, :] += core_recv[part, :].astype(F32)
        out_bf[part, :] = own[part, :].astype(BF)
        for to, where in peers(axis):
            src = out_bf.at[area(p, axis, to, to)]
            sum_copy(src, first_recv[p].at[me(axis)], p, 0, where).start()

    def second(p):
        axis, other = PIECES[p]
        arrived(batch(first_recv, p, axis), sum_rs.at[p, 0])
        total = own[area(p, axis)]
        for frm, _ in peers(axis):
            total = total + first_recv[p][frm].astype(F32)
        mid_sum[p][...] = total.astype(BF)
        for to, where in peers(other):
            sum_copy(mid_sum[p].at[mid_part(p, to)], second_recv[p].at[me(other)], p, 1, where).start()

    def mid_part(p, to):
        if PIECES[p][1] == "x":
            return pl.ds(pl.multiple_of(to * 16, 16), 16), pl.ds(0, 256)
        return pl.ds(0, ROWS[p] // 4), pl.ds(pl.multiple_of(to * 256, 256), 256)

    def y_copy(p):
        return sum_copy(y_send[p], y_recv[p], p, 2, dict(frame=other_half))

    def third(p):
        axis = PIECES[p][1]
        arrived(batch(second_recv, p, axis), sum_rs.at[p, 1])
        total = mid_sum[p][mid_part(p, me(axis))].astype(F32)
        for frm, _ in peers(axis):
            total = total + second_recv[p][frm].astype(F32)
        y_send[p][...] = total.astype(BF)
        y_copy(p).start()

    def gather(p, axes, axis, step):
        part = gw.at[area(p, axes, base=k * 256)]
        for _, where in peers(axis):
            sum_copy(part, part, p, step, where).start()

    def fourth(p):
        arrived(y_recv[p], sum_rs.at[p, 2])
        gw[area(p, "xz", base=k * 256)] = (
            y_send[p][...].astype(F32) + y_recv[p][...].astype(F32)).astype(BF)
        gather(p, "xz", PIECES[p][1], 3)

    def fifth(p):
        arrived(batch(second_recv, p, PIECES[p][1]), sum_rs.at[p, 3])
        gather(p, PIECES[p][0], PIECES[p][0], 4)

    def sixth(p):
        arrived(batch(first_recv, p, PIECES[p][0]), sum_rs.at[p, 4])
        part = gw.at[area(p, "", base=k * 256)]
        sum_copy(part, part, p, 5, dict(frame=other_core)).start()
        gw_write(p, k).start()

    def seventh(p):
        arrived(gw.at[area(p, "", base=(1 - k) * 256)], sum_rs.at[p, 5])
        gw_write(p, 1 - k).start()

    def gw_write(p, core):
        at = area(p, "", base=core * 256)
        return pltpu.make_async_copy(gw.at[at], gw_hbm.at[at], out_sem.at[3 + p * 2 + core])

    def backward(half, i):
        b = (x + i) & 3
        if half is far:
            for t in range(2):
                arrived(do_recv.at[2 * b + t], do_rs.at[2 * b + t])
        queries = q_recv[pl.ds(2 * b, 2)].reshape(256, 128)
        weights = probs[half, b]
        if half is far:
            grad_t = transposed(do_recv[pl.ds(2 * b, 2)].reshape(256, 128)) * rl[b]
            rl[b] = jnp.sum(grad_t * o_t[b], axis=0, keepdims=True)
            grads_t[b] = grad_t.astype(BF)
            do_recv[pl.ds(2 * b, 2)] = grad_t.T.astype(BF).reshape(2, 128, 128)
        delta = rl[b]
        grads = do_recv[pl.ds(2 * b, 2)].reshape(256, 128)
        grad_probs = dot(stacked(half, 1), grads_t[b])
        grad_scores = (weights.astype(F32) * (grad_probs - delta)).astype(BF)
        grad_q_t = dot(kt[half], grad_scores)
        if half is far:
            dq_acc[b] = grad_q_t
        else:
            grad_q_t = (grad_q_t + dq_acc[b]) * scale
            dq_send[pl.ds(2 * b, 2)] = grad_q_t.T.astype(BF).reshape(2, 128, 128)
            for t in range(2):
                send_block(dq_send, dq_recv, dq_ss, dq_rs, 2 * b + t)
        if i == 0:
            dk_acc[...] = dot(grad_scores, queries)
            dv_acc[...] = dot(weights, grads)
        else:
            dk_acc[...] += dot(grad_scores, queries)
            dv_acc[...] += dot(weights, grads)

    def far_copy():
        return remote(far_send, far_recv, far_ss, far_rs, frame=other_core)

    def dkv_copy(i):
        source = (u + i) & 7
        return remote(dkv_send.at[source], dkv_recv.at[u], dkv_ss.at[i], dkv_rs.at[u],
                      cam=(c + 7 + 2 * yh) & 7, frame=frame_of(source))

    far, near = 1 - k, k

    loads[4].wait()
    lo_done[:, :512] = dot_nt(gfull[hh], w[:, columns[0]])
    multiply(0)
    arrived(gfull.at[1 - hh], g_rs)
    multiply(1)
    cotangent()
    first(0)
    first(1)
    first(2)
    lo_send[...] = dot(
        a_rows[...], w[:, pl.ds(pl.multiple_of((1 - hh) * 1024, 1024), 1024)]).astype(BF)
    lo_copy = remote(lo_send, lo_recv, lo_ss, lo_rs, head=1 - hh)
    lo_copy.start()
    backward(far, 0)
    backward(far, 1)
    backward(far, 2)
    backward(far, 3)
    far_send[:, 0] = dk_acc[...].astype(BF).reshape(8, 128, 128)
    far_send[:, 1] = dv_acc[...].astype(BF).reshape(8, 128, 128)
    far_copy().start()
    second(0)
    second(1)
    backward(near, 0)
    second(2)
    backward(near, 1)
    third(0)
    third(1)
    backward(near, 2)
    backward(near, 3)
    far_copy().wait()
    for i, acc in enumerate((dk_acc, dv_acc)):
        total = acc[...].reshape(8, 128, 128) + far_recv[:, i].astype(F32)
        if i == 0:
            total = total * scale
        dkv_send[:, i] = total.astype(BF)
    each(8, lambda i: dkv_copy(i).start())
    fourth(0)
    fourth(1)
    third(2)
    fourth(2)
    fifth(0)
    fifth(1)
    fifth(2)

    lo_done[...] = dot(
        a_rows[...], w[:, pl.ds(pl.multiple_of(hh * 1024, 1024), 1024)])
    each(8, lambda i: arrived(dq_recv.at[i], dq_rs.at[i]))
    dq_write = pltpu.make_async_copy(dq_recv, dq_hbm, out_sem.at[1])
    dq_write.start()
    each(8, lambda i: arrived(dkv_recv.at[i], dkv_rs.at[i]))
    dkv_write = pltpu.make_async_copy(dkv_recv, dkv_hbm, out_sem.at[2])
    dkv_write.start()
    g_copy.wait_send()
    each(8, lambda i: kv_copy(i).wait_send())
    each(8, lambda i: hand_copy(i).wait_send())

    def sent(send, recv, ss, rs):
        each(7, lambda i: half_copy(send, recv, ss, rs, i + 1).wait_send())

    sent(q_send, q_recv, q_ss, q_rs)
    sent(do_send, do_recv, do_ss, do_rs)
    sent(att_send, att_recv, att_ss, att_rs)
    sent(dq_send, dq_recv, dq_ss, dq_rs)
    each(8, lambda i: dkv_copy(i).wait_send())
    for p in range(3):
        first_sent(p)
    for p in range(3):
        core_copy(p).wait_send()
        arrived(batch(second_recv, p, PIECES[p][1]), sum_ss.at[p, 1])
        y_copy(p).wait_send()
        arrived(batch(second_recv, p, PIECES[p][1]), sum_ss.at[p, 3])
    sixth(0)
    sixth(1)
    sixth(2)
    lo_copy.wait()
    lo_send[...] = (lo_done[...] + lo_recv[...].astype(F32)).astype(BF)
    lo_write = pltpu.make_async_copy(lo_send, lo_hbm, out_sem.at[0])
    lo_write.start()
    for p in range(3):
        seventh(p)

    for p in range(3):
        arrived(batch(first_recv, p, PIECES[p][0]), sum_ss.at[p, 4])
        arrived(gw.at[area(p, "", base=k * 256)], sum_ss.at[p, 5])
        gw_write(p, k).wait()
        gw_write(p, 1 - k).wait()
    lo_write.wait()
    dq_write.wait()
    dkv_write.wait()


def place_kernel(
    offs_hbm, lo_hbm, dq_hbm, dkv_hbm, gw_hbm, layer_hbm, gq_hbm, gk_hbm, gv_hbm, gwo_hbm,
    offs, dq, dkv, gw, lo, grid, rows, in_sem, out_sem,
):
    c = lax.axis_index("cam")
    loads = [pltpu.make_async_copy(offs_hbm, offs, in_sem.at[0]),
             pltpu.make_async_copy(dq_hbm, dq, in_sem.at[1]),
             pltpu.make_async_copy(dkv_hbm, dkv, in_sem.at[2]),
             pltpu.make_async_copy(lo_hbm, lo, in_sem.at[3])]
    part = [pl.ds(r * 128, 128) for r in range(4)]
    loads += [pltpu.make_async_copy(gw_hbm.at[part[r]], gw.at[part[r]], in_sem.at[4 + r])
              for r in range(4)]
    for load in loads:
        load.start()
    loads[0].wait()
    off = (offs[1, (c + 7) % 8], offs[0, c])
    sel = [selector_t(o) for o in off]
    writes = []

    def write(src, dst):
        writes.append(pltpu.make_async_copy(src, dst, out_sem.at[len(writes)]))
        writes[-1].start()

    for n, out in enumerate((gq_hbm, gk_hbm, gv_hbm)):
        if n < 2:
            loads[1 + n].wait()
        for side in range(2):
            for h in range(4):
                unit = h * 2 + (side if n == 0 else 1 - side)
                if n == 0:
                    placed = dot(sel[side], dq[unit])
                else:
                    placed = dot(sel[side], dkv[unit, n - 1])
                grid[n, :, :, side * 32:(side + 1) * 32, h * 128:(h + 1) * 128] = placed.reshape(
                    2, 4, 32, 128)
        write(grid.at[n], out)
    loads[3].wait()
    write(lo, layer_hbm)
    for r in range(4):
        loads[4 + r].wait()
        rows[part[r], :] = gw[part[r], :].astype(F32)
        write(rows.at[part[r]], gwo_hbm.at[part[r]])
    for copy in writes:
        copy.wait()


def on_device(queries, keys, values, offsets, w_out, grad_out):
    field = queries.shape[1:]
    dma = pltpu.SemaphoreType.DMA
    any_spec = pl.BlockSpec(memory_space=pl.ANY)
    tile = (128, 128)

    def buf(*shape):
        return pltpu.VMEM(shape, BF)

    mid = [
        jax.ShapeDtypeStruct((256, 1024), BF),
        jax.ShapeDtypeStruct((8,) + tile, BF),
        jax.ShapeDtypeStruct((8, 2) + tile, BF),
        jax.ShapeDtypeStruct((512, 2048), BF),
    ]
    offs = offsets.T
    parts = pl.pallas_call(
        main_kernel,
        out_shape=mid,
        in_specs=[any_spec] * 6,
        out_specs=[any_spec] * 4,
        scratch_shapes=[
            pltpu.SMEM((2, 8), jnp.int32),
            buf(*field), buf(*field), buf(*field), buf(512, 2048), buf(2, 256, 1024),
            buf(8, *tile), buf(8, 2, *tile), buf(8, *tile),
            buf(8, *tile), buf(2, 8, 2, *tile), buf(8, *tile),
            buf(2, 128, 1024), buf(2, 128, 1024), buf(2, 4, 1024, 256),
            pltpu.VMEM((4, 128, 256), F32), pltpu.VMEM((4, 1, 256), F32), buf(4, 128, 256),
            buf(8, *tile), buf(8, *tile), pltpu.VMEM((4, 128, 256), F32), buf(8, *tile), buf(8, *tile),
            pltpu.VMEM((1024, 128), F32), pltpu.VMEM((1024, 128), F32),
            buf(8, 2, *tile), buf(8, 2, *tile), buf(8, 2, *tile), buf(8, 2, *tile),
            buf(256, 512), buf(512, 256), buf(256, 2048), buf(256, 2048),
            pltpu.VMEM((256, 2048), F32), buf(256, 1024), buf(256, 1024), pltpu.VMEM((256, 1024), F32),
            buf(256, 2048), buf(512, 2048),
            [buf(4, n // 4, 2048) if axes == "xz" else buf(8, n, 256) for axes, n in zip(PIECES, ROWS)],
            [buf(n // 4, 2048) if axes == "xz" else buf(n, 256) for axes, n in zip(PIECES, ROWS)],
            [buf(8 if axes == "xz" else 4, n // 4, 256) for axes, n in zip(PIECES, ROWS)],
            [buf(n // 4, 256) for n in ROWS], [buf(n // 4, 256) for n in ROWS],
            dma((6,)), dma((11,)), dma, dma, dma((8,)), dma((8,)), dma((8,)), dma((8,)),
            dma((8,)), dma((8,)),
            dma((8,)), dma((8,)),
            dma((8,)), dma((8,)), dma((8,)), dma((8,)), dma, dma, dma((8,)), dma((8,)),
            dma((4,)), dma((4,)), dma, dma,
            dma((4, 6)), dma((4, 6)),
        ],
        compiler_params=pltpu.CompilerParams(
            collective_id=0, has_side_effects=True, vmem_limit_bytes=56 * 1024 * 1024),
        cost_estimate=pl.CostEstimate(
            flops=5 * 10**9, bytes_accessed=10 * 2**20, transcendentals=2 * 2**20),
        name="strip_attention",
    )(offs, queries.reshape(field), keys.reshape(field), values.reshape(field), w_out,
      grad_out.reshape(256, 1024))

    grid = jax.ShapeDtypeStruct(field, F32)
    layer, gq, gk, gv, gwo = pl.pallas_call(
        place_kernel,
        out_shape=(mid[0], grid, grid, grid, jax.ShapeDtypeStruct((512, 2048), F32)),
        in_specs=[any_spec] * 5,
        out_specs=(any_spec,) * 5,
        scratch_shapes=[
            pltpu.SMEM((2, 8), jnp.int32), buf(8, *tile), buf(8, 2, *tile), buf(512, 2048),
            buf(256, 1024), pltpu.VMEM((3,) + field, F32), pltpu.VMEM((512, 2048), F32),
            dma((8,)), dma((8,))],
        compiler_params=pltpu.CompilerParams(vmem_limit_bytes=60 * 1024 * 1024),
        cost_estimate=pl.CostEstimate(
            flops=10**8, bytes_accessed=10 * 2**20, transcendentals=0),
        name="place_gradients",
    )(offs, *parts)
    shape = queries.shape
    return (layer.reshape(grad_out.shape), gq.reshape(shape), gk.reshape(shape), gv.reshape(shape),
            gwo)


def solution(mesh):
    field = P("cam", "frame", None, None, "head")
    rows = P("cam", "frame", None, None, None, "head")
    return jax.shard_map(
        on_device,
        mesh=mesh,
        in_specs=(field, field, field, P(), P("head", None), rows),
        out_specs=(rows, field, field, field, P("head", None)),
        check_vma=False,
    )
```
